32 devices in a mesh: pert: 4 (over y, x), doc: 8 (over z, core).
Axes of the slice: x: 2, y: 2, z: 4, core: 2. Of those that a mesh axis runs over, the one named last changes fastest.
Arguments:
- counts: int32 [4, 64, 16384], P('pert', 'doc'), may hold values from 1 to 11
- tile_mask: int32 [4, 64, 128], P('pert', 'doc'), may hold values 0 or 1
- member_topics: float32 [4, 64, 64], P('pert', 'doc'), may hold values from 0.05 to 0.5
- start_dict: float32 [4, 16384, 64], P('pert', 'doc'), may hold values from 0.05 to 0.5
- align_perm: int32 [4, 64], P('pert'), may hold values from 0 to 63, each once within a row
- base_counts: int32 [128, 16384], P(('pert', 'doc')), may hold values from 1 to 11
- base_topics: float32 [128, 64], P(('pert', 'doc')), may hold values from 0.05 to 0.5
Outputs:
- median_dict: float32 [8, 4, 512, 64], P('doc', 'pert')
- refit_topics: float32 [128, 64], P(('pert', 'doc'))
The draws below stay inside these ranges and needn't reach their ends.
Inputs may be any that keep to these rules, and one draw needn't show every extreme that they name: `align_perm`: each row is a permutation of 0 to 63.
All inputs are finite; a program needn't handle non-finite values. No bound on the sum of `tile_mask` on one device may be relied on, other than what follows from the above.
Results may differ from the reference program's by a relative error of at most 0.0003.
Values sent between devices are 32-bit elements; how exact they have to be, the bound alone decides.
No kernel may reach another device: no remote copies, remote signals or barrier semaphores. Data moves between devices by JAX's collectives and lax.ppermute only.
A program may use at most 64 MiB of HBM per device.

```python
import math
import jax
import jax.numpy as jnp
from jax import lax

WORDS = 16384
K = 64
ODOC_DEV = 4
UPDATES = 3
REFITS = 2
MEMBERS = 4
MDOCS = 64
ODOCS = 128
WTILES = 128
SUB = 512
N_PERT = 4
N_DOC = 8


def with_ends(array, rng, low, high):
    longest = array.shape.index(max(array.shape))
    spots = []
    for shift in (0, 1):
        where = [jax.random.randint(jax.random.fold_in(rng, axis), (), 0, length) for axis, length in enumerate(array.shape)]
        where[longest] = (where[longest] + shift) % array.shape[longest]
        spots.append(tuple(where))
    return array.at[spots[0]].set(low).at[spots[1]].set(high)


def block_levels(rng, dims, shards, least, high):
    factor_of, own = 1.0, jax.random.fold_in(rng, 6)
    for axis_at, parts in shards:
        heights = jnp.exp(jax.random.uniform(jax.random.fold_in(own, axis_at), (parts,), jnp.float32, least / len(shards), high / len(shards)))
        factor_of = factor_of * jnp.repeat(heights, dims[axis_at] // parts).reshape([-1 if axis == axis_at else 1 for axis in range(len(dims))])
    return factor_of


def setup_inputs(seed: int = 0) -> dict:
    streams_of = jax.random.split(jax.random.key(seed), 8)
    return {
        "counts": with_ends(jax.random.randint(streams_of[0], (MEMBERS, MDOCS, WORDS), 1, 12), jax.random.fold_in(streams_of[0], 1), 1, 11).astype(jnp.int32),
        "tile_mask": with_ends((jax.random.randint(streams_of[1], (MEMBERS, MDOCS, WTILES), 0, 2) < 1).astype(jnp.int32), jax.random.fold_in(streams_of[1], 1), 0, 1),
        "member_topics": jnp.clip(jnp.exp(math.log(0.5) - 2.3025851 * jax.random.uniform(streams_of[2], (MEMBERS, MDOCS, K), jnp.float32) ** block_levels(streams_of[2], (MEMBERS, MDOCS, K), ((0, 4), (1, 8)), -0.2, 0.2)), 0.05, 0.5),
        "start_dict": jnp.clip(jnp.exp(math.log(0.5) - 2.3025851 * jax.random.uniform(streams_of[3], (MEMBERS, WORDS, K), jnp.float32) ** block_levels(streams_of[3], (MEMBERS, WORDS, K), ((0, 4), (1, 8)), -0.2, 0.2)), 0.05, 0.5),
        "align_perm": jax.vmap(lambda own: jax.random.permutation(own, K))(jax.random.split(streams_of[4], MEMBERS)).reshape((MEMBERS, K)).astype(jnp.int32),
        "base_counts": with_ends(jax.random.randint(streams_of[5], (ODOCS, WORDS), 1, 12), jax.random.fold_in(streams_of[5], 1), 1, 11).astype(jnp.int32),
        "base_topics": jnp.clip(jnp.exp(math.log(0.5) - 2.3025851 * jax.random.uniform(streams_of[6], (ODOCS, K), jnp.float32) ** block_levels(streams_of[6], (ODOCS, K), ((0, 32),), -0.2, 0.2)), 0.05, 0.5),
    }


HIGHEST_PRECISION = lax.Precision.HIGHEST


def product_t(left_side, right_side):
    return lax.dot_general(left_side, right_side, (((1,), (1,)), ((), ())), precision=HIGHEST_PRECISION)


def weight_update(topics, quotient, dictionary, col_total):
    return topics * jnp.dot(quotient, dictionary, precision=HIGHEST_PRECISION) / col_total


def middle(stacked):
    ordered = jnp.sort(stacked, axis=0)
    middle_at = stacked.shape[0] // 2
    return 0.5 * (ordered[middle_at - 1] + ordered[middle_at])


def occupied_counts(counts, mask, first_doc):
    doc_count, word_count = counts.shape
    tile_count = mask.shape[1]
    tile_width = word_count // tile_count
    tile_ids = lax.broadcasted_iota(jnp.int32, (doc_count, tile_count), 1)
    doc_ids = first_doc + lax.broadcasted_iota(jnp.int32, (doc_count, tile_count), 0)
    occupied = jnp.maximum(mask, (tile_ids == doc_ids % tile_count).astype(jnp.int32)).astype(jnp.float32)
    spread = counts.astype(jnp.float32).reshape(doc_count, tile_count, tile_width) * occupied[:, :, None]
    return spread.reshape(doc_count, word_count)


def reference(counts, tile_mask, member_topics, start_dict, align_perm, base_counts, base_topics):
    def one_member(inputs):
        counts_m, mask_m, topics, dictionary, perm_m = inputs
        weighted = occupied_counts(counts_m, mask_m, 0)
        col_total = jnp.sum(dictionary, axis=0)
        for iteration in range(UPDATES):
            quotient = weighted / product_t(topics, dictionary)
            topics = weight_update(topics, quotient, dictionary, col_total)
        quotient = weighted / product_t(topics, dictionary)
        numerator = lax.dot_general(quotient, topics, (((0,), (0,)), ((), ())), precision=HIGHEST_PRECISION)
        topic_load = jnp.sum(topics, axis=0)
        new_dict = dictionary * numerator / topic_load
        return jnp.take(new_dict, perm_m.astype(jnp.int32), axis=1)

    aligned = lax.map(one_member, (counts, tile_mask, member_topics, start_dict, align_perm))
    median = middle(aligned)
    median_total = jnp.sum(median, axis=0)

    def refit_block(inputs):
        counts_b, topics_b = inputs
        weighted = counts_b.astype(jnp.float32)
        for iteration in range(REFITS):
            quotient = weighted / product_t(topics_b, median)
            topics_b = weight_update(topics_b, quotient, median, median_total)
        return topics_b

    blocks = N_PERT * N_DOC
    refit = lax.map(refit_block, (base_counts.reshape(blocks, ODOC_DEV, WORDS), base_topics.reshape(blocks, ODOC_DEV, K)))
    return median.reshape(N_DOC, N_PERT, SUB, K), refit.reshape(ODOCS, K)
```

```python
import jax
import jax.numpy as jnp
from jax import lax
from jax.sharding import PartitionSpec as P

UPDATES = 3
REFITS = 2

HIGHEST_PRECISION = lax.Precision.HIGHEST


def dot(left, right, dims):
    return lax.dot_general(left, right, (dims, ((), ())), precision=HIGHEST_PRECISION)


def middle(pieces):
    pieces = list(pieces)
    count = len(pieces)
    for turn in range(count):
        for low in range(turn % 2, count - 1, 2):
            pieces[low], pieces[low + 1] = (
                jnp.minimum(pieces[low], pieces[low + 1]),
                jnp.maximum(pieces[low], pieces[low + 1]),
            )
    return 0.5 * (pieces[count // 2 - 1] + pieces[count // 2])


def occupied_counts(counts, mask, first_doc):
    doc_count, word_count = counts.shape
    tile_count = mask.shape[1]
    tile_width = word_count // tile_count
    tile_ids = lax.broadcasted_iota(jnp.int32, (doc_count, tile_count), 1)
    doc_ids = first_doc + lax.broadcasted_iota(jnp.int32, (doc_count, tile_count), 0)
    occupied = jnp.maximum(mask, (tile_ids == doc_ids % tile_count).astype(jnp.int32)).astype(
        jnp.float32
    )
    spread = (
        counts.astype(jnp.float32).reshape(doc_count, tile_count, tile_width) * occupied[:, :, None]
    )
    return spread.reshape(doc_count, word_count)


def partial_update(topics, weighted, dict_halves):
    width = dict_halves[0].shape[1]
    total = None
    for half, dict_half in enumerate(dict_halves):
        quotient = weighted[:, half * width : (half + 1) * width] / dot(
            topics, dict_half, ((1,), (0,))
        )
        part = dot(quotient, dict_half, ((1,), (1,)))
        total = part if total is None else total + part
    return total


def per_device(counts, tile_mask, member_topics, start_dict, align_perm, base_counts, base_topics):
    doc_size = lax.axis_size("doc")
    members = lax.axis_size("pert")
    cores = 2 - doc_size % 2
    chips = doc_size // cores
    at_pert = lax.axis_index("pert")
    at_doc = lax.axis_index("doc")
    at_chip, at_core = at_doc // cores, at_doc % cores
    docs, words = counts.shape[1:]
    base_docs = base_counts.shape[0]
    topic_count = member_topics.shape[2]
    owned = start_dict.shape[1]
    sub = owned // members

    def over_chips(array, step):
        return lax.ppermute(
            array,
            "doc",
            [(c * cores + k, (c ^ step) * cores + k) for c in range(chips) for k in range(cores)],
        )

    def over_cores(array):
        return lax.ppermute(array, "doc", [(d, d ^ 1) for d in range(doc_size)])

    def over_pert(array, step):
        return lax.ppermute(array, "pert", [(m, m ^ step) for m in range(members)])

    def sum_over_chips(own, rows):
        body, extra = own[: rows * chips], own[rows * chips :]
        blocks = body.reshape(chips, rows, topic_count)
        for step in range(1, chips):
            got = over_chips(own, step)
            order = [c ^ step for c in range(chips)]
            got_blocks = got[: rows * chips].reshape(chips, rows, topic_count)
            blocks = blocks + jnp.stack([got_blocks[c] for c in order])
            extra = extra + got[rows * chips :]
        return blocks.reshape(rows * chips, topic_count), extra

    weighted = occupied_counts(counts[0], tile_mask[0], at_doc * docs)

    def chip_words(array, chip):
        return [
            lax.dynamic_slice_in_dim(array, (chip * cores + (at_core ^ k)) * owned, owned, 1)
            for k in range(cores)
        ]

    sent = [
        jnp.concatenate(chip_words(weighted, at_chip ^ step) + [member_topics[0]], axis=1)
        for step in range(chips)
    ]
    payload = jnp.concatenate(
        [sent[0]] + [over_chips(sent[step], step) for step in range(1, chips)], axis=0
    )
    onehot = (
        lax.broadcasted_iota(jnp.int32, (topic_count, topic_count), 0) == align_perm[0][None, :]
    ).astype(jnp.float32)
    dict_own = dot(onehot, start_dict[0].T, ((0,), (0,)))
    dict_halves = [dict_own] + [over_cores(dict_own)] * (cores - 1)
    weighted_all = payload[:, : cores * owned]
    topics = dot(payload[:, cores * owned :], onehot, ((1,), (0,)))

    col_part = sum(jnp.sum(half, axis=1) for half in dict_halves)[None, :]
    for update in range(UPDATES):
        part = partial_update(topics, weighted_all, dict_halves)
        if update == 0:
            total, col_total = sum_over_chips(jnp.concatenate([part, col_part]), docs)
        else:
            total, _ = sum_over_chips(part, docs)
        topics = topics * total / col_total

    numerators = []
    for half, dict_half in enumerate(dict_halves):
        quotient = weighted_all[:, half * owned : (half + 1) * owned] / dot(
            topics, dict_half, ((1,), (0,))
        )
        numerators.append(dot(topics, quotient, ((0,), (0,))))
    topic_load = jnp.sum(topics, axis=0)[:, None]
    numerator = numerators[0]
    if cores > 1:
        sent_half = jnp.concatenate(
            [numerators[1], jnp.broadcast_to(topic_load, (topic_count, 128))], axis=1
        )
        got_half = over_cores(sent_half)
        numerator = numerator + got_half[:, :owned]
        topic_load = topic_load + got_half[:, owned : owned + 1]
    aligned = dict_own * numerator / topic_load

    def words_of(array, member):
        return lax.dynamic_slice_in_dim(array, member * sub, sub, 1)

    pieces = [words_of(aligned, at_pert)] + [
        over_pert(words_of(aligned, at_pert ^ step), step) for step in range(1, members)
    ]
    median = middle(pieces)

    def base_words(chip):
        return [
            lax.dynamic_slice_in_dim(
                base_counts,
                (chip * cores + (at_core ^ k)) * owned + (at_pert ^ m) * sub,
                sub,
                1,
            )
            for k in range(cores)
            for m in range(members)
        ]

    base_sent = [
        jnp.concatenate(
            [part.astype(jnp.float32) for part in base_words(at_chip ^ step)] + [base_topics],
            axis=1,
        )
        for step in range(chips)
    ]
    base_payload = jnp.concatenate(
        [base_sent[0]] + [over_chips(base_sent[step], step) for step in range(1, chips)], axis=0
    )
    base_all = base_payload[:, : cores * owned]
    refit = base_payload[:, cores * owned :]

    median_own = jnp.concatenate(
        [median] + [over_pert(median, step) for step in range(1, members)], axis=1
    )
    median_halves = [median_own] + [over_cores(median_own)] * (cores - 1)
    median_part = sum(jnp.sum(half, axis=1) for half in median_halves)[None, :]
    for update in range(REFITS - 1):
        part = partial_update(refit, base_all, median_halves)
        if update == 0:
            total, median_total = sum_over_chips(jnp.concatenate([part, median_part]), base_docs)
        else:
            total, _ = sum_over_chips(part, base_docs)
        refit = refit * total / median_total
    part = partial_update(refit, base_all, median_halves)
    total = part[:base_docs]
    for step in range(1, chips):
        total = total + over_chips(part[step * base_docs : (step + 1) * base_docs], step)
    refit = refit[:base_docs] * total / median_total
    return (median.T[None, None], refit)


def solution(mesh):
    return jax.shard_map(
        per_device,
        mesh=mesh,
        in_specs=(
            P("pert", "doc", None),
            P("pert", "doc", None),
            P("pert", "doc", None),
            P("pert", "doc", None),
            P("pert", None),
            P(("pert", "doc"), None),
            P(("pert", "doc"), None),
        ),
        out_specs=(P("doc", "pert", None, None), P(("pert", "doc"), None)),
        check_vma=False,
    )
```

```python
import functools

import jax
import jax.numpy as jnp
from jax import lax
from jax.experimental import pallas as pl
from jax.experimental.pallas import tpu as pltpu
from jax.sharding import PartitionSpec as P

UPDATES = 3
REFITS = 2

EXACT = lax.Precision.HIGHEST
ROUGH = lax.Precision.HIGH
VMEM_BYTES = 14 * 1024 * 1024
SPREAD_BYTES = 60 * 1024 * 1024


def dot(left, right, dims, precision=ROUGH):
    return lax.dot_general(left, right, (dims, ((), ())), precision=precision)


def middle(pieces):
    pieces = list(pieces)
    count = len(pieces)
    for turn in range(count):
        for low in range(turn % 2, count - 1, 2):
            pieces[low], pieces[low + 1] = (
                jnp.minimum(pieces[low], pieces[low + 1]),
                jnp.maximum(pieces[low], pieces[low + 1]),
            )
    return 0.5 * (pieces[count // 2 - 1] + pieces[count // 2])


def call(kernel, outs, *args, flops=0, moved=0):
    return pl.pallas_call(
        kernel,
        out_shape=outs,
        compiler_params=pltpu.CompilerParams(vmem_limit_bytes=VMEM_BYTES),
        cost_estimate=pl.CostEstimate(flops=flops, bytes_accessed=moved, transcendentals=0),
    )(*args)


def shape(*dims, dtype=jnp.float32):
    return jax.ShapeDtypeStruct(dims, dtype)


def high_low(x):
    high = x.astype(jnp.bfloat16).astype(jnp.float32)
    return high, x - high


def matmul(left, right):
    return jnp.dot(
        left.astype(jnp.bfloat16), right.astype(jnp.bfloat16), preferred_element_type=jnp.float32
    )


def spread_kernel(chips, cores, own_words, counts_hbm, mask_hbm, topics_hbm, base_hbm, base_topics_hbm, *refs):
    out_refs, (counts_ref, mask_ref, topics_ref, base_ref, base_topics_ref, sems) = (
        refs[:-6],
        refs[-6:],
    )
    copies = [
        pltpu.make_async_copy(src, dst, sems.at[at])
        for at, (src, dst) in enumerate(
            [
                (mask_hbm, mask_ref),
                (counts_hbm, counts_ref),
                (topics_hbm, topics_ref),
                (base_hbm, base_ref),
                (base_topics_hbm, base_topics_ref),
            ]
        )
    ]
    for copy in copies:
        copy.start()
    docs, words = counts_ref.shape
    base_docs = base_ref.shape[0]
    tiles = mask_ref.shape[1]
    width = words // tiles
    own_tiles = own_words // width
    at_doc = lax.axis_index("doc")
    at_chip, at_core = at_doc // cores, at_doc % cores
    tile_ids = lax.broadcasted_iota(jnp.int32, (docs, tiles), 1)
    doc_ids = at_doc * docs + lax.broadcasted_iota(jnp.int32, (docs, tiles), 0)
    forced = (tile_ids == doc_ids % tiles).astype(jnp.int32)
    copies[0].wait()
    occupied = jnp.maximum(mask_ref[...], forced).astype(jnp.float32)
    for copy in copies[1:]:
        copy.wait()
    for step in range(chips):
        base_out, base_row = (out_refs[step], docs) if step < 2 else (out_refs[chips + step - 2], 0)
        base_rows = slice(base_row, base_row + base_docs)
        for half in range(cores):
            block = (at_chip ^ step) * cores + (at_core ^ ((step + half) % cores))
            first = pl.multiple_of(block * own_words, 128)
            near = pltpu.roll(occupied, lax.rem(tiles - block * own_tiles, tiles), 1)
            for tile in range(own_tiles):
                at = slice(half * own_words + tile * width, half * own_words + (tile + 1) * width)
                picked = counts_ref[:, pl.ds(first + tile * width, width)].astype(jnp.float32)
                out_refs[step][:docs, at] = picked * near[:, tile : tile + 1]
            at = slice(half * own_words, (half + 1) * own_words)
            base_out[base_rows, at] = base_ref[:, pl.ds(first, own_words)].astype(jnp.float32)
        out_refs[step][:docs, cores * own_words :] = topics_ref[...]
        base_out[base_rows, cores * own_words :] = base_topics_ref[...]


def moved_columns(x, onehot):
    rows = x.shape[0]
    high, rest = high_low(x)
    mid, low = high_low(rest)
    moved = matmul(jnp.concatenate([high, mid, low], axis=0), onehot)
    return moved[:rows] + moved[rows : 2 * rows] + moved[2 * rows :]


def dictionary_kernel(half_count, perm_ref, *refs):
    topics, words = refs[0].shape
    wide_ref, tall_ref, total_ref, aligned_ref, onehot_ref = refs[half_count:]
    onehot = (
        lax.broadcasted_iota(jnp.int32, (topics, topics), 0) == perm_ref[...]
    ).astype(jnp.float32)
    onehot_ref[...] = onehot
    total = jnp.zeros((1, topics), jnp.float32)
    for half in range(half_count):
        at = slice(half * words, (half + 1) * words)
        full = refs[half][...]
        high, rest = high_low(full)
        mid, low = high_low(rest)
        wide_ref[:topics, at] = high.astype(jnp.bfloat16)
        wide_ref[topics:, at] = rest.astype(jnp.bfloat16)
        if half == 0:
            turned = onehot.T
            aligned_ref[...] = matmul(
                jnp.concatenate([turned] * 3, axis=1), jnp.concatenate([high, mid, low], axis=0)
            )
        tall = full.T
        total += jnp.sum(tall, axis=0, keepdims=True)
        tall_ref[at, :] = jnp.concatenate(high_low(tall), axis=1).astype(jnp.bfloat16)
    total_ref[...] = jnp.broadcast_to(total, total_ref.shape)


def recon_of(topics, wide):
    rows = topics.shape[0]
    high, low = high_low(topics)
    left = jnp.concatenate(
        [jnp.concatenate([high, high], axis=1), jnp.concatenate([low, low], axis=1)], axis=0
    )
    both = matmul(left, wide)
    return both[:rows] + both[rows:]


def product_of(quotient, tall):
    rows, topics = quotient.shape[0], tall.shape[1] // 2
    both = matmul(jnp.concatenate(high_low(quotient), axis=0), tall)
    both = both[:rows] + both[rows:]
    return both[:, :topics] + both[:, topics:]


def sum_blocks(rows, own, got):
    chips = len(got) + 1
    total = own[: chips * rows]
    for step in range(1, chips):
        total = total + jnp.concatenate(
            [got[step - 1][(c ^ step) * rows : ((c ^ step) + 1) * rows] for c in range(chips)], axis=0
        )
    return total


def first_kernel(chips, wide_ref, tall_ref, *refs):
    payload, (topics_ref, part_ref) = refs[:chips], refs[chips:]
    docs = topics_ref.shape[0] // chips
    span = wide_ref.shape[1]
    topics = jnp.concatenate([ref[:docs, span:] for ref in payload], axis=0)
    topics_ref[...] = topics
    weighted = jnp.concatenate([ref[:docs, :span] for ref in payload], axis=0)
    part_ref[...] = product_of(weighted / recon_of(topics, wide_ref[...]), tall_ref[...])


def update_kernel(chips, wide_ref, tall_ref, before_ref, total_ref, *refs):
    payload, parts, (topics_ref, part_ref) = refs[:chips], refs[chips : 2 * chips], refs[2 * chips :]
    docs = topics_ref.shape[0] // chips
    span = wide_ref.shape[1]
    total = sum_blocks(docs, parts[0][...], [ref[...] for ref in parts[1:]])
    topics = before_ref[...] * total / total_ref[:1]
    topics_ref[...] = topics
    weighted = jnp.concatenate([ref[:docs, :span] for ref in payload], axis=0)
    part_ref[...] = product_of(weighted / recon_of(topics, wide_ref[...]), tall_ref[...])


def numerator_of(topics, quotient):
    high, low = high_low(topics.T)
    quotient_high, quotient_low = high_low(quotient)
    return matmul(
        jnp.concatenate([high, low, high], axis=1),
        jnp.concatenate([quotient_high, quotient_high, quotient_low], axis=0),
    )


def last_kernel(chips, cores, wide_ref, onehot_ref, before_ref, total_ref, *refs):
    payload, parts, (topics_ref, out_ref) = refs[:chips], refs[chips : 2 * chips], refs[2 * chips :]
    docs = topics_ref.shape[0] // chips
    words = wide_ref.shape[1] // cores
    at = slice((cores - 1) * words, cores * words)
    total = sum_blocks(docs, parts[0][...], [ref[...] for ref in parts[1:]])
    topics = before_ref[...] * total / total_ref[:1]
    weighted = jnp.concatenate([ref[:docs, at] for ref in payload], axis=0)
    aligned = moved_columns(topics, onehot_ref[...])
    topics_ref[...] = jnp.concatenate([topics, aligned], axis=1)
    out_ref[:, :words] = numerator_of(aligned, weighted / recon_of(topics, wide_ref[:, at]))
    load = jnp.sum(aligned.T, axis=1, keepdims=True)
    out_ref[:, words:] = jnp.broadcast_to(load, (load.shape[0], out_ref.shape[1] - words))


def own_kernel(chips, wide_ref, topics_ref, *refs):
    payload, out_ref = refs[:chips], refs[chips]
    words = out_ref.shape[1]
    topic_count = out_ref.shape[0]
    topics, aligned = topics_ref[:, :topic_count], topics_ref[:, topic_count:]
    docs = topics.shape[0] // chips
    weighted = jnp.concatenate([ref[:docs, :words] for ref in payload], axis=0)
    out_ref[...] = numerator_of(aligned, weighted / recon_of(topics, wide_ref[:, :words]))


def aligned_kernel(own_ref, sent_ref, got_ref, dict_ref, out_ref):
    words = out_ref.shape[1]
    load = sent_ref[:, words : words + 1] + got_ref[:, words : words + 1]
    out_ref[...] = dict_ref[...] * (own_ref[...] + got_ref[:, :words]) / load


def base_rows_of(refs, base_docs, at):
    return jnp.concatenate([ref[ref.shape[0] - base_docs :, at] for ref in refs], axis=0)


def refit_kernel(chips, half, base_docs, median_ref, *refs):
    payload, before = refs[:chips], refs[chips:-4]
    wide_ref, tall_ref, part_ref, total_ref = refs[-4:]
    topics, words = median_ref.shape
    span = payload[0].shape[1] - topics
    high, low = high_low(median_ref[...])
    wide = jnp.concatenate([high, low], axis=0).astype(jnp.bfloat16)
    wide_ref[...] = wide
    tall_full = median_ref[...].T
    total = jnp.sum(tall_full, axis=0, keepdims=True)
    tall = jnp.concatenate(high_low(tall_full), axis=1).astype(jnp.bfloat16)
    tall_ref[...] = tall
    weighted = base_rows_of(payload, base_docs, slice(half * words, (half + 1) * words))
    refit = base_rows_of(payload, base_docs, slice(span, span + topics))
    part = product_of(weighted / recon_of(refit, wide), tall)
    if before:
        part = part + before[0][...]
        total = total + before[1][:1]
    part_ref[: part.shape[0]] = part
    if part_ref.shape[0] > part.shape[0]:
        part_ref[part.shape[0] :] = jnp.broadcast_to(total, (8, topics))
    total_ref[...] = jnp.broadcast_to(total, total_ref.shape)


def refit_again_kernel(chips, cores, base_docs, *refs):
    payload, parts, halves, (topics_ref, part_ref, total_ref) = (
        refs[:chips],
        refs[chips : 2 * chips],
        refs[2 * chips : -3],
        refs[-3:],
    )
    rows, topics = topics_ref.shape
    span = payload[0].shape[1] - topics
    words = span // cores
    total = sum_blocks(base_docs, parts[0][...], [ref[...] for ref in parts[1:]])
    median_total = parts[0][rows : rows + 1]
    for ref in parts[1:]:
        median_total = median_total + ref[rows : rows + 1]
    refit = base_rows_of(payload, base_docs, slice(span, span + topics)) * total / median_total
    topics_ref[...] = refit
    total_ref[...] = jnp.broadcast_to(median_total, total_ref.shape)
    part = jnp.zeros((rows, topics), jnp.float32)
    for half in range(cores):
        weighted = base_rows_of(payload, base_docs, slice(half * words, (half + 1) * words))
        wide_ref, tall_ref = halves[2 * half], halves[2 * half + 1]
        part = part + product_of(weighted / recon_of(refit, wide_ref[...]), tall_ref[...])
    part_ref[...] = part


def per_device(counts, tile_mask, member_topics, start_dict, align_perm, base_counts, base_topics):
    doc_size = lax.axis_size("doc")
    members = lax.axis_size("pert")
    cores = 2 - doc_size % 2
    chips = doc_size // cores
    at_pert = lax.axis_index("pert")
    at_doc = lax.axis_index("doc")
    at_chip, at_core = at_doc // cores, at_doc % cores
    docs = counts.shape[1]
    base_docs = base_counts.shape[0]
    topic_count = member_topics.shape[2]
    owned = start_dict.shape[1]
    span = cores * owned
    rows = chips * docs
    sub = owned // members

    def over_chips(array, step):
        return lax.ppermute(
            array,
            "doc",
            [
                (c * cores + k, (c ^ step) * cores + (k + step) % cores)
                for c in range(chips)
                for k in range(cores)
            ],
        )

    def over_cores(array):
        return lax.ppermute(array, "doc", [(d, d ^ 1) for d in range(doc_size)])

    def over_pert(array, step):
        return lax.ppermute(array, "pert", [(m, m ^ step) for m in range(members)])

    paired = min(chips, 2)
    sent = pl.pallas_call(
        functools.partial(spread_kernel, chips, cores, owned),
        out_shape=[
            shape(docs + (base_docs if step < paired else 0), span + topic_count)
            for step in range(chips)
        ]
        + [shape(base_docs, span + topic_count) for _ in range(paired, chips)],
        in_specs=[pl.BlockSpec(memory_space=pltpu.HBM)] * 5,
        scratch_shapes=[
            pltpu.VMEM(counts.shape[1:], jnp.int32),
            pltpu.VMEM(tile_mask.shape[1:], jnp.int32),
            pltpu.VMEM(member_topics.shape[1:], jnp.float32),
            pltpu.VMEM(base_counts.shape, jnp.int32),
            pltpu.VMEM(base_topics.shape, jnp.float32),
            pltpu.SemaphoreType.DMA((5,)),
        ],
        compiler_params=pltpu.CompilerParams(vmem_limit_bytes=SPREAD_BYTES),
        cost_estimate=pl.CostEstimate(flops=0, bytes_accessed=12 * counts.size, transcendentals=0),
    )(counts[0], tile_mask[0], member_topics[0], base_counts, base_topics)
    sent, base_sent = sent[:chips], sent[chips:]
    got = [over_chips(sent[step], step) for step in range(1, chips)]
    payload = [sent[0]] + got
    dict_own = start_dict[0].T
    halves = [dict_own] + [over_cores(dict_own)] * (cores - 1)
    sent, halves = lax.optimization_barrier((sent, halves))
    wide, tall, col_part, dict_own, onehot = call(
        functools.partial(dictionary_kernel, cores),
        [
            shape(2 * topic_count, span, dtype=jnp.bfloat16),
            shape(span, 2 * topic_count, dtype=jnp.bfloat16),
            shape(8, topic_count),
            shape(topic_count, owned),
            shape(topic_count, topic_count),
        ],
        align_perm,
        *halves,
        moved=4 * 4 * span * topic_count,
    )

    update_flops = 2 * 2 * 4 * rows * topic_count * span
    topics, part = call(
        functools.partial(first_kernel, chips),
        [shape(rows, topic_count), shape(rows, topic_count)],
        wide,
        tall,
        *payload,
        flops=update_flops,
        moved=4 * span * (rows + 2 * topic_count),
    )
    part = jnp.concatenate([part, col_part], axis=0)
    parts = [part] + [over_chips(part, step) for step in range(1, chips)]
    col_total = sum(p[rows:] for p in parts)
    for update in range(1, UPDATES):
        topics, part = call(
            functools.partial(update_kernel, chips),
            [shape(rows, topic_count), shape(rows, topic_count)],
            wide,
            tall,
            topics,
            col_total,
            *payload,
            *parts,
            flops=update_flops,
            moved=4 * span * (rows + 2 * topic_count),
        )
        parts = [part] + [over_chips(part, step) for step in range(1, chips)]

    topics, numerator = call(
        functools.partial(last_kernel, chips, cores),
        [shape(rows, 2 * topic_count), shape(topic_count, owned + 128)],
        wide,
        onehot,
        topics,
        col_total,
        *payload,
        *parts,
        flops=update_flops // 2,
        moved=2 * span * (rows + 2 * topic_count),
    )
    if cores > 1:
        got_half = over_cores(numerator)
        own_half = call(
            functools.partial(own_kernel, chips),
            shape(topic_count, owned),
            wide,
            topics,
            *payload,
            flops=update_flops // 2,
            moved=2 * span * (rows + 2 * topic_count),
        )
    else:
        got_half = jnp.zeros_like(numerator)
        own_half = numerator[:, :owned]
    aligned = call(
        aligned_kernel,
        shape(topic_count, owned),
        own_half,
        numerator,
        got_half,
        dict_own,
        moved=16 * topic_count * owned,
    )

    def words_of(array, member):
        return lax.dynamic_slice_in_dim(array, member * sub, sub, 1)

    aligned, base_sent = lax.optimization_barrier((aligned, base_sent))
    base_got = [over_chips(base_sent[step - paired], step) for step in range(paired, chips)]
    pieces = [words_of(aligned, at_pert)] + [
        over_pert(words_of(aligned, at_pert ^ step), step) for step in range(1, members)
    ]
    late = len(base_got) // 2
    pieces[1], base_got[late:] = lax.optimization_barrier((pieces[1], base_got[late:]))
    median = middle(pieces)
    gathered = [over_pert(median, step) for step in range(1, members)]
    gathered[0], base_got[:late] = lax.optimization_barrier((gathered[0], base_got[:late]))
    median_own = jnp.zeros((topic_count, owned), jnp.float32)
    for step, piece in enumerate([median] + gathered):
        median_own = lax.dynamic_update_slice_in_dim(median_own, piece, (at_pert ^ step) * sub, 1)
    base_all = list(payload[:paired]) + list(base_got)

    median_halves = [median_own] + [over_cores(median_own)] * (cores - 1)
    base_rows = chips * base_docs
    refit_flops = 2 * 2 * 4 * base_rows * topic_count * owned
    forms, before = [], []
    for half in range(cores):
        last = half == cores - 1
        wide, tall, part, total = call(
            functools.partial(refit_kernel, chips, half, base_docs),
            [
                shape(2 * topic_count, owned, dtype=jnp.bfloat16),
                shape(owned, 2 * topic_count, dtype=jnp.bfloat16),
                shape(base_rows + (8 if last else 0), topic_count),
                shape(8, topic_count),
            ],
            median_halves[half],
            *base_all,
            *before,
            flops=refit_flops,
            moved=16 * owned * topic_count,
        )
        forms += [wide, tall]
        before = [part, total]
    parts = [part] + [over_chips(part, step) for step in range(1, chips)]
    refit, part, median_total = call(
        functools.partial(refit_again_kernel, chips, cores, base_docs),
        [shape(base_rows, topic_count), shape(base_rows, topic_count), shape(8, topic_count)],
        *base_all,
        *parts,
        *forms,
        flops=2 * refit_flops,
        moved=16 * owned * topic_count,
    )
    total = part[:base_docs]
    for step in range(1, chips):
        total = total + over_chips(part[step * base_docs : (step + 1) * base_docs], step)
    refit = refit[:base_docs] * total / median_total[:1]
    return (median.T[None, None], refit)


def solution(mesh):
    return jax.shard_map(
        per_device,
        mesh=mesh,
        in_specs=(
            P("pert", "doc", None),
            P("pert", "doc", None),
            P("pert", "doc", None),
            P("pert", "doc", None),
            P("pert", None),
            P(("pert", "doc"), None),
            P(("pert", "doc"), None),
        ),
        out_specs=(P("doc", "pert", None, None), P(("pert", "doc"), None)),
        check_vma=False,
    )
```

```python
import functools

import jax
import jax.numpy as jnp
from jax import lax
from jax.experimental import pallas as pl
from jax.experimental.pallas import tpu as pltpu
from jax.sharding import PartitionSpec as P

UPDATES = 3
REFITS = 2

EXACT = lax.Precision.HIGHEST
ROUGH = lax.Precision.HIGH
VMEM_BYTES = 14 * 1024 * 1024
SPREAD_BYTES = 60 * 1024 * 1024


def dot(left, right, dims, precision=ROUGH):
    return lax.dot_general(left, right, (dims, ((), ())), precision=precision)


def middle(pieces):
    pieces = list(pieces)
    count = len(pieces)
    for turn in range(count):
        for low in range(turn % 2, count - 1, 2):
            pieces[low], pieces[low + 1] = (
                jnp.minimum(pieces[low], pieces[low + 1]),
                jnp.maximum(pieces[low], pieces[low + 1]),
            )
    return 0.5 * (pieces[count // 2 - 1] + pieces[count // 2])


def call(kernel, outs, *args, flops=0, moved=0, unread=0):
    read = len(args) - unread
    return pl.pallas_call(
        kernel,
        out_shape=outs,
        in_specs=[pl.BlockSpec(memory_space=pltpu.VMEM)] * read
        + [pl.BlockSpec(memory_space=pl.ANY)] * unread,
        compiler_params=pltpu.CompilerParams(vmem_limit_bytes=VMEM_BYTES),
        cost_estimate=pl.CostEstimate(flops=flops, bytes_accessed=moved, transcendentals=0),
    )(*args)


def shape(*dims, dtype=jnp.float32):
    return jax.ShapeDtypeStruct(dims, dtype)


def high_low(x):
    high = x.astype(jnp.bfloat16).astype(jnp.float32)
    return high, x - high


def matmul(left, right):
    return jnp.dot(
        left.astype(jnp.bfloat16), right.astype(jnp.bfloat16), preferred_element_type=jnp.float32
    )


def blocks_of(chips, cores, step):
    at_doc = lax.axis_index("doc")
    at_chip, at_core = at_doc // cores, at_doc % cores
    return [(at_chip ^ step) * cores + (at_core ^ ((step + half) % cores)) for half in range(cores)]


def spread_kernel(chips, cores, own_words, mask_hbm, topics_hbm, counts_hbm, *refs):
    out_hbms, (mask_ref, topics_ref, counts_ref, out_ref, small_sems, in_sems, out_sems) = (
        refs[:chips],
        refs[chips:],
    )
    small = [
        pltpu.make_async_copy(mask_hbm, mask_ref, small_sems.at[0]),
        pltpu.make_async_copy(topics_hbm, topics_ref, small_sems.at[1]),
    ]
    for copy in small:
        copy.start()
    steps = list(range(chips - 1, -1, -1))
    arriving = {}
    for step in steps:
        for half, block in enumerate(blocks_of(chips, cores, step)):
            at = slice(half * own_words, (half + 1) * own_words)
            arriving[step, half] = pltpu.make_async_copy(
                counts_hbm.at[:, pl.ds(pl.multiple_of(block * own_words, 128), own_words)],
                counts_ref.at[step, :, at],
                in_sems.at[step, half],
            )
            arriving[step, half].start()
    docs, tiles = mask_ref.shape
    width = chips * cores * own_words // tiles
    own_tiles = own_words // width
    tile_ids = lax.broadcasted_iota(jnp.int32, (docs, tiles), 1)
    doc_ids = lax.axis_index("doc") * docs + lax.broadcasted_iota(jnp.int32, (docs, tiles), 0)
    forced = (tile_ids == doc_ids % tiles).astype(jnp.int32)
    for copy in small:
        copy.wait()
    occupied = jnp.maximum(mask_ref[...], forced).astype(jnp.float32)
    leaving = []
    for step in steps:
        for half, block in enumerate(blocks_of(chips, cores, step)):
            near = pltpu.roll(occupied, lax.rem(tiles - block * own_tiles, tiles), 1)
            arriving[step, half].wait()
            for tile in range(own_tiles):
                at = slice(half * own_words + tile * width, half * own_words + (tile + 1) * width)
                picked = counts_ref[step, :, at].astype(jnp.float32)
                out_ref[step, :, at] = picked * near[:, tile : tile + 1]
        out_ref[step, :, cores * own_words :] = topics_ref[...]
        leaving.append(pltpu.make_async_copy(out_ref.at[step], out_hbms[step], out_sems.at[step]))
        leaving[-1].start()
    for copy in leaving:
        copy.wait()


def base_kernel(chips, cores, counts_ref, topics_ref, *out_refs):
    span = out_refs[0].shape[1] - topics_ref.shape[1]
    own_words = span // cores
    for step in range(chips):
        for half, block in enumerate(blocks_of(chips, cores, step)):
            at = slice(half * own_words, (half + 1) * own_words)
            first = pl.multiple_of(block * own_words, 128)
            out_refs[step][:, at] = counts_ref[:, pl.ds(first, own_words)].astype(jnp.float32)
        out_refs[step][:, span:] = topics_ref[...]


def moved_columns(x, onehot):
    rows = x.shape[0]
    high, rest = high_low(x)
    mid, low = high_low(rest)
    moved = matmul(jnp.concatenate([high, mid, low], axis=0), onehot)
    return moved[:rows] + moved[rows : 2 * rows] + moved[2 * rows :]


def dictionary_kernel(half_count, perm_ref, *refs):
    topics, words = refs[0].shape
    wide_ref, tall_ref, total_ref, aligned_ref, onehot_ref = refs[half_count:]
    onehot = (
        lax.broadcasted_iota(jnp.int32, (topics, topics), 0) == perm_ref[...]
    ).astype(jnp.float32)
    onehot_ref[...] = onehot
    total = jnp.zeros((1, topics), jnp.float32)
    for half in range(half_count):
        at = slice(half * words, (half + 1) * words)
        full = refs[half][...]
        high, rest = high_low(full)
        mid, low = high_low(rest)
        wide_ref[:topics, at] = high.astype(jnp.bfloat16)
        wide_ref[topics:, at] = rest.astype(jnp.bfloat16)
        if half == 0:
            turned = onehot.T
            aligned_ref[...] = matmul(
                jnp.concatenate([turned] * 3, axis=1), jnp.concatenate([high, mid, low], axis=0)
            )
        tall = full.T
        total += jnp.sum(tall, axis=0, keepdims=True)
        tall_ref[at, :] = jnp.concatenate(high_low(tall), axis=1).astype(jnp.bfloat16)
    total_ref[...] = jnp.broadcast_to(total, total_ref.shape)


def recon_of(topics, wide):
    rows = topics.shape[0]
    high, low = high_low(topics)
    left = jnp.concatenate(
        [jnp.concatenate([high, high], axis=1), jnp.concatenate([low, low], axis=1)], axis=0
    )
    both = matmul(left, wide)
    return both[:rows] + both[rows:]


def product_of(quotient, tall):
    rows, topics = quotient.shape[0], tall.shape[1] // 2
    both = matmul(jnp.concatenate(high_low(quotient), axis=0), tall)
    both = both[:rows] + both[rows:]
    return both[:, :topics] + both[:, topics:]


def sum_blocks(rows, own, got):
    got = got[::-1]
    chips = len(got) + 1
    total = own[: chips * rows]
    for step in range(1, chips):
        total = total + jnp.concatenate(
            [got[step - 1][(c ^ step) * rows : ((c ^ step) + 1) * rows] for c in range(chips)], axis=0
        )
    return total


def first_kernel(chips, wide_ref, tall_ref, *refs):
    payload, (topics_ref, part_ref) = refs[:chips][::-1], refs[-2:]
    docs = topics_ref.shape[0] // chips
    span = wide_ref.shape[1]
    topics = jnp.concatenate([ref[:, span:] for ref in payload], axis=0)
    topics_ref[...] = topics
    weighted = jnp.concatenate([ref[:, :span] for ref in payload], axis=0)
    part_ref[...] = product_of(weighted / recon_of(topics, wide_ref[...]), tall_ref[...])


def update_kernel(chips, wide_ref, tall_ref, before_ref, *refs):
    docs = before_ref.shape[0] // chips
    first = refs[-1].shape[0] == 8
    if first:
        payload, parts, (topics_ref, part_ref, total_ref) = refs[:chips][::-1], refs[chips:-3], refs[-3:]
        got = [ref[...] for ref in parts]
        total_ref[...] = sum(part[chips * docs :] for part in got)
    else:
        total_ref, payload, parts = refs[0], refs[1 : chips + 1][::-1], refs[chips + 1 : -2]
        topics_ref, part_ref = refs[-2:]
        got = [ref[...] for ref in parts]
    span = wide_ref.shape[1]
    topics = before_ref[...] * sum_blocks(docs, got[0], got[1:]) / total_ref[:1]
    topics_ref[...] = topics
    weighted = jnp.concatenate([ref[:, :span] for ref in payload], axis=0)
    part_ref[...] = product_of(weighted / recon_of(topics, wide_ref[...]), tall_ref[...])


def numerator_of(topics, quotient):
    high, low = high_low(topics.T)
    quotient_high, quotient_low = high_low(quotient)
    return matmul(
        jnp.concatenate([high, low, high], axis=1),
        jnp.concatenate([quotient_high, quotient_high, quotient_low], axis=0),
    )


def last_kernel(chips, cores, wide_ref, onehot_ref, before_ref, total_ref, *refs):
    payload, parts, (topics_ref, out_ref) = refs[:chips][::-1], refs[chips : 2 * chips], refs[2 * chips :]
    docs = topics_ref.shape[0] // chips
    words = wide_ref.shape[1] // cores
    at = slice((cores - 1) * words, cores * words)
    total = sum_blocks(docs, parts[0][...], [ref[...] for ref in parts[1:]])
    topics = before_ref[...] * total / total_ref[:1]
    weighted = jnp.concatenate([ref[:, at] for ref in payload], axis=0)
    aligned = moved_columns(topics, onehot_ref[...])
    topics_ref[...] = jnp.concatenate([topics, aligned], axis=1)
    out_ref[:, :words] = numerator_of(aligned, weighted / recon_of(topics, wide_ref[:, at]))
    load = jnp.sum(aligned.T, axis=1, keepdims=True)
    out_ref[:, words:] = jnp.broadcast_to(load, (load.shape[0], out_ref.shape[1] - words))


def own_kernel(chips, wide_ref, topics_ref, *refs):
    payload, out_ref = refs[:chips][::-1], refs[chips]
    words = out_ref.shape[1]
    topic_count = out_ref.shape[0]
    topics, aligned = topics_ref[:, :topic_count], topics_ref[:, topic_count:]
    docs = topics.shape[0] // chips
    weighted = jnp.concatenate([ref[:, :words] for ref in payload], axis=0)
    out_ref[...] = numerator_of(aligned, weighted / recon_of(topics, wide_ref[:, :words]))


def aligned_kernel(own_ref, sent_ref, got_ref, dict_ref, out_ref):
    words = out_ref.shape[1]
    load = sent_ref[:, words : words + 1] + got_ref[:, words : words + 1]
    out_ref[...] = dict_ref[...] * (own_ref[...] + got_ref[:, :words]) / load


def base_rows_of(refs, at):
    return jnp.concatenate([ref[:, at] for ref in refs], axis=0)


def refit_kernel(chips, half, median_ref, *refs):
    payload, refs = refs[:chips], refs[chips:]
    if half == 0:
        before, (sub_ref, wide_ref, tall_ref, part_ref, sub_out_ref) = [], refs
        sub_out_ref[...] = sub_ref[...]
    else:
        *before, wide_ref, tall_ref, part_ref = refs
    topics, words = median_ref.shape
    span = payload[0].shape[1] - topics
    high, low = high_low(median_ref[...])
    wide = jnp.concatenate([high, low], axis=0).astype(jnp.bfloat16)
    wide_ref[...] = wide
    tall_full = median_ref[...].T
    total = jnp.broadcast_to(jnp.sum(tall_full, axis=0, keepdims=True), (8, topics))
    tall = jnp.concatenate(high_low(tall_full), axis=1).astype(jnp.bfloat16)
    tall_ref[...] = tall
    weighted = base_rows_of(payload, slice(half * words, (half + 1) * words))
    refit = base_rows_of(payload, slice(span, span + topics))
    part = product_of(weighted / recon_of(refit, wide), tall)
    rows = part.shape[0]
    if before:
        part = part + before[0][:rows]
        total = total + before[0][rows:]
    part_ref[:rows] = part
    part_ref[rows:] = total


def refit_again_kernel(chips, cores, base_docs, *refs):
    payload, parts, halves = refs[:chips], refs[chips : 2 * chips], refs[2 * chips : 2 * (chips + cores)]
    scale_ref, *part_refs = refs[2 * (chips + cores) :]
    topics = scale_ref.shape[1]
    rows = chips * base_docs
    span = payload[0].shape[1] - topics
    words = span // cores
    got = [ref[...] for ref in parts]
    median_total = sum(part[rows : rows + 1] for part in got)
    total = sum_blocks(base_docs, got[0], got[1:])
    refit = base_rows_of(payload, slice(span, span + topics)) * total / median_total
    scale_ref[...] = refit[:base_docs] / median_total
    part = jnp.zeros((rows, topics), jnp.float32)
    for half in range(cores):
        weighted = base_rows_of(payload, slice(half * words, (half + 1) * words))
        wide_ref, tall_ref = halves[2 * half], halves[2 * half + 1]
        part = part + product_of(weighted / recon_of(refit, wide_ref[...]), tall_ref[...])
    for step in range(chips):
        part_refs[step][...] = part[step * base_docs : (step + 1) * base_docs]


def finish_kernel(scale_ref, *refs):
    parts, out_ref = refs[:-1], refs[-1]
    out_ref[...] = scale_ref[...] * sum(ref[...] for ref in parts)


def median_kernel(members, *refs):
    refs[-1][...] = middle([ref[...] for ref in refs[:members]])


def assemble_kernel(members, *refs):
    out_ref = refs[-1]
    sub = refs[0].shape[1]
    for me in range(members):

        @pl.when(lax.axis_index("pert") == me)
        def _():
            for at in range(members):
                step = (members - at) % members
                owner = me ^ step
                out_ref[:, owner * sub : (owner + 1) * sub] = refs[at][...]


def per_device(counts, tile_mask, member_topics, start_dict, align_perm, base_counts, base_topics):
    doc_size = lax.axis_size("doc")
    members = lax.axis_size("pert")
    cores = 2 - doc_size % 2
    chips = doc_size // cores
    at_pert = lax.axis_index("pert")
    at_doc = lax.axis_index("doc")
    at_chip, at_core = at_doc // cores, at_doc % cores
    docs = counts.shape[1]
    base_docs = base_counts.shape[0]
    topic_count = member_topics.shape[2]
    owned = start_dict.shape[1]
    span = cores * owned
    rows = chips * docs
    sub = owned // members

    def over_chips(array, step):
        return lax.ppermute(
            array,
            "doc",
            [
                (c * cores + k, (c ^ step) * cores + (k + step) % cores)
                for c in range(chips)
                for k in range(cores)
            ],
        )

    def over_cores(array):
        return lax.ppermute(array, "doc", [(d, d ^ 1) for d in range(doc_size)])

    def over_pert(array, step):
        return lax.ppermute(array, "pert", [(m, m ^ step) for m in range(members)])

    sent = pl.pallas_call(
        functools.partial(spread_kernel, chips, cores, owned),
        out_shape=[shape(docs, span + topic_count)] * chips,
        in_specs=[pl.BlockSpec(memory_space=pl.ANY)] * 3,
        out_specs=[pl.BlockSpec(memory_space=pl.ANY)] * chips,
        scratch_shapes=[
            pltpu.VMEM(tile_mask.shape[1:], jnp.int32),
            pltpu.VMEM(member_topics.shape[1:], jnp.float32),
            pltpu.VMEM((chips, docs, span), jnp.int32),
            pltpu.VMEM((chips, docs, span + topic_count), jnp.float32),
            pltpu.SemaphoreType.DMA((2,)),
            pltpu.SemaphoreType.DMA((chips, cores)),
            pltpu.SemaphoreType.DMA((chips,)),
        ],
        compiler_params=pltpu.CompilerParams(vmem_limit_bytes=SPREAD_BYTES),
        cost_estimate=pl.CostEstimate(flops=0, bytes_accessed=12 * counts.size, transcendentals=0),
    )(tile_mask[0], member_topics[0], counts[0])
    base_sent = call(
        functools.partial(base_kernel, chips, cores),
        [shape(base_docs, span + topic_count)] * chips,
        base_counts,
        base_topics,
        moved=8 * base_counts.size,
    )
    got = [over_chips(sent[step], step) for step in range(chips - 1, 0, -1)][::-1]
    payload = [sent[0]] + got
    near = [over_chips(base_sent[step], step) for step in range(1, min(chips, 2))]
    dict_own = start_dict[0].T
    halves = [dict_own] + [over_cores(dict_own)] * (cores - 1)
    wide, tall, col_part, dict_own, onehot = call(
        functools.partial(dictionary_kernel, cores),
        [
            shape(2 * topic_count, span, dtype=jnp.bfloat16),
            shape(span, 2 * topic_count, dtype=jnp.bfloat16),
            shape(8, topic_count),
            shape(topic_count, owned),
            shape(topic_count, topic_count),
        ],
        align_perm,
        *halves,
        moved=4 * 4 * span * topic_count,
    )

    update_flops = 2 * 2 * 4 * rows * topic_count * span
    topics, part = call(
        functools.partial(first_kernel, chips),
        [shape(rows, topic_count), shape(rows, topic_count)],
        wide,
        tall,
        *payload[::-1],
        *near,
        unread=len(near),
        flops=update_flops,
        moved=4 * span * (rows + 2 * topic_count),
    )
    part = jnp.concatenate([part, col_part], axis=0)
    parts = [part] + [over_chips(part, step) for step in range(chips - 1, 0, -1)]
    totals = []
    for update in range(1, UPDATES):
        topics, part, *new_totals = call(
            functools.partial(update_kernel, chips),
            [shape(rows, topic_count), shape(rows, topic_count)]
            + ([] if totals else [shape(8, topic_count)]),
            wide,
            tall,
            topics,
            *totals,
            *payload[::-1],
            *parts,
            flops=update_flops,
            moved=4 * span * (rows + 2 * topic_count),
        )
        totals = totals or new_totals
        parts = [part] + [over_chips(part, step) for step in range(chips - 1, 0, -1)]
    (col_total,) = totals

    topics, numerator = call(
        functools.partial(last_kernel, chips, cores),
        [shape(rows, 2 * topic_count), shape(topic_count, owned + 128)],
        wide,
        onehot,
        topics,
        col_total,
        *payload[::-1],
        *parts,
        flops=update_flops // 2,
        moved=2 * span * (rows + 2 * topic_count),
    )
    if cores > 1:
        got_half = over_cores(numerator)
        own_half = call(
            functools.partial(own_kernel, chips),
            shape(topic_count, owned),
            wide,
            topics,
            *payload[::-1],
            flops=update_flops // 2,
            moved=2 * span * (rows + 2 * topic_count),
        )
    else:
        got_half = jnp.zeros_like(numerator)
        own_half = numerator[:, :owned]
    aligned = call(
        aligned_kernel,
        shape(topic_count, owned),
        own_half,
        numerator,
        got_half,
        dict_own,
        moved=16 * topic_count * owned,
    )

    def words_of(array, member):
        return lax.dynamic_slice_in_dim(array, member * sub, sub, 1)

    aligned, base_sent = lax.optimization_barrier((aligned, base_sent))
    base_got = [over_chips(base_sent[step], step) for step in range(2, chips)]
    late = len(base_got) // 2
    median = call(
        functools.partial(median_kernel, members),
        shape(topic_count, sub),
        words_of(aligned, at_pert),
        *[over_pert(words_of(aligned, at_pert ^ step), step) for step in range(members - 1, 0, -1)],
        *base_got[late:],
        unread=len(base_got) - late,
    )
    median_own = call(
        functools.partial(assemble_kernel, members),
        shape(topic_count, owned),
        median,
        *[over_pert(median, step) for step in range(members - 1, 0, -1)],
        *base_got[:late],
        unread=late,
    )
    base_all = [base_sent[0]] + near + base_got

    median_halves = [median_own] + [over_cores(median_own)] * (cores - 1)
    base_rows = chips * base_docs
    refit_flops = 2 * 2 * 4 * base_rows * topic_count * owned
    forms, before = [], [median]
    for half in range(cores):
        wide, tall, part, *own_median = call(
            functools.partial(refit_kernel, chips, half),
            [
                shape(2 * topic_count, owned, dtype=jnp.bfloat16),
                shape(owned, 2 * topic_count, dtype=jnp.bfloat16),
                shape(base_rows + 8, topic_count),
            ]
            + ([] if half else [shape(topic_count, sub)]),
            median_halves[half],
            *base_all,
            *before,
            flops=refit_flops,
            moved=16 * owned * topic_count,
        )
        forms += [wide, tall]
        before = [part]
        median = own_median[0] if own_median else median
    scale, *parts = call(
        functools.partial(refit_again_kernel, chips, cores, base_docs),
        [shape(base_docs, topic_count)] * (chips + 1),
        *base_all,
        part,
        *[over_chips(part, step) for step in range(chips - 1, 0, -1)],
        *forms,
        flops=2 * refit_flops,
        moved=16 * owned * topic_count,
    )
    refit = call(
        finish_kernel,
        shape(base_docs, topic_count),
        scale,
        parts[0],
        *[over_chips(parts[step], step) for step in range(chips - 1, 0, -1)],
    )
    return (median.T[None, None], refit)


def solution(mesh):
    return jax.shard_map(
        per_device,
        mesh=mesh,
        in_specs=(
            P("pert", "doc", None),
            P("pert", "doc", None),
            P("pert", "doc", None),
            P("pert", "doc", None),
            P("pert", None),
            P(("pert", "doc"), None),
            P(("pert", "doc"), None),
        ),
        out_specs=(P("doc", "pert", None, None), P(("pert", "doc"), None)),
        check_vma=False,
    )
```

```python
import functools

import jax
import jax.numpy as jnp
from jax import lax
from jax.experimental import pallas as pl
from jax.experimental.pallas import tpu as pltpu
from jax.sharding import PartitionSpec as P

UPDATES = 3
REFITS = 2

EXACT = lax.Precision.HIGHEST
ROUGH = lax.Precision.HIGH
VMEM_BYTES = 14 * 1024 * 1024
SPREAD_BYTES = 60 * 1024 * 1024


def dot(left, right, dims, precision=ROUGH):
    return lax.dot_general(left, right, (dims, ((), ())), precision=precision)


def middle(pieces):
    pieces = list(pieces)
    count = len(pieces)
    for turn in range(count):
        for low in range(turn % 2, count - 1, 2):
            pieces[low], pieces[low + 1] = (
                jnp.minimum(pieces[low], pieces[low + 1]),
                jnp.maximum(pieces[low], pieces[low + 1]),
            )
    return 0.5 * (pieces[count // 2 - 1] + pieces[count // 2])


def call(kernel, outs, *args, flops=0, moved=0, unread=0, scratch=()):
    read = len(args) - unread
    return pl.pallas_call(
        kernel,
        out_shape=outs,
        in_specs=[pl.BlockSpec(memory_space=pltpu.VMEM)] * read
        + [pl.BlockSpec(memory_space=pl.ANY)] * unread,
        scratch_shapes=scratch,
        compiler_params=pltpu.CompilerParams(vmem_limit_bytes=VMEM_BYTES),
        cost_estimate=pl.CostEstimate(flops=flops, bytes_accessed=moved, transcendentals=0),
    )(*args)


def shape(*dims, dtype=jnp.float32):
    return jax.ShapeDtypeStruct(dims, dtype)


def high_low(x):
    high = x.astype(jnp.bfloat16).astype(jnp.float32)
    return high, x - high


def matmul(left, right):
    return jnp.dot(
        left.astype(jnp.bfloat16), right.astype(jnp.bfloat16), preferred_element_type=jnp.float32
    )


def blocks_of(chips, cores, step):
    at_doc = lax.axis_index("doc")
    at_chip, at_core = at_doc // cores, at_doc % cores
    return [(at_chip ^ step) * cores + (at_core ^ ((step + half) % cores)) for half in range(cores)]


def spread_kernel(chips, cores, own_words, mask_hbm, topics_hbm, counts_hbm, *refs):
    out_refs, (mask_ref, topics_ref, counts_ref, small_sems, in_sems) = (
        refs[:chips],
        refs[chips:],
    )
    small = [
        pltpu.make_async_copy(mask_hbm, mask_ref, small_sems.at[0]),
        pltpu.make_async_copy(topics_hbm, topics_ref, small_sems.at[1]),
    ]
    for copy in small:
        copy.start()
    steps = list(range(chips - 1, -1, -1))
    arriving = {}
    for step in steps:
        for half, block in enumerate(blocks_of(chips, cores, step)):
            at = slice(half * own_words, (half + 1) * own_words)
            arriving[step, half] = pltpu.make_async_copy(
                counts_hbm.at[:, pl.ds(pl.multiple_of(block * own_words, 128), own_words)],
                counts_ref.at[step, :, at],
                in_sems.at[step, half],
            )
            arriving[step, half].start()
    docs, tiles = mask_ref.shape
    width = chips * cores * own_words // tiles
    own_tiles = own_words // width
    tile_ids = lax.broadcasted_iota(jnp.int32, (docs, tiles), 1)
    doc_ids = lax.axis_index("doc") * docs + lax.broadcasted_iota(jnp.int32, (docs, tiles), 0)
    forced = (tile_ids == doc_ids % tiles).astype(jnp.int32)
    for copy in small:
        copy.wait()
    occupied = jnp.maximum(mask_ref[...], forced).astype(jnp.float32)
    for step in steps:
        for half, block in enumerate(blocks_of(chips, cores, step)):
            near = pltpu.roll(occupied, lax.rem(tiles - block * own_tiles, tiles), 1)
            arriving[step, half].wait()
            for tile in range(own_tiles):
                at = slice(half * own_words + tile * width, half * own_words + (tile + 1) * width)
                picked = counts_ref[step, :, at].astype(jnp.float32)
                out_refs[step][:, at] = picked * near[:, tile : tile + 1]
        out_refs[step][:, cores * own_words :] = jnp.concatenate([topics_ref[...]] * 2, axis=1)


def base_kernel(chips, cores, counts_ref, topics_ref, *out_refs):
    span = out_refs[0].shape[1] - 2 * topics_ref.shape[1]
    own_words = span // cores
    for step in range(chips):
        for half, block in enumerate(blocks_of(chips, cores, step)):
            at = slice(half * own_words, (half + 1) * own_words)
            first = pl.multiple_of(block * own_words, 128)
            out_refs[step][:, at] = counts_ref[:, pl.ds(first, own_words)].astype(jnp.float32)
        out_refs[step][:, span:] = jnp.concatenate([topics_ref[...]] * 2, axis=1)


def moved_columns(x, onehot):
    rows = x.shape[0]
    high, rest = high_low(x)
    mid, low = high_low(rest)
    moved = matmul(jnp.concatenate([high, mid, low], axis=0), onehot)
    return moved[:rows] + moved[rows : 2 * rows] + moved[2 * rows :]


def dictionary_kernel(half_count, perm_ref, *refs):
    topics, words = refs[0].shape
    wide_ref, tall_ref, total_ref, aligned_ref, onehot_ref = refs[half_count:]
    onehot = (
        lax.broadcasted_iota(jnp.int32, (topics, topics), 0) == perm_ref[...]
    ).astype(jnp.float32)
    onehot_ref[...] = onehot
    total = jnp.zeros((1, topics), jnp.float32)
    for half in range(half_count):
        at = slice(half * words, (half + 1) * words)
        full = refs[half][...]
        high, rest = high_low(full)
        mid, low = high_low(rest)
        wide_ref[:topics, at] = high.astype(jnp.bfloat16)
        wide_ref[topics:, at] = rest.astype(jnp.bfloat16)
        if half == 0:
            turned = onehot.T
            aligned_ref[...] = matmul(
                jnp.concatenate([turned] * 3, axis=1), jnp.concatenate([high, mid, low], axis=0)
            )
        tall = full.T
        total += jnp.sum(tall, axis=0, keepdims=True)
        tall_ref[at, :] = jnp.concatenate(high_low(tall), axis=1).astype(jnp.bfloat16)
    total_ref[...] = jnp.concatenate([jnp.broadcast_to(total, (8, topics))] * 2, axis=1)


def recon_of(doubled, wide):
    rows = doubled.shape[0]
    both = matmul(jnp.concatenate(high_low(doubled), axis=0), wide)
    return both[:rows] + both[rows:]


def product_of(quotient, tall):
    rows = quotient.shape[0]
    both = matmul(jnp.concatenate(high_low(quotient), axis=0), tall)
    both = both[:rows] + both[rows:]
    return both + turned(both)


def turned(x):
    return pltpu.roll(x, x.shape[1] // 2, 1)


def left_half(x):
    return lax.broadcasted_iota(jnp.int32, x.shape, 1) < x.shape[1] // 2


def pack(doubled):
    half = doubled.shape[0] // 2
    lower, upper = doubled[:half], doubled[half:]
    return jnp.where(left_half(lower), lower, upper)


def sum_packed(chips, parts):
    parts = [parts[0], *parts[:0:-1]]
    side = max(chips // 2, 1)
    rows = parts[0].shape[0] // side

    def moved(x, step):
        if step == 0:
            return x
        return jnp.concatenate([x[(c ^ step) * rows : ((c ^ step) + 1) * rows] for c in range(side)], axis=0)

    sums = []
    for first in range(0, chips, side):
        sums.append(sum(moved(parts[step], step - first) for step in range(first, first + side)))
    packed, other = sums[0] + turned(sums[1]), turned(sums[0]) + sums[1]
    left = left_half(packed)
    return jnp.concatenate([jnp.where(left, packed, other), jnp.where(left, other, packed)], axis=0)


def write_parts(refs, part):
    rows = part.shape[0]
    for ref in refs:
        ref[:rows] = part
        if ref.shape[0] > rows:
            ref[rows:] = jnp.zeros((ref.shape[0] - rows, part.shape[1]), part.dtype)


def first_kernel(chips, cores, wide_ref, tall_ref, col_part_ref, *refs):
    payload, (topics_ref, part_ref, *half_refs) = refs[:chips][::-1], refs[-2 - cores :]
    span = wide_ref.shape[1]
    topics = jnp.concatenate([ref[:, span:] for ref in payload], axis=0)
    topics_ref[...] = topics
    weighted = jnp.concatenate([ref[:, :span] for ref in payload], axis=0)
    part = pack(product_of(weighted / recon_of(topics, wide_ref[...]), tall_ref[...]))
    part_ref[: part.shape[0]] = part
    part_ref[part.shape[0] :] = col_part_ref[...]
    words = span // cores
    for half, ref in enumerate(half_refs):
        ref[...] = weighted[:, half * words : (half + 1) * words]


def update_kernel(chips, wide_ref, tall_ref, before_ref, *refs):
    packed = before_ref.shape[0] // 2
    if refs[-1].shape[0] == 8:
        payload, parts = refs[:chips][::-1], refs[chips : 2 * chips]
        topics_ref, *part_refs, total_ref = refs[2 * chips :]
        total_ref[...] = sum(ref[packed:] for ref in parts)
    else:
        total_ref, payload, parts = refs[0], refs[1 : chips + 1][::-1], refs[chips + 1 : 2 * chips + 1]
        topics_ref, *part_refs = refs[2 * chips + 1 :]
    span = wide_ref.shape[1]
    total = sum_packed(chips, [ref[:packed] for ref in parts])
    topics = before_ref[...] / total_ref[:1] * total
    topics_ref[...] = topics
    weighted = jnp.concatenate([ref[:, :span] for ref in payload], axis=0)
    write_parts(part_refs, pack(product_of(weighted / recon_of(topics, wide_ref[...]), tall_ref[...])))


def numerator_of(topics, quotient):
    high, low = high_low(topics.T)
    quotient_high, quotient_low = high_low(quotient)
    return matmul(
        jnp.concatenate([high, low, high], axis=1),
        jnp.concatenate([quotient_high, quotient_high, quotient_low], axis=0),
    )


def topics_kernel(chips, before_ref, total_ref, *refs):
    parts, topics_ref = refs[:chips], refs[-1]
    total = sum_packed(chips, [ref[: before_ref.shape[0] // 2] for ref in parts])
    topics_ref[...] = before_ref[...] / total_ref[:1] * total


def numerator_kernel(wide_ref, onehot_ref, topics_ref, weighted_ref, *refs):
    before, out_ref = refs[:-1], refs[-1]
    topic_count, words = onehot_ref.shape[0], weighted_ref.shape[1]
    quotient = weighted_ref[...] / recon_of(topics_ref[...], wide_ref[:, :words])
    aligned = moved_columns(topics_ref[:, :topic_count], onehot_ref[...])
    numerator = numerator_of(aligned, quotient)
    load = jnp.sum(aligned.T, axis=1, keepdims=True)
    if out_ref.shape[1] > words:
        out_ref[:, :words] = numerator
        out_ref[:, words:] = jnp.broadcast_to(load, (topic_count, out_ref.shape[1] - words))
    else:
        dict_ref, *other = before
        for ref in other:
            numerator = numerator + ref[:, :words]
            load = load + ref[:, words : words + 1]
        out_ref[...] = dict_ref[...] * numerator / load


def base_rows_of(refs, at):
    return jnp.concatenate([ref[:, at] for ref in refs], axis=0)


def refit_kernel(members, chips, half, *refs):
    pieces, payload = refs[:members], refs[members : members + chips]
    *before, wide_ref, tall_ref, part_ref, median_ref = refs[members + chips :]
    sub = pieces[0].shape[1]
    for me in range(members):

        @pl.when(lax.axis_index("pert") == me)
        def _():
            for at in range(members):
                owner = me ^ ((members - at) % members)
                median_ref[:, owner * sub : (owner + 1) * sub] = pieces[at][...]

    words = median_ref.shape[1]
    span = payload[0].shape[1] - part_ref.shape[1]
    wide = jnp.concatenate(high_low(median_ref[...]), axis=0).astype(jnp.bfloat16)
    wide_ref[...] = wide
    tall = jnp.concatenate(high_low(median_ref[...].T), axis=1)
    total = jnp.sum(tall, axis=0, keepdims=True)
    total = jnp.broadcast_to(total + turned(total), (8, total.shape[1]))
    tall = tall.astype(jnp.bfloat16)
    tall_ref[...] = tall
    weighted = base_rows_of(payload, slice(half * words, (half + 1) * words))
    refit = base_rows_of(payload, slice(span, None))
    part = pack(product_of(weighted / recon_of(refit, wide), tall))
    both = jnp.concatenate([part, total], axis=0)
    part_ref[...] = both + before[0][...] if before else both


def refit_again_kernel(chips, cores, base_docs, *refs):
    payload, parts, halves = refs[:chips], refs[chips : 2 * chips], refs[2 * chips : 2 * (chips + cores)]
    scale_ref, *part_refs = refs[2 * (chips + cores) :]
    packed = chips * base_docs // 2
    span = payload[0].shape[1] - scale_ref.shape[1]
    words = span // cores
    median_total = sum(ref[packed : packed + 1] for ref in parts)
    total = sum_packed(chips, [ref[:packed] for ref in parts])
    refit = base_rows_of(payload, slice(span, None)) / median_total * total
    scale_ref[...] = refit[:base_docs] / median_total
    part = None
    for half in range(cores):
        weighted = base_rows_of(payload, slice(half * words, (half + 1) * words))
        wide_ref, tall_ref = halves[2 * half], halves[2 * half + 1]
        new = product_of(weighted / recon_of(refit, wide_ref[...]), tall_ref[...])
        part = new if part is None else part + new
    for step in range(chips):
        part_refs[step][...] = part[step * base_docs : (step + 1) * base_docs]


def finish_kernel(scale_ref, *refs):
    parts, out_ref = refs[:-1], refs[-1]
    out_ref[...] = (scale_ref[...] * sum(ref[...] for ref in parts))[:, : out_ref.shape[1]]


def median_kernel(members, *refs):
    refs[-1][...] = middle([ref[...] for ref in refs[:members]])


def per_device(counts, tile_mask, member_topics, start_dict, align_perm, base_counts, base_topics):
    doc_size = lax.axis_size("doc")
    members = lax.axis_size("pert")
    cores = 2 - doc_size % 2
    chips = doc_size // cores
    at_pert = lax.axis_index("pert")
    at_doc = lax.axis_index("doc")
    at_chip, at_core = at_doc // cores, at_doc % cores
    docs = counts.shape[1]
    base_docs = base_counts.shape[0]
    topic_count = member_topics.shape[2]
    owned = start_dict.shape[1]
    span = cores * owned
    rows = chips * docs
    sub = owned // members

    def over_chips(array, step):
        return lax.ppermute(
            array,
            "doc",
            [
                (c * cores + k, (c ^ step) * cores + (k + step) % cores)
                for c in range(chips)
                for k in range(cores)
            ],
        )

    def over_cores(array):
        return lax.ppermute(array, "doc", [(d, d ^ 1) for d in range(doc_size)])

    def over_pert(array, step):
        return lax.ppermute(array, "pert", [(m, m ^ step) for m in range(members)])

    sent = pl.pallas_call(
        functools.partial(spread_kernel, chips, cores, owned),
        out_shape=[pltpu.VMEM((docs, span + 2 * topic_count), jnp.float32)] * chips,
        in_specs=[pl.BlockSpec(memory_space=pltpu.HBM)] * 3,
        out_specs=[pl.BlockSpec(memory_space=pltpu.VMEM)] * chips,
        scratch_shapes=[
            pltpu.VMEM(tile_mask.shape[1:], jnp.int32),
            pltpu.VMEM(member_topics.shape[1:], jnp.float32),
            pltpu.VMEM((chips, docs, span), jnp.int32),
            pltpu.SemaphoreType.DMA((2,)),
            pltpu.SemaphoreType.DMA((chips, cores)),
        ],
        compiler_params=pltpu.CompilerParams(vmem_limit_bytes=VMEM_BYTES),
        cost_estimate=pl.CostEstimate(flops=0, bytes_accessed=12 * counts.size, transcendentals=0),
    )(*[pltpu.with_memory_space_constraint(x, pltpu.HBM) for x in (tile_mask[0], member_topics[0], counts[0])])
    base_sent = call(
        functools.partial(base_kernel, chips, cores),
        [shape(base_docs, span + 2 * topic_count)] * chips,
        base_counts,
        base_topics,
        moved=8 * base_counts.size,
    )
    got = [over_chips(sent[step], step) for step in range(chips - 1, 0, -1)][::-1]
    payload = [sent[0]] + got
    near = [over_chips(base_sent[step], step) for step in range(1, min(chips, 2))]
    dict_own = start_dict[0].T
    halves = [dict_own] + [over_cores(dict_own)] * (cores - 1)
    wide, tall, col_part, dict_own, onehot = call(
        functools.partial(dictionary_kernel, cores),
        [
            shape(2 * topic_count, span, dtype=jnp.bfloat16),
            shape(span, 2 * topic_count, dtype=jnp.bfloat16),
            shape(8, 2 * topic_count),
            shape(topic_count, owned),
            shape(topic_count, topic_count),
        ],
        align_perm,
        *halves,
        moved=4 * 4 * span * topic_count,
    )

    update_flops = 2 * 2 * 4 * rows * topic_count * span
    topics, part, *weighted = call(
        functools.partial(first_kernel, chips, cores),
        [shape(rows, 2 * topic_count), shape(rows // 2 + 8, 2 * topic_count)]
        + [shape(rows, owned)] * cores,
        wide,
        tall,
        col_part,
        *payload[::-1],
        *near,
        unread=len(near),
        flops=update_flops,
        moved=4 * span * (rows + 2 * topic_count),
    )
    parts = [part] + [over_chips(part, step) for step in range(chips - 1, 0, -1)]
    crossed = [over_cores(weighted[1])] if cores > 1 else []
    totals = []
    for update in range(1, UPDATES):
        topics, *outs = call(
            functools.partial(update_kernel, chips),
            [shape(rows, 2 * topic_count)]
            + [shape(rows // 2 + 8 * (step - 1), 2 * topic_count) for step in range(1, chips)]
            + ([] if totals else [shape(8, 2 * topic_count)]),
            wide,
            tall,
            topics,
            *totals,
            *payload[::-1],
            *parts,
            flops=update_flops,
            moved=4 * span * (rows + 2 * topic_count),
        )
        totals = totals or outs[chips - 1 :]
        parts = [outs[0]] + [over_chips(outs[step - 1], step) for step in range(chips - 1, 0, -1)]
    (col_total,) = totals

    topics = call(
        functools.partial(topics_kernel, chips),
        shape(rows, 2 * topic_count),
        topics,
        col_total,
        *parts,
        *crossed,
        unread=len(crossed),
    )
    other = []
    if cores > 1:
        other_topics = over_cores(topics)
        other = [
            call(
                numerator_kernel,
                shape(topic_count, owned + 128),
                wide,
                onehot,
                topics,
                weighted[0],
                flops=update_flops // 2,
                moved=2 * span * (rows + 2 * topic_count),
            )
        ]
        topics, weighted = other_topics, crossed
    aligned = call(
        numerator_kernel,
        shape(topic_count, owned),
        wide,
        onehot,
        topics,
        weighted[0],
        dict_own,
        *other,
        flops=update_flops // 2,
        moved=2 * span * (rows + 2 * topic_count),
    )

    def words_of(array, member):
        return lax.dynamic_slice_in_dim(array, member * sub, sub, 1)

    aligned, base_sent = lax.optimization_barrier((aligned, base_sent))
    base_got = [over_chips(base_sent[step], step) for step in range(2, chips)]
    late = len(base_got) // 2
    base_got = base_got[::-1]
    median = call(
        functools.partial(median_kernel, members),
        pltpu.VMEM((topic_count, sub), jnp.float32),
        words_of(aligned, at_pert),
        *[over_pert(words_of(aligned, at_pert ^ step), step) for step in range(members - 1, 0, -1)],
        *base_got[late:],
        unread=len(base_got) - late,
    )
    pieces = [median] + [over_pert(median, step) for step in range(members - 1, 0, -1)]
    pieces[1], *base_got[:late] = lax.optimization_barrier((pieces[1], *base_got[:late]))
    median_halves = [pieces] + [[over_cores(piece) for piece in pieces]] * (cores - 1)
    base_all = [base_sent[0]] + near + base_got[::-1]

    base_rows = chips * base_docs
    refit_flops = 2 * 2 * 4 * base_rows * topic_count * owned
    forms, before = [], []
    for half in range(cores):
        wide, tall, part = call(
            functools.partial(refit_kernel, members, chips, half),
            [
                shape(2 * topic_count, owned, dtype=jnp.bfloat16),
                shape(owned, 2 * topic_count, dtype=jnp.bfloat16),
                shape(base_rows // 2 + 8, 2 * topic_count),
            ],
            *median_halves[half],
            *base_all,
            *before,
            flops=refit_flops,
            moved=16 * owned * topic_count,
            scratch=[pltpu.VMEM((topic_count, owned), jnp.float32)],
        )
        forms += [wide, tall]
        before = [part]
    scale, *parts = call(
        functools.partial(refit_again_kernel, chips, cores, base_docs),
        [shape(base_docs, 2 * topic_count)] * (chips + 1),
        *base_all,
        part,
        *[over_chips(part, step) for step in range(chips - 1, 0, -1)],
        *forms,
        flops=2 * refit_flops,
        moved=16 * owned * topic_count,
    )
    refit = call(
        finish_kernel,
        shape(base_docs, topic_count),
        scale,
        parts[0],
        *[over_chips(parts[step], step) for step in range(chips - 1, 0, -1)],
    )
    return (median.T[None, None], refit)


def solution(mesh):
    return jax.shard_map(
        per_device,
        mesh=mesh,
        in_specs=(
            P("pert", "doc", None),
            P("pert", "doc", None),
            P("pert", "doc", None),
            P("pert", "doc", None),
            P("pert", None),
            P(("pert", "doc"), None),
            P(("pert", "doc"), None),
        ),
        out_specs=(P("doc", "pert", None, None), P(("pert", "doc"), None)),
        check_vma=False,
    )
```

```python
import functools

import jax
import jax.numpy as jnp
from jax import lax
from jax.experimental import pallas as pl
from jax.experimental.pallas import tpu as pltpu
from jax.sharding import PartitionSpec as P

UPDATES = 3
REFITS = 2

EXACT = lax.Precision.HIGHEST
ROUGH = lax.Precision.HIGH
VMEM_BYTES = 14 * 1024 * 1024
SPREAD_BYTES = 60 * 1024 * 1024


def dot(left, right, dims, precision=ROUGH):
    return lax.dot_general(left, right, (dims, ((), ())), precision=precision)


def middle(pieces):
    pieces = list(pieces)
    count = len(pieces)
    for turn in range(count):
        for low in range(turn % 2, count - 1, 2):
            pieces[low], pieces[low + 1] = (
                jnp.minimum(pieces[low], pieces[low + 1]),
                jnp.maximum(pieces[low], pieces[low + 1]),
            )
    return 0.5 * (pieces[count // 2 - 1] + pieces[count // 2])


def call(kernel, outs, *args, flops=0, moved=0, unread=0, scratch=()):
    read = len(args) - unread
    return pl.pallas_call(
        kernel,
        out_shape=outs,
        in_specs=[pl.BlockSpec(memory_space=pltpu.VMEM)] * read
        + [pl.BlockSpec(memory_space=pl.ANY)] * unread,
        scratch_shapes=scratch,
        compiler_params=pltpu.CompilerParams(vmem_limit_bytes=VMEM_BYTES),
        cost_estimate=pl.CostEstimate(flops=flops, bytes_accessed=moved, transcendentals=0),
    )(*args)


def shape(*dims, dtype=jnp.float32):
    return jax.ShapeDtypeStruct(dims, dtype)


def high_low(x):
    high = x.astype(jnp.bfloat16).astype(jnp.float32)
    return high, x - high


def matmul(left, right):
    return jnp.dot(
        left.astype(jnp.bfloat16), right.astype(jnp.bfloat16), preferred_element_type=jnp.float32
    )


def blocks_of(chips, cores, step):
    at_doc = lax.axis_index("doc")
    at_chip, at_core = at_doc // cores, at_doc % cores
    return [(at_chip ^ step) * cores + (at_core ^ ((step + half) % cores)) for half in range(cores)]


def spread_kernel(chips, cores, own_words, mask_hbm, topics_hbm, perm_hbm, counts_hbm, *refs):
    out_refs, (mask_ref, topics_ref, perm_ref, counts_ref, small_sems, in_sems) = (
        refs[:chips],
        refs[chips:],
    )
    small = [
        pltpu.make_async_copy(mask_hbm, mask_ref, small_sems.at[0]),
        pltpu.make_async_copy(topics_hbm, topics_ref, small_sems.at[1]),
        pltpu.make_async_copy(perm_hbm, perm_ref, small_sems.at[2]),
    ]
    for copy in small:
        copy.start()
    steps = list(range(chips - 1, -1, -1))
    arriving = {}
    for step in steps:
        for half, block in enumerate(blocks_of(chips, cores, step)):
            at = slice(half * own_words, (half + 1) * own_words)
            arriving[step, half] = pltpu.make_async_copy(
                counts_hbm.at[:, pl.ds(pl.multiple_of(block * own_words, 128), own_words)],
                counts_ref.at[step, :, at],
                in_sems.at[step, half],
            )
            arriving[step, half].start()
    docs, tiles = mask_ref.shape
    width = chips * cores * own_words // tiles
    own_tiles = own_words // width
    tile_ids = lax.broadcasted_iota(jnp.int32, (docs, tiles), 1)
    doc_ids = lax.axis_index("doc") * docs + lax.broadcasted_iota(jnp.int32, (docs, tiles), 0)
    forced = (tile_ids == doc_ids % tiles).astype(jnp.int32)
    for copy in small:
        copy.wait()
    occupied = jnp.maximum(mask_ref[...], forced).astype(jnp.float32)
    topic_count = topics_ref.shape[1]
    onehot = lax.broadcasted_iota(jnp.int32, (topic_count, 2 * topic_count), 0) == jnp.concatenate(
        [perm_ref[...]] * 2, axis=1
    )
    topics = moved_columns(topics_ref[...], onehot.astype(jnp.float32))
    for step in steps:
        for half, block in enumerate(blocks_of(chips, cores, step)):
            near = pltpu.roll(occupied, lax.rem(tiles - block * own_tiles, tiles), 1)
            arriving[step, half].wait()
            for tile in range(own_tiles):
                at = slice(half * own_words + tile * width, half * own_words + (tile + 1) * width)
                picked = counts_ref[step, :, at].astype(jnp.float32)
                out_refs[step][:, at] = picked * near[:, tile : tile + 1]
        out_refs[step][:, cores * own_words :] = topics


def base_kernel(chips, cores, counts_ref, topics_ref, *out_refs):
    span = out_refs[0].shape[1] - 2 * topics_ref.shape[1]
    own_words = span // cores
    for step in range(chips):
        for half, block in enumerate(blocks_of(chips, cores, step)):
            at = slice(half * own_words, (half + 1) * own_words)
            first = pl.multiple_of(block * own_words, 128)
            out_refs[step][:, at] = counts_ref[:, pl.ds(first, own_words)].astype(jnp.float32)
        out_refs[step][:, span:] = jnp.concatenate([topics_ref[...]] * 2, axis=1)


def moved_columns(x, onehot):
    rows = x.shape[0]
    high, rest = high_low(x)
    mid, low = high_low(rest)
    moved = matmul(jnp.concatenate([high, mid, low], axis=0), onehot)
    return moved[:rows] + moved[rows : 2 * rows] + moved[2 * rows :]


def dictionary_kernel(half_count, perm_ref, *refs):
    topics, words = refs[0].shape
    wide_ref, tall_ref, total_ref, own_ref = refs[half_count:]
    turned_onehot = (
        (lax.broadcasted_iota(jnp.int32, (topics, topics), 0) == perm_ref[...]).astype(jnp.float32).T
    )
    total = jnp.zeros((1, 2 * topics), jnp.float32)
    for half in range(half_count):
        at = slice(half * words, (half + 1) * words)
        high, rest = high_low(refs[half][...])
        mid, low = high_low(rest)
        aligned = matmul(
            jnp.concatenate([turned_onehot] * 3, axis=1), jnp.concatenate([high, mid, low], axis=0)
        )
        if half == 0:
            own_ref[...] = aligned
        wide = jnp.concatenate(high_low(aligned), axis=0)
        wide_ref[:, at] = wide.astype(jnp.bfloat16)
        tall = wide.T
        total += jnp.sum(tall, axis=0, keepdims=True)
        tall_ref[at, :] = tall.astype(jnp.bfloat16)
    total_ref[...] = jnp.broadcast_to(total + turned(total), total_ref.shape)


def recon_of(doubled, wide):
    rows = doubled.shape[0]
    both = matmul(jnp.concatenate(high_low(doubled), axis=0), wide)
    return both[:rows] + both[rows:]


def product_of(quotient, tall, ones=0):
    rows = quotient.shape[0]
    left = [*high_low(quotient)] + [jnp.ones((ones, quotient.shape[1]), jnp.float32)] * (ones > 0)
    both = matmul(jnp.concatenate(left, axis=0), tall)
    both = [both[:rows] + both[rows : 2 * rows], both[2 * rows :]]
    both = jnp.concatenate(both, axis=0) if ones else both[0]
    return both + turned(both)


def turned(x):
    return pltpu.roll(x, x.shape[1] // 2, 1)


def left_half(x):
    return lax.broadcasted_iota(jnp.int32, x.shape, 1) < x.shape[1] // 2


def pack(doubled):
    half = doubled.shape[0] // 2
    lower, upper = doubled[:half], doubled[half:]
    return jnp.where(left_half(lower), lower, upper)


def sum_packed(chips, parts):
    parts = [parts[0], *parts[:0:-1]]
    side = max(chips // 2, 1)
    rows = parts[0].shape[0] // side

    def moved(x, step):
        if step == 0:
            return x
        return jnp.concatenate([x[(c ^ step) * rows : ((c ^ step) + 1) * rows] for c in range(side)], axis=0)

    sums = []
    for first in range(0, chips, side):
        sums.append(sum(moved(parts[step], step - first) for step in range(first, first + side)))
    packed, other = sums[0] + turned(sums[1]), turned(sums[0]) + sums[1]
    left = left_half(packed)
    return jnp.concatenate([jnp.where(left, packed, other), jnp.where(left, other, packed)], axis=0)


def write_parts(refs, part):
    rows = part.shape[0]
    for ref in refs:
        ref[:rows] = part
        if ref.shape[0] > rows:
            ref[rows:] = jnp.zeros((ref.shape[0] - rows, part.shape[1]), part.dtype)


def first_kernel(chips, cores, order, wide_ref, tall_ref, col_part_ref, *refs):
    payload = [refs[order.index(step)] for step in range(chips)]
    topics_ref, part_ref, *half_refs = refs[-2 - cores :]
    span = wide_ref.shape[1]
    topics = jnp.concatenate([ref[:, span:] for ref in payload], axis=0)
    topics_ref[...] = topics
    weighted = jnp.concatenate([ref[:, :span] for ref in payload], axis=0)
    part = pack(product_of(weighted / recon_of(topics, wide_ref[...]), tall_ref[...]))
    part_ref[: part.shape[0]] = part
    part_ref[part.shape[0] :] = col_part_ref[...]
    words = span // cores
    for half, ref in enumerate(half_refs):
        ref[...] = weighted[:, half * words : (half + 1) * words]


def update_kernel(chips, wide_ref, tall_ref, before_ref, *refs):
    packed = before_ref.shape[0] // 2
    if refs[-1].shape[0] == 8:
        payload, parts = refs[:chips][::-1], refs[chips : 2 * chips]
        topics_ref, *part_refs, total_ref = refs[2 * chips :]
        total_ref[...] = sum(ref[packed:] for ref in parts)
    else:
        total_ref, payload, parts = refs[0], refs[1 : chips + 1][::-1], refs[chips + 1 : 2 * chips + 1]
        topics_ref, *part_refs = refs[2 * chips + 1 :]
    span = wide_ref.shape[1]
    total = sum_packed(chips, [ref[:packed] for ref in parts])
    topics = before_ref[...] / total_ref[:1] * total
    topics_ref[...] = topics
    weighted = jnp.concatenate([ref[:, :span] for ref in payload], axis=0)
    write_parts(part_refs, pack(product_of(weighted / recon_of(topics, wide_ref[...]), tall_ref[...])))


def numerator_of(topics, quotient):
    high, low = high_low(topics.T[: topics.shape[1] // 2])
    quotient_high, quotient_low = high_low(quotient)
    return matmul(
        jnp.concatenate([high, low, high], axis=1),
        jnp.concatenate([quotient_high, quotient_high, quotient_low], axis=0),
    )


def topics_kernel(chips, before_ref, total_ref, *refs):
    parts, topics_ref = refs[:chips], refs[-1]
    total = sum_packed(chips, [ref[: before_ref.shape[0] // 2] for ref in parts])
    topics_ref[...] = before_ref[...] / total_ref[:1] * total


def numerator_kernel(wide_ref, topics_ref, weighted_ref, *refs):
    before, out_ref = refs[:-1], refs[-1]
    words = weighted_ref.shape[1]
    topics = topics_ref[...]
    load = jnp.sum(topics.T[: topics.shape[1] // 2], axis=1, keepdims=True)
    numerator = numerator_of(topics, weighted_ref[...] / recon_of(topics, wide_ref[:, :words]))
    if out_ref.shape[1] > words:
        out_ref[:, :words] = numerator
        out_ref[:, words:] = jnp.broadcast_to(load, (load.shape[0], out_ref.shape[1] - words))
    else:
        dict_ref, *other = before
        for ref in other:
            numerator = numerator + ref[:, :words]
            load = load + ref[:, words : words + 1]
        out_ref[...] = dict_ref[...] / load * numerator


def base_rows_of(refs, at):
    return jnp.concatenate([ref[:, at] for ref in refs], axis=0)


def refit_kernel(members, chips, half, *refs):
    pieces, payload = refs[:members], refs[members : members + chips]
    *before, wide_ref, tall_ref, part_ref, median_ref = refs[members + chips :]
    sub = pieces[0].shape[1]
    for me in range(members):

        @pl.when(lax.axis_index("pert") == me)
        def _():
            for at in range(members):
                owner = me ^ ((members - at) % members)
                median_ref[:, owner * sub : (owner + 1) * sub] = pieces[at][...]

    words = median_ref.shape[1]
    span = payload[0].shape[1] - part_ref.shape[1]
    wide = jnp.concatenate(high_low(median_ref[...]), axis=0)
    tall = wide.T.astype(jnp.bfloat16)
    wide = wide.astype(jnp.bfloat16)
    wide_ref[...] = wide
    tall_ref[...] = tall
    weighted = base_rows_of(payload, slice(half * words, (half + 1) * words))
    refit = base_rows_of(payload, slice(span, None))
    both = product_of(weighted / recon_of(refit, wide), tall, ones=8)
    both = jnp.concatenate([pack(both[:-8]), both[-8:]], axis=0)
    part_ref[...] = both + before[0][...] if before else both


def refit_again_kernel(chips, cores, base_docs, *refs):
    payload, parts, halves = refs[:chips], refs[chips : 2 * chips], refs[2 * chips : 2 * (chips + cores)]
    scale_ref, *part_refs = refs[2 * (chips + cores) :]
    packed = chips * base_docs // 2
    span = payload[0].shape[1] - scale_ref.shape[1]
    words = span // cores
    median_total = sum(ref[packed : packed + 1] for ref in parts)
    total = sum_packed(chips, [ref[:packed] for ref in parts])
    refit = base_rows_of(payload, slice(span, None)) / median_total * total
    scale_ref[...] = refit[:base_docs] / median_total
    part = None
    for half in range(cores):
        weighted = base_rows_of(payload, slice(half * words, (half + 1) * words))
        wide_ref, tall_ref = halves[2 * half], halves[2 * half + 1]
        new = product_of(weighted / recon_of(refit, wide_ref[...]), tall_ref[...])
        part = new if part is None else part + new
    for step in range(chips):
        part_refs[step][...] = part[step * base_docs : (step + 1) * base_docs]


def finish_kernel(scale_ref, *refs):
    parts, out_ref = refs[:-1], refs[-1]
    out_ref[...] = (scale_ref[...] * sum(ref[...] for ref in parts))[:, : out_ref.shape[1]]


def median_kernel(members, *refs):
    refs[-1][...] = middle([ref[...] for ref in refs[:members]])


def per_device(counts, tile_mask, member_topics, start_dict, align_perm, base_counts, base_topics):
    doc_size = lax.axis_size("doc")
    members = lax.axis_size("pert")
    cores = 2 - doc_size % 2
    chips = doc_size // cores
    at_pert = lax.axis_index("pert")
    at_doc = lax.axis_index("doc")
    at_chip, at_core = at_doc // cores, at_doc % cores
    docs = counts.shape[1]
    base_docs = base_counts.shape[0]
    topic_count = member_topics.shape[2]
    owned = start_dict.shape[1]
    span = cores * owned
    rows = chips * docs
    sub = owned // members

    def over_chips(array, step):
        return lax.ppermute(
            array,
            "doc",
            [
                (c * cores + k, (c ^ step) * cores + (k + step) % cores)
                for c in range(chips)
                for k in range(cores)
            ],
        )

    def over_cores(array):
        return lax.ppermute(array, "doc", [(d, d ^ 1) for d in range(doc_size)])

    def over_pert(array, step):
        return lax.ppermute(array, "pert", [(m, m ^ step) for m in range(members)])

    sent = pl.pallas_call(
        functools.partial(spread_kernel, chips, cores, owned),
        out_shape=[pltpu.VMEM((docs, span + 2 * topic_count), jnp.float32)] * chips,
        in_specs=[pl.BlockSpec(memory_space=pltpu.HBM)] * 4,
        out_specs=[pl.BlockSpec(memory_space=pltpu.VMEM)] * chips,
        scratch_shapes=[
            pltpu.VMEM(tile_mask.shape[1:], jnp.int32),
            pltpu.VMEM(member_topics.shape[1:], jnp.float32),
            pltpu.VMEM(align_perm.shape, jnp.int32),
            pltpu.VMEM((chips, docs, span), jnp.int32),
            pltpu.SemaphoreType.DMA((3,)),
            pltpu.SemaphoreType.DMA((chips, cores)),
        ],
        compiler_params=pltpu.CompilerParams(vmem_limit_bytes=VMEM_BYTES),
        cost_estimate=pl.CostEstimate(flops=0, bytes_accessed=12 * counts.size, transcendentals=0),
    )(*[pltpu.with_memory_space_constraint(x, pltpu.HBM) for x in (tile_mask[0], member_topics[0], align_perm, counts[0])])
    base_sent = call(
        functools.partial(base_kernel, chips, cores),
        [shape(base_docs, span + 2 * topic_count)] * chips,
        base_counts,
        base_topics,
        moved=8 * base_counts.size,
    )
    got = [over_chips(sent[step], step) for step in range(chips - 1, 0, -1)][::-1]
    payload = [sent[0]] + got
    near = [over_chips(base_sent[step], step) for step in range(1, min(chips, 2))]
    dict_own = start_dict[0].T
    halves = [dict_own] + [over_cores(dict_own)] * (cores - 1)
    wide, tall, col_part, dict_own = call(
        functools.partial(dictionary_kernel, cores),
        [
            shape(2 * topic_count, span, dtype=jnp.bfloat16),
            shape(span, 2 * topic_count, dtype=jnp.bfloat16),
            shape(8, 2 * topic_count),
            shape(topic_count, owned),
        ],
        align_perm,
        *halves,
        moved=4 * 4 * span * topic_count,
    )

    update_flops = 2 * 2 * 4 * rows * topic_count * span
    count_order = [chips // 2] + [s for s in range(1, chips) if s != chips // 2] + [0]
    topics, part, *weighted = call(
        functools.partial(first_kernel, chips, cores, count_order),
        [shape(rows, 2 * topic_count), shape(rows // 2 + 8, 2 * topic_count)]
        + [shape(rows, owned)] * cores,
        wide,
        tall,
        col_part,
        *[payload[step] for step in count_order],
        *near,
        unread=len(near),
        flops=update_flops,
        moved=4 * span * (rows + 2 * topic_count),
    )
    parts = [part] + [over_chips(part, step) for step in range(chips - 1, 0, -1)]
    crossed = [over_cores(weighted[1])] if cores > 1 else []
    totals = []
    for update in range(1, UPDATES):
        topics, *outs = call(
            functools.partial(update_kernel, chips),
            [shape(rows, 2 * topic_count)]
            + [shape(rows // 2 + 8 * (step - 1), 2 * topic_count) for step in range(1, chips)]
            + ([] if totals else [shape(8, 2 * topic_count)]),
            wide,
            tall,
            topics,
            *totals,
            *payload[::-1],
            *parts,
            flops=update_flops,
            moved=4 * span * (rows + 2 * topic_count),
        )
        totals = totals or outs[chips - 1 :]
        parts = [outs[0]] + [over_chips(outs[step - 1], step) for step in range(chips - 1, 0, -1)]
    (col_total,) = totals

    topics = call(
        functools.partial(topics_kernel, chips),
        shape(rows, 2 * topic_count),
        topics,
        col_total,
        *parts,
        *crossed,
        unread=len(crossed),
    )
    other = []
    if cores > 1:
        other_topics = over_cores(topics)
        other = [
            call(
                numerator_kernel,
                shape(topic_count, owned + 128),
                wide,
                topics,
                weighted[0],
                flops=update_flops // 2,
                moved=2 * span * (rows + 2 * topic_count),
            )
        ]
        topics, weighted = other_topics, crossed
    aligned = call(
        numerator_kernel,
        shape(topic_count, owned),
        wide,
        topics,
        weighted[0],
        dict_own,
        *other,
        flops=update_flops // 2,
        moved=2 * span * (rows + 2 * topic_count),
    )

    def words_of(array, member):
        return lax.dynamic_slice_in_dim(array, member * sub, sub, 1)

    aligned, base_sent = lax.optimization_barrier((aligned, base_sent))
    base_got = [over_chips(base_sent[step], step) for step in range(2, chips)]
    late = len(base_got) // 2
    base_got = base_got[::-1]
    median = call(
        functools.partial(median_kernel, members),
        pltpu.VMEM((topic_count, sub), jnp.float32),
        words_of(aligned, at_pert),
        *[over_pert(words_of(aligned, at_pert ^ step), step) for step in range(members - 1, 0, -1)],
        *base_got[late:],
        unread=len(base_got) - late,
    )
    pieces = [median] + [over_pert(median, step) for step in range(members - 1, 0, -1)]
    pieces[1], *base_got[:late] = lax.optimization_barrier((pieces[1], *base_got[:late]))
    median_halves = [pieces] + [[over_cores(piece) for piece in pieces]] * (cores - 1)
    base_all = [base_sent[0]] + near + base_got[::-1]

    base_rows = chips * base_docs
    refit_flops = 2 * 2 * 4 * base_rows * topic_count * owned
    forms, before = [], []
    for half in range(cores):
        wide, tall, part = call(
            functools.partial(refit_kernel, members, chips, half),
            [
                shape(2 * topic_count, owned, dtype=jnp.bfloat16),
                shape(owned, 2 * topic_count, dtype=jnp.bfloat16),
                shape(base_rows // 2 + 8, 2 * topic_count),
            ],
            *median_halves[half],
            *base_all,
            *before,
            flops=refit_flops,
            moved=16 * owned * topic_count,
            scratch=[pltpu.VMEM((topic_count, owned), jnp.float32)],
        )
        forms += [wide, tall]
        before = [part]
    scale, *parts = call(
        functools.partial(refit_again_kernel, chips, cores, base_docs),
        [shape(base_docs, 2 * topic_count)] * (chips + 1),
        *base_all,
        part,
        *[over_chips(part, step) for step in range(chips - 1, 0, -1)],
        *forms,
        flops=2 * refit_flops,
        moved=16 * owned * topic_count,
    )
    refit = call(
        finish_kernel,
        shape(base_docs, topic_count),
        scale,
        parts[0],
        *[over_chips(parts[step], step) for step in range(chips - 1, 0, -1)],
    )
    return (median.T[None, None], refit)


def solution(mesh):
    return jax.shard_map(
        per_device,
        mesh=mesh,
        in_specs=(
            P("pert", "doc", None),
            P("pert", "doc", None),
            P("pert", "doc", None),
            P("pert", "doc", None),
            P("pert", None),
            P(("pert", "doc"), None),
            P(("pert", "doc"), None),
        ),
        out_specs=(P("doc", "pert", None, None), P(("pert", "doc"), None)),
        check_vma=False,
    )
```

```python
import functools

import jax
import jax.numpy as jnp
from jax import lax
from jax.experimental import pallas as pl
from jax.experimental.pallas import tpu as pltpu
from jax.sharding import PartitionSpec as P

UPDATES = 3
REFITS = 2

EXACT = lax.Precision.HIGHEST
ROUGH = lax.Precision.HIGH
VMEM_BYTES = 14 * 1024 * 1024
SPREAD_BYTES = 60 * 1024 * 1024


def dot(left, right, dims, precision=ROUGH):
    return lax.dot_general(left, right, (dims, ((), ())), precision=precision)


def middle(pieces):
    pieces = list(pieces)
    count = len(pieces)
    for turn in range(count):
        for low in range(turn % 2, count - 1, 2):
            pieces[low], pieces[low + 1] = (
                jnp.minimum(pieces[low], pieces[low + 1]),
                jnp.maximum(pieces[low], pieces[low + 1]),
            )
    return 0.5 * (pieces[count // 2 - 1] + pieces[count // 2])


def call(kernel, outs, *args, flops=0, moved=0, unread=0, scratch=()):
    read = len(args) - unread
    return pl.pallas_call(
        kernel,
        out_shape=outs,
        in_specs=[pl.BlockSpec(memory_space=pltpu.VMEM)] * read
        + [pl.BlockSpec(memory_space=pl.ANY)] * unread,
        scratch_shapes=scratch,
        compiler_params=pltpu.CompilerParams(vmem_limit_bytes=VMEM_BYTES),
        cost_estimate=pl.CostEstimate(flops=flops, bytes_accessed=moved, transcendentals=0),
    )(*args)


def shape(*dims, dtype=jnp.float32):
    return jax.ShapeDtypeStruct(dims, dtype)


def high_low(x):
    high = x.astype(jnp.bfloat16).astype(jnp.float32)
    return high, x - high


def matmul(left, right):
    return jnp.dot(
        left.astype(jnp.bfloat16), right.astype(jnp.bfloat16), preferred_element_type=jnp.float32
    )


def blocks_of(chips, cores, step):
    at_doc = lax.axis_index("doc")
    at_chip, at_core = at_doc // cores, at_doc % cores
    return [(at_chip ^ step) * cores + (at_core ^ ((step + half) % cores)) for half in range(cores)]


def spread_kernel(chips, cores, own_words, mask_hbm, topics_hbm, perm_hbm, counts_hbm, *refs):
    out_refs, (mask_ref, topics_ref, perm_ref, counts_ref, small_sems, in_sems) = (
        refs[:chips],
        refs[chips:],
    )
    small = [
        pltpu.make_async_copy(mask_hbm, mask_ref, small_sems.at[0]),
        pltpu.make_async_copy(topics_hbm, topics_ref, small_sems.at[1]),
        pltpu.make_async_copy(perm_hbm, perm_ref, small_sems.at[2]),
    ]
    for copy in small:
        copy.start()
    steps = list(range(chips - 1, -1, -1))
    arriving = {}
    for step in steps:
        for half, block in enumerate(blocks_of(chips, cores, step)):
            at = slice(half * own_words, (half + 1) * own_words)
            arriving[step, half] = pltpu.make_async_copy(
                counts_hbm.at[:, pl.ds(pl.multiple_of(block * own_words, 128), own_words)],
                counts_ref.at[step, :, at],
                in_sems.at[step, half],
            )
            arriving[step, half].start()
    docs, tiles = mask_ref.shape
    width = chips * cores * own_words // tiles
    own_tiles = own_words // width
    tile_ids = lax.broadcasted_iota(jnp.int32, (docs, tiles), 1)
    doc_ids = lax.axis_index("doc") * docs + lax.broadcasted_iota(jnp.int32, (docs, tiles), 0)
    forced = (tile_ids == doc_ids % tiles).astype(jnp.int32)
    for copy in small:
        copy.wait()
    occupied = jnp.maximum(mask_ref[...], forced).astype(jnp.float32)
    topic_count = topics_ref.shape[1]
    onehot = lax.broadcasted_iota(jnp.int32, (topic_count, 2 * topic_count), 0) == jnp.concatenate(
        [perm_ref[...]] * 2, axis=1
    )
    topics = moved_columns(topics_ref[...], onehot.astype(jnp.float32))
    for step in steps:
        for half, block in enumerate(blocks_of(chips, cores, step)):
            near = pltpu.roll(occupied, lax.rem(tiles - block * own_tiles, tiles), 1)
            arriving[step, half].wait()
            for tile in range(own_tiles):
                at = slice(half * own_words + tile * width, half * own_words + (tile + 1) * width)
                picked = counts_ref[step, :, at].astype(jnp.float32)
                out_refs[step][:, at] = picked * near[:, tile : tile + 1]
        out_refs[step][:, cores * own_words :] = topics


def base_kernel(chips, cores, counts_ref, topics_ref, *out_refs):
    span = out_refs[0].shape[1] - 2 * topics_ref.shape[1]
    own_words = span // cores
    for step in range(chips):
        for half, block in enumerate(blocks_of(chips, cores, step)):
            at = slice(half * own_words, (half + 1) * own_words)
            first = pl.multiple_of(block * own_words, 128)
            out_refs[step][:, at] = counts_ref[:, pl.ds(first, own_words)].astype(jnp.float32)
        out_refs[step][:, span:] = jnp.concatenate([topics_ref[...]] * 2, axis=1)


def moved_columns(x, onehot):
    rows = x.shape[0]
    high, rest = high_low(x)
    mid, low = high_low(rest)
    moved = matmul(jnp.concatenate([high, mid, low], axis=0), onehot)
    return moved[:rows] + moved[rows : 2 * rows] + moved[2 * rows :]


def dictionary_kernel(half_count, perm_ref, *refs):
    topics, words = refs[0].shape
    wide_ref, tall_ref, total_ref, own_ref = refs[half_count:]
    turned_onehot = (
        (lax.broadcasted_iota(jnp.int32, (topics, topics), 0) == perm_ref[...]).astype(jnp.float32).T
    )
    total = jnp.zeros((1, 2 * topics), jnp.float32)
    for half in range(half_count):
        at = slice(half * words, (half + 1) * words)
        high, rest = high_low(refs[half][...])
        mid, low = high_low(rest)
        aligned = matmul(
            jnp.concatenate([turned_onehot] * 3, axis=1), jnp.concatenate([high, mid, low], axis=0)
        )
        if half == 0:
            own_ref[...] = aligned
        wide = jnp.concatenate(high_low(aligned), axis=0)
        wide_ref[:, at] = wide.astype(jnp.bfloat16)
        tall = wide.T
        total += jnp.sum(tall, axis=0, keepdims=True)
        tall_ref[at, :] = tall.astype(jnp.bfloat16)
    total_ref[...] = jnp.broadcast_to(total + turned(total), total_ref.shape)


def recon_of(doubled, wide):
    rows = doubled.shape[0]
    both = matmul(jnp.concatenate(high_low(doubled), axis=0), wide)
    return both[:rows] + both[rows:]


def product_of(quotient, tall, ones=0):
    rows = quotient.shape[0]
    left = [*high_low(quotient)] + [jnp.ones((ones, quotient.shape[1]), jnp.float32)] * (ones > 0)
    both = matmul(jnp.concatenate(left, axis=0), tall)
    both = [both[:rows] + both[rows : 2 * rows], both[2 * rows :]]
    both = jnp.concatenate(both, axis=0) if ones else both[0]
    return both + turned(both)


def turned(x):
    return pltpu.roll(x, x.shape[1] // 2, 1)


def left_half(x):
    return lax.broadcasted_iota(jnp.int32, x.shape, 1) < x.shape[1] // 2


def pack(doubled):
    half = doubled.shape[0] // 2
    lower, upper = doubled[:half], doubled[half:]
    return jnp.where(left_half(lower), lower, upper)


def sum_packed(chips, parts):
    parts = [parts[0], *parts[:0:-1]]
    side = max(chips // 2, 1)
    rows = parts[0].shape[0] // side

    def moved(x, step):
        if step == 0:
            return x
        return jnp.concatenate([x[(c ^ step) * rows : ((c ^ step) + 1) * rows] for c in range(side)], axis=0)

    sums = []
    for first in range(0, chips, side):
        sums.append(sum(moved(parts[step], step - first) for step in range(first, first + side)))
    packed, other = sums[0] + turned(sums[1]), turned(sums[0]) + sums[1]
    left = left_half(packed)
    return jnp.concatenate([jnp.where(left, packed, other), jnp.where(left, other, packed)], axis=0)


def write_parts(refs, part):
    rows = part.shape[0]
    for ref in refs:
        ref[:rows] = part
        if ref.shape[0] > rows:
            ref[rows:] = jnp.zeros((ref.shape[0] - rows, part.shape[1]), part.dtype)


def first_kernel(chips, cores, order, wide_ref, tall_ref, col_part_ref, *refs):
    payload = [refs[order.index(step)] for step in range(chips)]
    topics_ref, part_ref, *half_refs = refs[-2 - cores :]
    span = wide_ref.shape[1]
    topics = jnp.concatenate([ref[:, span:] for ref in payload], axis=0)
    topics_ref[...] = topics
    weighted = jnp.concatenate([ref[:, :span] for ref in payload], axis=0)
    part = pack(product_of(weighted / recon_of(topics, wide_ref[...]), tall_ref[...]))
    part_ref[: part.shape[0]] = part
    part_ref[part.shape[0] :] = col_part_ref[...]
    words = span // cores
    for half, ref in enumerate(half_refs):
        ref[...] = weighted[:, half * words : (half + 1) * words]


def update_kernel(chips, wide_ref, tall_ref, before_ref, *refs):
    packed = before_ref.shape[0] // 2
    if refs[-1].shape[0] == 8:
        payload, parts = refs[:chips][::-1], refs[chips : 2 * chips]
        topics_ref, *part_refs, total_ref = refs[2 * chips :]
        total_ref[...] = sum(ref[packed:] for ref in parts)
    else:
        total_ref, payload, parts = refs[0], refs[1 : chips + 1][::-1], refs[chips + 1 : 2 * chips + 1]
        topics_ref, *part_refs = refs[2 * chips + 1 :]
    span = wide_ref.shape[1]
    total = sum_packed(chips, [ref[:packed] for ref in parts])
    topics = before_ref[...] / total_ref[:1] * total
    topics_ref[...] = topics
    weighted = jnp.concatenate([ref[:, :span] for ref in payload], axis=0)
    write_parts(part_refs, pack(product_of(weighted / recon_of(topics, wide_ref[...]), tall_ref[...])))


def numerator_of(topics, quotient):
    high, low = high_low(topics.T[: topics.shape[1] // 2])
    quotient_high, quotient_low = high_low(quotient)
    return matmul(
        jnp.concatenate([high, low, high], axis=1),
        jnp.concatenate([quotient_high, quotient_high, quotient_low], axis=0),
    )


def topics_kernel(chips, before_ref, total_ref, *refs):
    parts, topics_ref = refs[:chips], refs[-1]
    total = sum_packed(chips, [ref[: before_ref.shape[0] // 2] for ref in parts])
    topics_ref[...] = before_ref[...] / total_ref[:1] * total


def numerator_kernel(wide_ref, topics_ref, weighted_ref, *refs):
    before, out_ref = refs[:-1], refs[-1]
    words = weighted_ref.shape[1]
    topics = topics_ref[...]
    load = jnp.sum(topics.T[: topics.shape[1] // 2], axis=1, keepdims=True)
    numerator = numerator_of(topics, weighted_ref[...] / recon_of(topics, wide_ref[:, :words]))
    if out_ref.shape[1] > words:
        out_ref[:, :words] = numerator
        out_ref[:, words:] = jnp.broadcast_to(load, (load.shape[0], out_ref.shape[1] - words))
    else:
        dict_ref, *other = before
        for ref in other:
            numerator = numerator + ref[:, :words]
            load = load + ref[:, words : words + 1]
        out_ref[...] = dict_ref[...] / load * numerator


def base_rows_of(refs, at):
    return jnp.concatenate([ref[:, at] for ref in refs], axis=0)


def refit_kernel(members, chips, half, *refs):
    pieces, payload = refs[:members], refs[members : members + chips]
    *before, wide_ref, tall_ref, part_ref, median_ref = refs[members + chips :]
    sub = pieces[0].shape[1]
    for me in range(members):

        @pl.when(lax.axis_index("pert") == me)
        def _():
            for at in range(members):
                owner = me ^ ((members - at) % members)
                median_ref[:, owner * sub : (owner + 1) * sub] = pieces[at][...]

    words = median_ref.shape[1]
    span = payload[0].shape[1] - part_ref.shape[1]
    wide = jnp.concatenate(high_low(median_ref[...]), axis=0)
    tall = wide.T.astype(jnp.bfloat16)
    wide = wide.astype(jnp.bfloat16)
    wide_ref[...] = wide
    tall_ref[...] = tall
    weighted = base_rows_of(payload, slice(half * words, (half + 1) * words))
    refit = base_rows_of(payload, slice(span, None))
    both = product_of(weighted / recon_of(refit, wide), tall, ones=8)
    both = jnp.concatenate([pack(both[:-8]), both[-8:]], axis=0)
    part_ref[...] = both + before[0][...] if before else both


def refit_again_kernel(chips, cores, base_docs, *refs):
    payload, parts, halves = refs[:chips], refs[chips : 2 * chips], refs[2 * chips : 2 * (chips + cores)]
    scale_ref, *part_refs = refs[2 * (chips + cores) :]
    packed = chips * base_docs // 2
    span = payload[0].shape[1] - scale_ref.shape[1]
    words = span // cores
    median_total = sum(ref[packed : packed + 1] for ref in parts)
    total = sum_packed(chips, [ref[:packed] for ref in parts])
    refit = base_rows_of(payload, slice(span, None)) / median_total * total
    scale_ref[...] = refit[:base_docs] / median_total
    part = None
    for half in range(cores):
        weighted = base_rows_of(payload, slice(half * words, (half + 1) * words))
        wide_ref, tall_ref = halves[2 * half], halves[2 * half + 1]
        new = product_of(weighted / recon_of(refit, wide_ref[...]), tall_ref[...])
        part = new if part is None else part + new
    for step in range(chips):
        part_refs[step][...] = part[step * base_docs : (step + 1) * base_docs]


def finish_kernel(scale_ref, *refs):
    parts, out_ref = refs[:-1], refs[-1]
    out_ref[...] = (scale_ref[...] * sum(ref[...] for ref in parts))[:, : out_ref.shape[1]]


def median_kernel(members, *refs):
    refs[-1][...] = middle([ref[...] for ref in refs[:members]])


def per_device(counts, tile_mask, member_topics, start_dict, align_perm, base_counts, base_topics):
    doc_size = lax.axis_size("doc")
    members = lax.axis_size("pert")
    cores = 2 - doc_size % 2
    chips = doc_size // cores
    at_pert = lax.axis_index("pert")
    at_doc = lax.axis_index("doc")
    at_chip, at_core = at_doc // cores, at_doc % cores
    docs = counts.shape[1]
    base_docs = base_counts.shape[0]
    topic_count = member_topics.shape[2]
    owned = start_dict.shape[1]
    span = cores * owned
    rows = chips * docs
    sub = owned // members

    def over_chips(array, step):
        return lax.ppermute(
            array,
            "doc",
            [
                (c * cores + k, (c ^ step) * cores + (k + step) % cores)
                for c in range(chips)
                for k in range(cores)
            ],
        )

    def over_cores(array):
        return lax.ppermute(array, "doc", [(d, d ^ 1) for d in range(doc_size)])

    def over_pert(array, step):
        return lax.ppermute(array, "pert", [(m, m ^ step) for m in range(members)])

    sent = pl.pallas_call(
        functools.partial(spread_kernel, chips, cores, owned),
        out_shape=[pltpu.VMEM((docs, span + 2 * topic_count), jnp.float32)] * chips,
        in_specs=[pl.BlockSpec(memory_space=pltpu.HBM)] * 4,
        out_specs=[pl.BlockSpec(memory_space=pltpu.VMEM)] * chips,
        scratch_shapes=[
            pltpu.VMEM(tile_mask.shape[1:], jnp.int32),
            pltpu.VMEM(member_topics.shape[1:], jnp.float32),
            pltpu.VMEM(align_perm.shape, jnp.int32),
            pltpu.VMEM((chips, docs, span), jnp.int32),
            pltpu.SemaphoreType.DMA((3,)),
            pltpu.SemaphoreType.DMA((chips, cores)),
        ],
        compiler_params=pltpu.CompilerParams(vmem_limit_bytes=VMEM_BYTES),
        cost_estimate=pl.CostEstimate(flops=0, bytes_accessed=12 * counts.size, transcendentals=0),
    )(*[pltpu.with_memory_space_constraint(x, pltpu.HBM) for x in (tile_mask[0], member_topics[0], align_perm, counts[0])])
    base_sent = call(
        functools.partial(base_kernel, chips, cores),
        [shape(base_docs, span + 2 * topic_count)] * chips,
        base_counts,
        base_topics,
        moved=8 * base_counts.size,
    )
    got = [over_chips(sent[step], step) for step in range(chips - 1, 0, -1)][::-1]
    payload = [sent[0]] + got
    near = [over_chips(base_sent[step], step) for step in range(1, min(chips, 2))]
    dict_own = start_dict[0].T
    halves = [dict_own] + [over_cores(dict_own)] * (cores - 1)
    wide, tall, col_part, dict_own = call(
        functools.partial(dictionary_kernel, cores),
        [
            shape(2 * topic_count, span, dtype=jnp.bfloat16),
            shape(span, 2 * topic_count, dtype=jnp.bfloat16),
            shape(8, 2 * topic_count),
            shape(topic_count, owned),
        ],
        align_perm,
        *halves,
        moved=4 * 4 * span * topic_count,
    )

    update_flops = 2 * 2 * 4 * rows * topic_count * span
    count_order = [chips - 1] + list(range(1, chips - 1)) + [0]
    topics, part, *weighted = call(
        functools.partial(first_kernel, chips, cores, count_order),
        [shape(rows, 2 * topic_count), shape(rows // 2 + 8, 2 * topic_count)]
        + [shape(rows, owned)] * cores,
        wide,
        tall,
        col_part,
        *[payload[step] for step in count_order],
        *near,
        unread=len(near),
        flops=update_flops,
        moved=4 * span * (rows + 2 * topic_count),
    )
    parts = [part] + [over_chips(part, step) for step in range(chips - 1, 0, -1)]
    crossed = [over_cores(weighted[1])] if cores > 1 else []
    totals = []
    for update in range(1, UPDATES):
        topics, *outs = call(
            functools.partial(update_kernel, chips),
            [shape(rows, 2 * topic_count)]
            + [shape(rows // 2 + (0 if totals else step - 1), 2 * topic_count) for step in range(1, chips)]
            + ([] if totals else [shape(8, 2 * topic_count)]),
            wide,
            tall,
            topics,
            *totals,
            *payload[::-1],
            *parts,
            flops=update_flops,
            moved=4 * span * (rows + 2 * topic_count),
        )
        totals = totals or outs[chips - 1 :]
        parts = [outs[0]] + [over_chips(outs[step - 1], step) for step in range(chips - 1, 0, -1)]
    (col_total,) = totals

    topics = call(
        functools.partial(topics_kernel, chips),
        shape(rows, 2 * topic_count),
        topics,
        col_total,
        *parts,
        *crossed,
        unread=len(crossed),
    )
    other = []
    if cores > 1:
        other_topics = over_cores(topics)
        other = [
            call(
                numerator_kernel,
                shape(topic_count, owned + 128),
                wide,
                topics,
                weighted[0],
                flops=update_flops // 2,
                moved=2 * span * (rows + 2 * topic_count),
            )
        ]
        topics, weighted = other_topics, crossed
    aligned = call(
        numerator_kernel,
        shape(topic_count, owned),
        wide,
        topics,
        weighted[0],
        dict_own,
        *other,
        flops=update_flops // 2,
        moved=2 * span * (rows + 2 * topic_count),
    )

    def words_of(array, member):
        return lax.dynamic_slice_in_dim(array, member * sub, sub, 1)

    aligned, base_sent = lax.optimization_barrier((aligned, base_sent))
    base_got = [over_chips(base_sent[step], step) for step in range(2, chips)]
    late = len(base_got) // 2
    base_got = base_got[::-1]
    median = call(
        functools.partial(median_kernel, members),
        pltpu.VMEM((topic_count, sub), jnp.float32),
        words_of(aligned, at_pert),
        *[over_pert(words_of(aligned, at_pert ^ step), step) for step in range(members - 1, 0, -1)],
        *base_got[late:],
        unread=len(base_got) - late,
    )
    pieces = [median] + [over_pert(median, step) for step in range(members - 1, 0, -1)]
    pieces[1], *base_got[:late] = lax.optimization_barrier((pieces[1], *base_got[:late]))
    median_halves = [pieces] + [[over_cores(piece) for piece in pieces]] * (cores - 1)
    base_all = [base_sent[0]] + near + base_got[::-1]

    base_rows = chips * base_docs
    refit_flops = 2 * 2 * 4 * base_rows * topic_count * owned
    forms, before = [], []
    for half in range(cores):
        wide, tall, part = call(
            functools.partial(refit_kernel, members, chips, half),
            [
                shape(2 * topic_count, owned, dtype=jnp.bfloat16),
                shape(owned, 2 * topic_count, dtype=jnp.bfloat16),
                shape(base_rows // 2 + 8, 2 * topic_count),
            ],
            *median_halves[half],
            *base_all,
            *before,
            flops=refit_flops,
            moved=16 * owned * topic_count,
            scratch=[pltpu.VMEM((topic_count, owned), jnp.float32)],
        )
        forms += [wide, tall]
        before = [part]
    scale, *parts = call(
        functools.partial(refit_again_kernel, chips, cores, base_docs),
        [shape(base_docs, 2 * topic_count)] * (chips + 1),
        *base_all,
        part,
        *[over_chips(part, step) for step in range(chips - 1, 0, -1)],
        *forms,
        flops=2 * refit_flops,
        moved=16 * owned * topic_count,
    )
    refit = call(
        finish_kernel,
        shape(base_docs, topic_count),
        scale,
        parts[0],
        *[over_chips(parts[step], step) for step in range(chips - 1, 0, -1)],
    )
    return (median.T[None, None], refit)


def solution(mesh):
    return jax.shard_map(
        per_device,
        mesh=mesh,
        in_specs=(
            P("pert", "doc", None),
            P("pert", "doc", None),
            P("pert", "doc", None),
            P("pert", "doc", None),
            P("pert", None),
            P(("pert", "doc"), None),
            P(("pert", "doc"), None),
        ),
        out_specs=(P("doc", "pert", None, None), P(("pert", "doc"), None)),
        check_vma=False,
    )
```

```python
import functools

import jax
import jax.numpy as jnp
from jax import lax
from jax.experimental import pallas as pl
from jax.experimental.pallas import tpu as pltpu
from jax.sharding import PartitionSpec as P

UPDATES = 3
REFITS = 2

EXACT = lax.Precision.HIGHEST
ROUGH = lax.Precision.HIGH
VMEM_BYTES = 14 * 1024 * 1024
SPREAD_BYTES = 60 * 1024 * 1024


def dot(left, right, dims, precision=ROUGH):
    return lax.dot_general(left, right, (dims, ((), ())), precision=precision)


def middle(pieces):
    pieces = list(pieces)
    count = len(pieces)
    for turn in range(count):
        for low in range(turn % 2, count - 1, 2):
            pieces[low], pieces[low + 1] = (
                jnp.minimum(pieces[low], pieces[low + 1]),
                jnp.maximum(pieces[low], pieces[low + 1]),
            )
    return 0.5 * (pieces[count // 2 - 1] + pieces[count // 2])


def call(kernel, outs, *args, flops=0, moved=0, unread=0, scratch=()):
    read = len(args) - unread
    return pl.pallas_call(
        kernel,
        out_shape=outs,
        in_specs=[pl.BlockSpec(memory_space=pltpu.VMEM)] * read
        + [pl.BlockSpec(memory_space=pl.ANY)] * unread,
        scratch_shapes=scratch,
        compiler_params=pltpu.CompilerParams(vmem_limit_bytes=VMEM_BYTES),
        cost_estimate=pl.CostEstimate(flops=flops, bytes_accessed=moved, transcendentals=0),
    )(*args)


def shape(*dims, dtype=jnp.float32):
    return jax.ShapeDtypeStruct(dims, dtype)


def high_low(x):
    high = x.astype(jnp.bfloat16).astype(jnp.float32)
    return high, x - high


def matmul(left, right):
    return jnp.dot(
        left.astype(jnp.bfloat16), right.astype(jnp.bfloat16), preferred_element_type=jnp.float32
    )


def blocks_of(chips, cores, step):
    at_doc = lax.axis_index("doc")
    at_chip, at_core = at_doc // cores, at_doc % cores
    return [(at_chip ^ step) * cores + (at_core ^ ((step + half) % cores)) for half in range(cores)]


def spread_kernel(chips, cores, own_words, mask_hbm, topics_hbm, perm_hbm, counts_hbm, *refs):
    out_refs, (mask_ref, topics_ref, perm_ref, counts_ref, small_sems, in_sems) = (
        refs[:chips],
        refs[chips:],
    )
    small = [
        pltpu.make_async_copy(mask_hbm, mask_ref, small_sems.at[0]),
        pltpu.make_async_copy(topics_hbm, topics_ref, small_sems.at[1]),
        pltpu.make_async_copy(perm_hbm, perm_ref, small_sems.at[2]),
    ]
    for copy in small:
        copy.start()
    steps = list(range(chips - 1, -1, -1))
    at_chip = lax.axis_index("doc") // cores
    arriving = {}
    for step in steps:
        first = (at_chip ^ step) * cores * own_words
        arriving[step] = pltpu.make_async_copy(
            counts_hbm.at[:, pl.ds(pl.multiple_of(first, 128), cores * own_words)],
            counts_ref.at[step],
            in_sems.at[step],
        )
        arriving[step].start()
    docs, tiles = mask_ref.shape
    width = chips * cores * own_words // tiles
    own_tiles = own_words // width
    tile_ids = lax.broadcasted_iota(jnp.int32, (docs, tiles), 1)
    doc_ids = lax.axis_index("doc") * docs + lax.broadcasted_iota(jnp.int32, (docs, tiles), 0)
    forced = (tile_ids == doc_ids % tiles).astype(jnp.int32)
    for copy in small:
        copy.wait()
    occupied = jnp.maximum(mask_ref[...], forced).astype(jnp.float32)
    topic_count = topics_ref.shape[1]
    onehot = lax.broadcasted_iota(jnp.int32, (topic_count, 2 * topic_count), 0) == jnp.concatenate(
        [perm_ref[...]] * 2, axis=1
    )
    topics = moved_columns(topics_ref[...], onehot.astype(jnp.float32))
    for step in steps:
        for half, block in enumerate(blocks_of(chips, cores, step)):
            near = pltpu.roll(occupied, lax.rem(tiles - block * own_tiles, tiles), 1)
            if half == 0:
                arriving[step].wait()
            first = lax.rem(block, cores) * own_words
            for tile in range(own_tiles):
                at = slice(half * own_words + tile * width, half * own_words + (tile + 1) * width)
                picked = counts_ref[step, :, pl.ds(pl.multiple_of(first + tile * width, 128), width)]
                picked = picked.astype(jnp.float32)
                out_refs[step][:, at] = picked * near[:, tile : tile + 1]
        out_refs[step][:, cores * own_words :] = topics


def base_kernel(chips, cores, counts_ref, topics_ref, *out_refs):
    span = out_refs[0].shape[1] - 2 * topics_ref.shape[1]
    own_words = span // cores
    for step in range(chips):
        for half, block in enumerate(blocks_of(chips, cores, step)):
            at = slice(half * own_words, (half + 1) * own_words)
            first = pl.multiple_of(block * own_words, 128)
            out_refs[step][:, at] = counts_ref[:, pl.ds(first, own_words)].astype(jnp.float32)
        out_refs[step][:, span:] = jnp.concatenate([topics_ref[...]] * 2, axis=1)


def moved_columns(x, onehot):
    rows = x.shape[0]
    high, rest = high_low(x)
    mid, low = high_low(rest)
    moved = matmul(jnp.concatenate([high, mid, low], axis=0), onehot)
    return moved[:rows] + moved[rows : 2 * rows] + moved[2 * rows :]


def dictionary_kernel(half_count, perm_ref, *refs):
    topics, words = refs[0].shape
    wide_ref, tall_ref, total_ref, own_ref = refs[half_count:]
    turned_onehot = (
        (lax.broadcasted_iota(jnp.int32, (topics, topics), 0) == perm_ref[...]).astype(jnp.float32).T
    )
    total = jnp.zeros((1, 2 * topics), jnp.float32)
    for half in range(half_count):
        at = slice(half * words, (half + 1) * words)
        high, rest = high_low(refs[half][...])
        mid, low = high_low(rest)
        aligned = matmul(
            jnp.concatenate([turned_onehot] * 3, axis=1), jnp.concatenate([high, mid, low], axis=0)
        )
        if half == 0:
            own_ref[...] = aligned
        wide = jnp.concatenate(high_low(aligned), axis=0)
        wide_ref[:, at] = wide.astype(jnp.bfloat16)
        tall = wide.T
        total += jnp.sum(tall, axis=0, keepdims=True)
        tall_ref[at, :] = tall.astype(jnp.bfloat16)
    total_ref[...] = jnp.broadcast_to(total + turned(total), total_ref.shape)


def recon_of(doubled, wide):
    rows = doubled.shape[0]
    both = matmul(jnp.concatenate(high_low(doubled), axis=0), wide)
    return both[:rows] + both[rows:]


def product_of(quotient, tall, ones=0):
    rows = quotient.shape[0]
    left = [*high_low(quotient)] + [jnp.ones((ones, quotient.shape[1]), jnp.float32)] * (ones > 0)
    both = matmul(jnp.concatenate(left, axis=0), tall)
    both = [both[:rows] + both[rows : 2 * rows], both[2 * rows :]]
    both = jnp.concatenate(both, axis=0) if ones else both[0]
    return both + turned(both)


def turned(x):
    return pltpu.roll(x, x.shape[1] // 2, 1)


def left_half(x):
    return lax.broadcasted_iota(jnp.int32, x.shape, 1) < x.shape[1] // 2


def pack(doubled):
    half = doubled.shape[0] // 2
    lower, upper = doubled[:half], doubled[half:]
    return jnp.where(left_half(lower), lower, upper)


def sum_packed(chips, parts):
    parts = [parts[0], *parts[:0:-1]]
    side = max(chips // 2, 1)
    rows = parts[0].shape[0] // side

    def moved(x, step):
        if step == 0:
            return x
        return jnp.concatenate([x[(c ^ step) * rows : ((c ^ step) + 1) * rows] for c in range(side)], axis=0)

    sums = []
    for first in range(0, chips, side):
        sums.append(sum(moved(parts[step], step - first) for step in range(first, first + side)))
    packed, other = sums[0] + turned(sums[1]), turned(sums[0]) + sums[1]
    left = left_half(packed)
    return jnp.concatenate([jnp.where(left, packed, other), jnp.where(left, other, packed)], axis=0)


def write_parts(refs, part):
    rows = part.shape[0]
    for ref in refs:
        ref[:rows] = part
        if ref.shape[0] > rows:
            ref[rows:] = jnp.zeros((ref.shape[0] - rows, part.shape[1]), part.dtype)


def first_kernel(chips, cores, order, wide_ref, tall_ref, col_part_ref, *refs):
    payload = [refs[order.index(step)] for step in range(chips)]
    topics_ref, part_ref, *half_refs = refs[-2 - cores :]
    span = wide_ref.shape[1]
    topics = jnp.concatenate([ref[:, span:] for ref in payload], axis=0)
    topics_ref[...] = topics
    weighted = jnp.concatenate([ref[:, :span] for ref in payload], axis=0)
    part = pack(product_of(weighted / recon_of(topics, wide_ref[...]), tall_ref[...]))
    part_ref[: part.shape[0]] = part
    part_ref[part.shape[0] :] = col_part_ref[...]
    words = span // cores
    for half, ref in enumerate(half_refs):
        ref[...] = weighted[:, half * words : (half + 1) * words]


def update_kernel(chips, wide_ref, tall_ref, before_ref, *refs):
    packed = before_ref.shape[0] // 2
    if refs[-1].shape[0] == 8:
        payload, parts = refs[:chips][::-1], refs[chips : 2 * chips]
        topics_ref, *part_refs, total_ref = refs[2 * chips :]
        total_ref[...] = sum(ref[packed:] for ref in parts)
    else:
        total_ref, payload, parts = refs[0], refs[1 : chips + 1][::-1], refs[chips + 1 : 2 * chips + 1]
        topics_ref, *part_refs = refs[2 * chips + 1 :]
    span = wide_ref.shape[1]
    total = sum_packed(chips, [ref[:packed] for ref in parts])
    topics = before_ref[...] / total_ref[:1] * total
    topics_ref[...] = topics
    weighted = jnp.concatenate([ref[:, :span] for ref in payload], axis=0)
    write_parts(part_refs, pack(product_of(weighted / recon_of(topics, wide_ref[...]), tall_ref[...])))


def numerator_of(topics, quotient):
    high, low = high_low(topics.T[: topics.shape[1] // 2])
    quotient_high, quotient_low = high_low(quotient)
    return matmul(
        jnp.concatenate([high, low, high], axis=1),
        jnp.concatenate([quotient_high, quotient_high, quotient_low], axis=0),
    )


def topics_kernel(chips, before_ref, total_ref, *refs):
    parts, topics_ref = refs[:chips], refs[-1]
    total = sum_packed(chips, [ref[: before_ref.shape[0] // 2] for ref in parts])
    topics_ref[...] = before_ref[...] / total_ref[:1] * total


def numerator_kernel(wide_ref, topics_ref, weighted_ref, *refs):
    before, out_ref = refs[:-1], refs[-1]
    words = weighted_ref.shape[1]
    topics = topics_ref[...]
    load = jnp.sum(topics.T[: topics.shape[1] // 2], axis=1, keepdims=True)
    numerator = numerator_of(topics, weighted_ref[...] / recon_of(topics, wide_ref[:, :words]))
    if out_ref.shape[1] > words:
        out_ref[:, :words] = numerator
        out_ref[:, words:] = jnp.broadcast_to(load, (load.shape[0], out_ref.shape[1] - words))
    else:
        dict_ref, *other = before
        for ref in other:
            numerator = numerator + ref[:, :words]
            load = load + ref[:, words : words + 1]
        out_ref[...] = dict_ref[...] / load * numerator


def base_rows_of(refs, at):
    return jnp.concatenate([ref[:, at] for ref in refs], axis=0)


def refit_kernel(members, chips, half, *refs):
    pieces, payload = refs[:members], refs[members : members + chips]
    *before, wide_ref, tall_ref, part_ref, median_ref = refs[members + chips :]
    sub = pieces[0].shape[1]
    for me in range(members):

        @pl.when(lax.axis_index("pert") == me)
        def _():
            for at in range(members):
                owner = me ^ ((members - at) % members)
                median_ref[:, owner * sub : (owner + 1) * sub] = pieces[at][...]

    words = median_ref.shape[1]
    span = payload[0].shape[1] - part_ref.shape[1]
    wide = jnp.concatenate(high_low(median_ref[...]), axis=0)
    tall = wide.T.astype(jnp.bfloat16)
    wide = wide.astype(jnp.bfloat16)
    wide_ref[...] = wide
    tall_ref[...] = tall
    weighted = base_rows_of(payload, slice(half * words, (half + 1) * words))
    refit = base_rows_of(payload, slice(span, None))
    both = product_of(weighted / recon_of(refit, wide), tall, ones=8)
    both = jnp.concatenate([pack(both[:-8]), both[-8:]], axis=0)
    part_ref[...] = both + before[0][...] if before else both


def refit_again_kernel(chips, cores, base_docs, *refs):
    payload, parts, halves = refs[:chips], refs[chips : 2 * chips], refs[2 * chips : 2 * (chips + cores)]
    scale_ref, *part_refs = refs[2 * (chips + cores) :]
    packed = chips * base_docs // 2
    span = payload[0].shape[1] - scale_ref.shape[1]
    words = span // cores
    median_total = sum(ref[packed : packed + 1] for ref in parts)
    total = sum_packed(chips, [ref[:packed] for ref in parts])
    refit = base_rows_of(payload, slice(span, None)) / median_total * total
    scale_ref[...] = refit[:base_docs] / median_total
    part = None
    for half in range(cores):
        weighted = base_rows_of(payload, slice(half * words, (half + 1) * words))
        wide_ref, tall_ref = halves[2 * half], halves[2 * half + 1]
        new = product_of(weighted / recon_of(refit, wide_ref[...]), tall_ref[...])
        part = new if part is None else part + new
    for step in range(chips):
        part_refs[step][...] = part[step * base_docs : (step + 1) * base_docs]


def finish_kernel(scale_ref, *refs):
    parts, out_ref = refs[:-1], refs[-1]
    out_ref[...] = (scale_ref[...] * sum(ref[...] for ref in parts))[:, : out_ref.shape[1]]


def median_kernel(members, *refs):
    refs[-1][...] = middle([ref[...] for ref in refs[:members]])


def per_device(counts, tile_mask, member_topics, start_dict, align_perm, base_counts, base_topics):
    doc_size = lax.axis_size("doc")
    members = lax.axis_size("pert")
    cores = 2 - doc_size % 2
    chips = doc_size // cores
    at_pert = lax.axis_index("pert")
    at_doc = lax.axis_index("doc")
    at_chip, at_core = at_doc // cores, at_doc % cores
    docs = counts.shape[1]
    base_docs = base_counts.shape[0]
    topic_count = member_topics.shape[2]
    owned = start_dict.shape[1]
    span = cores * owned
    rows = chips * docs
    sub = owned // members

    def over_chips(array, step):
        return lax.ppermute(
            array,
            "doc",
            [
                (c * cores + k, (c ^ step) * cores + (k + step) % cores)
                for c in range(chips)
                for k in range(cores)
            ],
        )

    def over_cores(array):
        return lax.ppermute(array, "doc", [(d, d ^ 1) for d in range(doc_size)])

    def over_pert(array, step):
        return lax.ppermute(array, "pert", [(m, m ^ step) for m in range(members)])

    sent = pl.pallas_call(
        functools.partial(spread_kernel, chips, cores, owned),
        out_shape=[pltpu.VMEM((docs, span + 2 * topic_count), jnp.float32)] * chips,
        in_specs=[pl.BlockSpec(memory_space=pltpu.HBM)] * 4,
        out_specs=[pl.BlockSpec(memory_space=pltpu.VMEM)] * chips,
        scratch_shapes=[
            pltpu.VMEM(tile_mask.shape[1:], jnp.int32),
            pltpu.VMEM(member_topics.shape[1:], jnp.float32),
            pltpu.VMEM(align_perm.shape, jnp.int32),
            pltpu.VMEM((chips, docs, span), jnp.int32),
            pltpu.SemaphoreType.DMA((3,)),
            pltpu.SemaphoreType.DMA((chips,)),
        ],
        compiler_params=pltpu.CompilerParams(vmem_limit_bytes=VMEM_BYTES),
        cost_estimate=pl.CostEstimate(flops=0, bytes_accessed=12 * counts.size, transcendentals=0),
    )(*[pltpu.with_memory_space_constraint(x, pltpu.HBM) for x in (tile_mask[0], member_topics[0], align_perm, counts[0])])
    base_sent = call(
        functools.partial(base_kernel, chips, cores),
        [shape(base_docs, span + 2 * topic_count)] * chips,
        base_counts,
        base_topics,
        moved=8 * base_counts.size,
    )
    got = [over_chips(sent[step], step) for step in range(chips - 1, 0, -1)][::-1]
    payload = [sent[0]] + got
    near = [over_chips(base_sent[step], step) for step in range(1, min(chips, 2))]
    dict_own = start_dict[0].T
    halves = [dict_own] + [over_cores(dict_own)] * (cores - 1)
    wide, tall, col_part, dict_own = call(
        functools.partial(dictionary_kernel, cores),
        [
            shape(2 * topic_count, span, dtype=jnp.bfloat16),
            shape(span, 2 * topic_count, dtype=jnp.bfloat16),
            shape(8, 2 * topic_count),
            shape(topic_count, owned),
        ],
        align_perm,
        *halves,
        moved=4 * 4 * span * topic_count,
    )

    update_flops = 2 * 2 * 4 * rows * topic_count * span
    count_order = [chips - 1] + list(range(1, chips - 1)) + [0]
    topics, part, *weighted = call(
        functools.partial(first_kernel, chips, cores, count_order),
        [shape(rows, 2 * topic_count), shape(rows // 2 + 8, 2 * topic_count)]
        + [shape(rows, owned)] * cores,
        wide,
        tall,
        col_part,
        *[payload[step] for step in count_order],
        *near,
        unread=len(near),
        flops=update_flops,
        moved=4 * span * (rows + 2 * topic_count),
    )
    parts = [part] + [over_chips(part, step) for step in range(chips - 1, 0, -1)]
    crossed = [over_cores(weighted[1])] if cores > 1 else []
    totals = []
    for update in range(1, UPDATES):
        topics, *outs = call(
            functools.partial(update_kernel, chips),
            [shape(rows, 2 * topic_count)]
            + [shape(rows // 2 + (0 if totals else step - 1), 2 * topic_count) for step in range(1, chips)]
            + ([] if totals else [shape(8, 2 * topic_count)]),
            wide,
            tall,
            topics,
            *totals,
            *payload[::-1],
            *parts,
            flops=update_flops,
            moved=4 * span * (rows + 2 * topic_count),
        )
        totals = totals or outs[chips - 1 :]
        parts = [outs[0]] + [over_chips(outs[step - 1], step) for step in range(chips - 1, 0, -1)]
    (col_total,) = totals

    topics = call(
        functools.partial(topics_kernel, chips),
        shape(rows, 2 * topic_count),
        topics,
        col_total,
        *parts,
        *crossed,
        unread=len(crossed),
    )
    other = []
    if cores > 1:
        other_topics = over_cores(topics)
        other = [
            call(
                numerator_kernel,
                shape(topic_count, owned + 128),
                wide,
                topics,
                weighted[0],
                flops=update_flops // 2,
                moved=2 * span * (rows + 2 * topic_count),
            )
        ]
        topics, weighted = other_topics, crossed
    aligned = call(
        numerator_kernel,
        shape(topic_count, owned),
        wide,
        topics,
        weighted[0],
        dict_own,
        *other,
        flops=update_flops // 2,
        moved=2 * span * (rows + 2 * topic_count),
    )

    def words_of(array, member):
        return lax.dynamic_slice_in_dim(array, member * sub, sub, 1)

    aligned, base_sent = lax.optimization_barrier((aligned, base_sent))
    base_got = [over_chips(base_sent[step], step) for step in range(2, chips)]
    late = len(base_got) // 2
    base_got = base_got[::-1]
    median = call(
        functools.partial(median_kernel, members),
        pltpu.VMEM((topic_count, sub), jnp.float32),
        words_of(aligned, at_pert),
        *[over_pert(words_of(aligned, at_pert ^ step), step) for step in range(members - 1, 0, -1)],
        *base_got[late:],
        unread=len(base_got) - late,
    )
    pieces = [median] + [over_pert(median, step) for step in range(members - 1, 0, -1)]
    pieces[1], *base_got[:late] = lax.optimization_barrier((pieces[1], *base_got[:late]))
    median_halves = [pieces] + [[over_cores(piece) for piece in pieces]] * (cores - 1)
    base_all = [base_sent[0]] + near + base_got[::-1]

    base_rows = chips * base_docs
    refit_flops = 2 * 2 * 4 * base_rows * topic_count * owned
    forms, before = [], []
    for half in range(cores):
        wide, tall, part = call(
            functools.partial(refit_kernel, members, chips, half),
            [
                shape(2 * topic_count, owned, dtype=jnp.bfloat16),
                shape(owned, 2 * topic_count, dtype=jnp.bfloat16),
                shape(base_rows // 2 + 8, 2 * topic_count),
            ],
            *median_halves[half],
            *base_all,
            *before,
            flops=refit_flops,
            moved=16 * owned * topic_count,
            scratch=[pltpu.VMEM((topic_count, owned), jnp.float32)],
        )
        forms += [wide, tall]
        before = [part]
    scale, *parts = call(
        functools.partial(refit_again_kernel, chips, cores, base_docs),
        [shape(base_docs, 2 * topic_count)] * (chips + 1),
        *base_all,
        part,
        *[over_chips(part, step) for step in range(chips - 1, 0, -1)],
        *forms,
        flops=2 * refit_flops,
        moved=16 * owned * topic_count,
    )
    refit = call(
        finish_kernel,
        shape(base_docs, topic_count),
        scale,
        parts[0],
        *[over_chips(parts[step], step) for step in range(chips - 1, 0, -1)],
    )
    return (median.T[None, None], refit)


def solution(mesh):
    return jax.shard_map(
        per_device,
        mesh=mesh,
        in_specs=(
            P("pert", "doc", None),
            P("pert", "doc", None),
            P("pert", "doc", None),
            P("pert", "doc", None),
            P("pert", None),
            P(("pert", "doc"), None),
            P(("pert", "doc"), None),
        ),
        out_specs=(P("doc", "pert", None, None), P(("pert", "doc"), None)),
        check_vma=False,
    )
```

```python
import functools

import jax
import jax.numpy as jnp
from jax import lax
from jax.experimental import pallas as pl
from jax.experimental.pallas import tpu as pltpu
from jax.sharding import PartitionSpec as P

UPDATES = 3
REFITS = 2

EXACT = lax.Precision.HIGHEST
ROUGH = lax.Precision.HIGH
VMEM_BYTES = 14 * 1024 * 1024
SPREAD_BYTES = 60 * 1024 * 1024


def dot(left, right, dims, precision=ROUGH):
    return lax.dot_general(left, right, (dims, ((), ())), precision=precision)


def middle(pieces):
    pieces = list(pieces)
    count = len(pieces)
    for turn in range(count):
        for low in range(turn % 2, count - 1, 2):
            pieces[low], pieces[low + 1] = (
                jnp.minimum(pieces[low], pieces[low + 1]),
                jnp.maximum(pieces[low], pieces[low + 1]),
            )
    return 0.5 * (pieces[count // 2 - 1] + pieces[count // 2])


def call(kernel, outs, *args, flops=0, moved=0, unread=0, scratch=()):
    read = len(args) - unread
    return pl.pallas_call(
        kernel,
        out_shape=outs,
        in_specs=[pl.BlockSpec(memory_space=pltpu.VMEM)] * read
        + [pl.BlockSpec(memory_space=pl.ANY)] * unread,
        scratch_shapes=scratch,
        compiler_params=pltpu.CompilerParams(vmem_limit_bytes=VMEM_BYTES),
        cost_estimate=pl.CostEstimate(flops=flops, bytes_accessed=moved, transcendentals=0),
    )(*args)


def shape(*dims, dtype=jnp.float32):
    return jax.ShapeDtypeStruct(dims, dtype)


def high_low(x):
    high = x.astype(jnp.bfloat16).astype(jnp.float32)
    return high, x - high


def matmul(left, right):
    return jnp.dot(
        left.astype(jnp.bfloat16), right.astype(jnp.bfloat16), preferred_element_type=jnp.float32
    )


def blocks_of(chips, cores, step):
    at_doc = lax.axis_index("doc")
    at_chip, at_core = at_doc // cores, at_doc % cores
    return [(at_chip ^ step) * cores + (at_core ^ ((step + half) % cores)) for half in range(cores)]


def spread_kernel(chips, cores, own_words, mask_hbm, topics_hbm, perm_hbm, counts_hbm, *refs):
    out_refs, (mask_ref, topics_ref, perm_ref, counts_ref, small_sems, in_sems) = (
        refs[:chips],
        refs[chips:],
    )
    small = [
        pltpu.make_async_copy(mask_hbm, mask_ref, small_sems.at[0]),
        pltpu.make_async_copy(topics_hbm, topics_ref, small_sems.at[1]),
        pltpu.make_async_copy(perm_hbm, perm_ref, small_sems.at[2]),
    ]
    for copy in small:
        copy.start()
    steps = list(range(chips - 1, -1, -1))
    at_chip = lax.axis_index("doc") // cores
    arriving = {}
    for step in steps:
        first = (at_chip ^ step) * cores * own_words
        arriving[step] = pltpu.make_async_copy(
            counts_hbm.at[:, pl.ds(pl.multiple_of(first, 128), cores * own_words)],
            counts_ref.at[step],
            in_sems.at[step],
        )
        arriving[step].start()
    docs, tiles = mask_ref.shape
    width = chips * cores * own_words // tiles
    own_tiles = own_words // width
    tile_ids = lax.broadcasted_iota(jnp.int32, (docs, tiles), 1)
    doc_ids = lax.axis_index("doc") * docs + lax.broadcasted_iota(jnp.int32, (docs, tiles), 0)
    forced = (tile_ids == doc_ids % tiles).astype(jnp.int32)
    for copy in small:
        copy.wait()
    occupied = jnp.maximum(mask_ref[...], forced).astype(jnp.float32)
    topic_count = topics_ref.shape[1]
    onehot = lax.broadcasted_iota(jnp.int32, (topic_count, 2 * topic_count), 0) == jnp.concatenate(
        [perm_ref[...]] * 2, axis=1
    )
    topics = moved_columns(topics_ref[...], onehot.astype(jnp.float32))
    for step in steps:
        for half, block in enumerate(blocks_of(chips, cores, step)):
            near = pltpu.roll(occupied, lax.rem(tiles - block * own_tiles, tiles), 1)
            for tile in range(own_tiles):
                at = slice(half * own_words + tile * width, half * own_words + (tile + 1) * width)
                out_refs[step][:, at] = jnp.broadcast_to(near[:, tile : tile + 1], (docs, width))
        out_refs[step][:, cores * own_words :] = topics
    for step in steps:
        arriving[step].wait()
        for half, block in enumerate(blocks_of(chips, cores, step)):
            at = slice(half * own_words, (half + 1) * own_words)
            first = pl.multiple_of(lax.rem(block, cores) * own_words, 128)
            out_refs[step][:, at] *= counts_ref[step, :, pl.ds(first, own_words)].astype(jnp.float32)


def base_kernel(chips, cores, counts_ref, topics_ref, *out_refs):
    span = out_refs[0].shape[1] - 2 * topics_ref.shape[1]
    own_words = span // cores
    for step in range(chips):
        for half, block in enumerate(blocks_of(chips, cores, step)):
            at = slice(half * own_words, (half + 1) * own_words)
            first = pl.multiple_of(block * own_words, 128)
            out_refs[step][:, at] = counts_ref[:, pl.ds(first, own_words)].astype(jnp.float32)
        out_refs[step][:, span:] = jnp.concatenate([topics_ref[...]] * 2, axis=1)


def moved_columns(x, onehot):
    rows = x.shape[0]
    high, rest = high_low(x)
    mid, low = high_low(rest)
    moved = matmul(jnp.concatenate([high, mid, low], axis=0), onehot)
    return moved[:rows] + moved[rows : 2 * rows] + moved[2 * rows :]


def dictionary_kernel(half_count, perm_ref, *refs):
    topics, words = refs[0].shape
    wide_ref, tall_ref, total_ref, own_ref = refs[half_count:]
    turned_onehot = (
        (lax.broadcasted_iota(jnp.int32, (topics, topics), 0) == perm_ref[...]).astype(jnp.float32).T
    )
    total = jnp.zeros((1, 2 * topics), jnp.float32)
    for half in range(half_count):
        at = slice(half * words, (half + 1) * words)
        high, rest = high_low(refs[half][...])
        mid, low = high_low(rest)
        aligned = matmul(
            jnp.concatenate([turned_onehot] * 3, axis=1), jnp.concatenate([high, mid, low], axis=0)
        )
        if half == 0:
            own_ref[...] = aligned
        wide = jnp.concatenate(high_low(aligned), axis=0)
        wide_ref[:, at] = wide.astype(jnp.bfloat16)
        tall = wide.T
        total += jnp.sum(tall, axis=0, keepdims=True)
        tall_ref[at, :] = tall.astype(jnp.bfloat16)
    total_ref[...] = jnp.broadcast_to(total + turned(total), total_ref.shape)


def recon_of(doubled, wide):
    rows = doubled.shape[0]
    both = matmul(jnp.concatenate(high_low(doubled), axis=0), wide)
    return both[:rows] + both[rows:]


def product_of(quotient, tall, ones=0):
    rows = quotient.shape[0]
    left = [*high_low(quotient)] + [jnp.ones((ones, quotient.shape[1]), jnp.float32)] * (ones > 0)
    both = matmul(jnp.concatenate(left, axis=0), tall)
    both = [both[:rows] + both[rows : 2 * rows], both[2 * rows :]]
    both = jnp.concatenate(both, axis=0) if ones else both[0]
    return both + turned(both)


def turned(x):
    return pltpu.roll(x, x.shape[1] // 2, 1)


def left_half(x):
    return lax.broadcasted_iota(jnp.int32, x.shape, 1) < x.shape[1] // 2


def pack(doubled):
    half = doubled.shape[0] // 2
    lower, upper = doubled[:half], doubled[half:]
    return jnp.where(left_half(lower), lower, upper)


def sum_packed(chips, parts):
    parts = [parts[0], *parts[:0:-1]]
    side = max(chips // 2, 1)
    rows = parts[0].shape[0] // side

    def moved(x, step):
        if step == 0:
            return x
        return jnp.concatenate([x[(c ^ step) * rows : ((c ^ step) + 1) * rows] for c in range(side)], axis=0)

    sums = []
    for first in range(0, chips, side):
        sums.append(sum(moved(parts[step], step - first) for step in range(first, first + side)))
    packed, other = sums[0] + turned(sums[1]), turned(sums[0]) + sums[1]
    left = left_half(packed)
    return jnp.concatenate([jnp.where(left, packed, other), jnp.where(left, other, packed)], axis=0)


def write_parts(refs, part):
    rows = part.shape[0]
    for ref in refs:
        ref[:rows] = part
        if ref.shape[0] > rows:
            ref[rows:] = jnp.zeros((ref.shape[0] - rows, part.shape[1]), part.dtype)


def first_kernel(chips, cores, order, wide_ref, tall_ref, col_part_ref, *refs):
    payload = [refs[order.index(step)] for step in range(chips)]
    topics_ref, part_ref, *half_refs = refs[-2 - cores :]
    span = wide_ref.shape[1]
    topics = jnp.concatenate([ref[:, span:] for ref in payload], axis=0)
    topics_ref[...] = topics
    weighted = jnp.concatenate([ref[:, :span] for ref in payload], axis=0)
    part = pack(product_of(weighted / recon_of(topics, wide_ref[...]), tall_ref[...]))
    part_ref[: part.shape[0]] = part
    part_ref[part.shape[0] :] = col_part_ref[...]
    words = span // cores
    for half, ref in enumerate(half_refs):
        ref[...] = weighted[:, half * words : (half + 1) * words]


def update_kernel(chips, wide_ref, tall_ref, before_ref, *refs):
    packed = before_ref.shape[0] // 2
    if refs[-1].shape[0] == 8:
        payload, parts = refs[:chips][::-1], refs[chips : 2 * chips]
        topics_ref, *part_refs, total_ref = refs[2 * chips :]
        total_ref[...] = sum(ref[packed:] for ref in parts)
    else:
        total_ref, payload, parts = refs[0], refs[1 : chips + 1][::-1], refs[chips + 1 : 2 * chips + 1]
        topics_ref, *part_refs = refs[2 * chips + 1 :]
    span = wide_ref.shape[1]
    total = sum_packed(chips, [ref[:packed] for ref in parts])
    topics = before_ref[...] / total_ref[:1] * total
    topics_ref[...] = topics
    weighted = jnp.concatenate([ref[:, :span] for ref in payload], axis=0)
    write_parts(part_refs, pack(product_of(weighted / recon_of(topics, wide_ref[...]), tall_ref[...])))


def numerator_of(topics, quotient):
    high, low = high_low(topics.T[: topics.shape[1] // 2])
    quotient_high, quotient_low = high_low(quotient)
    return matmul(
        jnp.concatenate([high, low, high], axis=1),
        jnp.concatenate([quotient_high, quotient_high, quotient_low], axis=0),
    )


def topics_kernel(chips, before_ref, total_ref, *refs):
    parts, topics_ref = refs[:chips], refs[-1]
    total = sum_packed(chips, [ref[: before_ref.shape[0] // 2] for ref in parts])
    topics_ref[...] = before_ref[...] / total_ref[:1] * total


def numerator_kernel(wide_ref, topics_ref, weighted_ref, *refs):
    before, out_ref = refs[:-1], refs[-1]
    words = weighted_ref.shape[1]
    topics = topics_ref[...]
    load = jnp.sum(topics.T[: topics.shape[1] // 2], axis=1, keepdims=True)
    numerator = numerator_of(topics, weighted_ref[...] / recon_of(topics, wide_ref[:, :words]))
    if out_ref.shape[1] > words:
        out_ref[:, :words] = numerator
        out_ref[:, words:] = jnp.broadcast_to(load, (load.shape[0], out_ref.shape[1] - words))
    else:
        dict_ref, *other = before
        for ref in other:
            numerator = numerator + ref[:, :words]
            load = load + ref[:, words : words + 1]
        out_ref[...] = dict_ref[...] / load * numerator


def base_rows_of(refs, at):
    return jnp.concatenate([ref[:, at] for ref in refs], axis=0)


def refit_kernel(members, chips, half, *refs):
    pieces, payload = refs[:members], refs[members : members + chips]
    *before, wide_ref, tall_ref, part_ref, median_ref = refs[members + chips :]
    sub = pieces[0].shape[1]
    for me in range(members):

        @pl.when(lax.axis_index("pert") == me)
        def _():
            for at in range(members):
                owner = me ^ ((members - at) % members)
                median_ref[:, owner * sub : (owner + 1) * sub] = pieces[at][...]

    words = median_ref.shape[1]
    span = payload[0].shape[1] - part_ref.shape[1]
    wide = jnp.concatenate(high_low(median_ref[...]), axis=0)
    tall = wide.T.astype(jnp.bfloat16)
    wide = wide.astype(jnp.bfloat16)
    wide_ref[...] = wide
    tall_ref[...] = tall
    weighted = base_rows_of(payload, slice(half * words, (half + 1) * words))
    refit = base_rows_of(payload, slice(span, None))
    both = product_of(weighted / recon_of(refit, wide), tall, ones=8)
    both = jnp.concatenate([pack(both[:-8]), both[-8:]], axis=0)
    part_ref[...] = both + before[0][...] if before else both


def refit_again_kernel(chips, cores, base_docs, *refs):
    payload, parts, halves = refs[:chips], refs[chips : 2 * chips], refs[2 * chips : 2 * (chips + cores)]
    scale_ref, *part_refs = refs[2 * (chips + cores) :]
    packed = chips * base_docs // 2
    span = payload[0].shape[1] - scale_ref.shape[1]
    words = span // cores
    median_total = sum(ref[packed : packed + 1] for ref in parts)
    total = sum_packed(chips, [ref[:packed] for ref in parts])
    refit = base_rows_of(payload, slice(span, None)) / median_total * total
    scale_ref[...] = refit[:base_docs] / median_total
    part = None
    for half in range(cores):
        weighted = base_rows_of(payload, slice(half * words, (half + 1) * words))
        wide_ref, tall_ref = halves[2 * half], halves[2 * half + 1]
        new = product_of(weighted / recon_of(refit, wide_ref[...]), tall_ref[...])
        part = new if part is None else part + new
    for step in range(chips):
        part_refs[step][...] = part[step * base_docs : (step + 1) * base_docs]


def finish_kernel(scale_ref, *refs):
    parts, out_ref = refs[:-1], refs[-1]
    out_ref[...] = (scale_ref[...] * sum(ref[...] for ref in parts))[:, : out_ref.shape[1]]


def median_kernel(members, *refs):
    refs[-1][...] = middle([ref[...] for ref in refs[:members]])


def per_device(counts, tile_mask, member_topics, start_dict, align_perm, base_counts, base_topics):
    doc_size = lax.axis_size("doc")
    members = lax.axis_size("pert")
    cores = 2 - doc_size % 2
    chips = doc_size // cores
    at_pert = lax.axis_index("pert")
    at_doc = lax.axis_index("doc")
    at_chip, at_core = at_doc // cores, at_doc % cores
    docs = counts.shape[1]
    base_docs = base_counts.shape[0]
    topic_count = member_topics.shape[2]
    owned = start_dict.shape[1]
    span = cores * owned
    rows = chips * docs
    sub = owned // members

    def over_chips(array, step):
        return lax.ppermute(
            array,
            "doc",
            [
                (c * cores + k, (c ^ step) * cores + (k + step) % cores)
                for c in range(chips)
                for k in range(cores)
            ],
        )

    def over_cores(array):
        return lax.ppermute(array, "doc", [(d, d ^ 1) for d in range(doc_size)])

    def over_pert(array, step):
        return lax.ppermute(array, "pert", [(m, m ^ step) for m in range(members)])

    sent = pl.pallas_call(
        functools.partial(spread_kernel, chips, cores, owned),
        out_shape=[pltpu.VMEM((docs, span + 2 * topic_count), jnp.float32)] * chips,
        in_specs=[pl.BlockSpec(memory_space=pltpu.HBM)] * 4,
        out_specs=[pl.BlockSpec(memory_space=pltpu.VMEM)] * chips,
        scratch_shapes=[
            pltpu.VMEM(tile_mask.shape[1:], jnp.int32),
            pltpu.VMEM(member_topics.shape[1:], jnp.float32),
            pltpu.VMEM(align_perm.shape, jnp.int32),
            pltpu.VMEM((chips, docs, span), jnp.int32),
            pltpu.SemaphoreType.DMA((3,)),
            pltpu.SemaphoreType.DMA((chips,)),
        ],
        compiler_params=pltpu.CompilerParams(vmem_limit_bytes=VMEM_BYTES),
        cost_estimate=pl.CostEstimate(flops=0, bytes_accessed=12 * counts.size, transcendentals=0),
    )(*[pltpu.with_memory_space_constraint(x, pltpu.HBM) for x in (tile_mask[0], member_topics[0], align_perm, counts[0])])
    base_sent = call(
        functools.partial(base_kernel, chips, cores),
        [shape(base_docs, span + 2 * topic_count)] * chips,
        base_counts,
        base_topics,
        moved=8 * base_counts.size,
    )
    got = [over_chips(sent[step], step) for step in range(chips - 1, 0, -1)][::-1]
    payload = [sent[0]] + got
    near = [over_chips(base_sent[step], step) for step in range(1, min(chips, 2))]
    dict_own = start_dict[0].T
    halves = [dict_own] + [over_cores(dict_own)] * (cores - 1)
    wide, tall, col_part, dict_own = call(
        functools.partial(dictionary_kernel, cores),
        [
            shape(2 * topic_count, span, dtype=jnp.bfloat16),
            shape(span, 2 * topic_count, dtype=jnp.bfloat16),
            shape(8, 2 * topic_count),
            shape(topic_count, owned),
        ],
        align_perm,
        *halves,
        moved=4 * 4 * span * topic_count,
    )

    update_flops = 2 * 2 * 4 * rows * topic_count * span
    count_order = [chips - 1] + list(range(1, chips - 1)) + [0]
    topics, part, *weighted = call(
        functools.partial(first_kernel, chips, cores, count_order),
        [shape(rows, 2 * topic_count), shape(rows // 2 + 8, 2 * topic_count)]
        + [shape(rows, owned)] * cores,
        wide,
        tall,
        col_part,
        *[payload[step] for step in count_order],
        *near,
        unread=len(near),
        flops=update_flops,
        moved=4 * span * (rows + 2 * topic_count),
    )
    parts = [part] + [over_chips(part, step) for step in range(chips - 1, 0, -1)]
    crossed = [over_cores(weighted[1])] if cores > 1 else []
    totals = []
    for update in range(1, UPDATES):
        topics, *outs = call(
            functools.partial(update_kernel, chips),
            [shape(rows, 2 * topic_count)]
            + [shape(rows // 2 + (0 if totals else step - 1), 2 * topic_count) for step in range(1, chips)]
            + ([] if totals else [shape(8, 2 * topic_count)]),
            wide,
            tall,
            topics,
            *totals,
            *payload[::-1],
            *parts,
            flops=update_flops,
            moved=4 * span * (rows + 2 * topic_count),
        )
        totals = totals or outs[chips - 1 :]
        parts = [outs[0]] + [over_chips(outs[step - 1], step) for step in range(chips - 1, 0, -1)]
    (col_total,) = totals

    topics = call(
        functools.partial(topics_kernel, chips),
        shape(rows, 2 * topic_count),
        topics,
        col_total,
        *parts,
        *crossed,
        unread=len(crossed),
    )
    other = []
    if cores > 1:
        other_topics = over_cores(topics)
        other = [
            call(
                numerator_kernel,
                shape(topic_count, owned + 128),
                wide,
                topics,
                weighted[0],
                flops=update_flops // 2,
                moved=2 * span * (rows + 2 * topic_count),
            )
        ]
        topics, weighted = other_topics, crossed
    aligned = call(
        numerator_kernel,
        shape(topic_count, owned),
        wide,
        topics,
        weighted[0],
        dict_own,
        *other,
        flops=update_flops // 2,
        moved=2 * span * (rows + 2 * topic_count),
    )

    def words_of(array, member):
        return lax.dynamic_slice_in_dim(array, member * sub, sub, 1)

    aligned, base_sent = lax.optimization_barrier((aligned, base_sent))
    base_got = [over_chips(base_sent[step], step) for step in range(2, chips)]
    late = len(base_got) // 2
    base_got = base_got[::-1]
    median = call(
        functools.partial(median_kernel, members),
        pltpu.VMEM((topic_count, sub), jnp.float32),
        words_of(aligned, at_pert),
        *[over_pert(words_of(aligned, at_pert ^ step), step) for step in range(members - 1, 0, -1)],
        *base_got[late:],
        unread=len(base_got) - late,
    )
    pieces = [median] + [over_pert(median, step) for step in range(members - 1, 0, -1)]
    pieces[1], *base_got[:late] = lax.optimization_barrier((pieces[1], *base_got[:late]))
    median_halves = [pieces] + [[over_cores(piece) for piece in pieces]] * (cores - 1)
    base_all = [base_sent[0]] + near + base_got[::-1]

    base_rows = chips * base_docs
    refit_flops = 2 * 2 * 4 * base_rows * topic_count * owned
    forms, before = [], []
    for half in range(cores):
        wide, tall, part = call(
            functools.partial(refit_kernel, members, chips, half),
            [
                shape(2 * topic_count, owned, dtype=jnp.bfloat16),
                shape(owned, 2 * topic_count, dtype=jnp.bfloat16),
                shape(base_rows // 2 + 8, 2 * topic_count),
            ],
            *median_halves[half],
            *base_all,
            *before,
            flops=refit_flops,
            moved=16 * owned * topic_count,
            scratch=[pltpu.VMEM((topic_count, owned), jnp.float32)],
        )
        forms += [wide, tall]
        before = [part]
    scale, *parts = call(
        functools.partial(refit_again_kernel, chips, cores, base_docs),
        [shape(base_docs, 2 * topic_count)] * (chips + 1),
        *base_all,
        part,
        *[over_chips(part, step) for step in range(chips - 1, 0, -1)],
        *forms,
        flops=2 * refit_flops,
        moved=16 * owned * topic_count,
    )
    refit = call(
        finish_kernel,
        shape(base_docs, topic_count),
        scale,
        parts[0],
        *[over_chips(parts[step], step) for step in range(chips - 1, 0, -1)],
    )
    return (median.T[None, None], refit)


def solution(mesh):
    return jax.shard_map(
        per_device,
        mesh=mesh,
        in_specs=(
            P("pert", "doc", None),
            P("pert", "doc", None),
            P("pert", "doc", None),
            P("pert", "doc", None),
            P("pert", None),
            P(("pert", "doc"), None),
            P(("pert", "doc"), None),
        ),
        out_specs=(P("doc", "pert", None, None), P(("pert", "doc"), None)),
        check_vma=False,
    )
```

```python
import functools

import jax
import jax.numpy as jnp
from jax import lax
from jax.experimental import pallas as pl
from jax.experimental.pallas import tpu as pltpu
from jax.sharding import PartitionSpec as P

UPDATES = 3
REFITS = 2

EXACT = lax.Precision.HIGHEST
ROUGH = lax.Precision.HIGH
VMEM_BYTES = 14 * 1024 * 1024
SPREAD_BYTES = 60 * 1024 * 1024


def dot(left, right, dims, precision=ROUGH):
    return lax.dot_general(left, right, (dims, ((), ())), precision=precision)


def middle(pieces):
    pieces = list(pieces)
    count = len(pieces)
    for turn in range(count):
        for low in range(turn % 2, count - 1, 2):
            pieces[low], pieces[low + 1] = (
                jnp.minimum(pieces[low], pieces[low + 1]),
                jnp.maximum(pieces[low], pieces[low + 1]),
            )
    return 0.5 * (pieces[count // 2 - 1] + pieces[count // 2])


def call(kernel, outs, *args, flops=0, moved=0, unread=0, scratch=()):
    read = len(args) - unread
    return pl.pallas_call(
        kernel,
        out_shape=outs,
        in_specs=[pl.BlockSpec(memory_space=pltpu.VMEM)] * read
        + [pl.BlockSpec(memory_space=pl.ANY)] * unread,
        scratch_shapes=scratch,
        compiler_params=pltpu.CompilerParams(vmem_limit_bytes=VMEM_BYTES),
        cost_estimate=pl.CostEstimate(flops=flops, bytes_accessed=moved, transcendentals=0),
    )(*args)


def shape(*dims, dtype=jnp.float32):
    return jax.ShapeDtypeStruct(dims, dtype)


def high_low(x):
    high = x.astype(jnp.bfloat16).astype(jnp.float32)
    return high, x - high


def matmul(left, right):
    return jnp.dot(
        left.astype(jnp.bfloat16), right.astype(jnp.bfloat16), preferred_element_type=jnp.float32
    )


def blocks_of(chips, cores, step):
    at_doc = lax.axis_index("doc")
    at_chip, at_core = at_doc // cores, at_doc % cores
    return [(at_chip ^ step) * cores + (at_core ^ ((step + half) % cores)) for half in range(cores)]


def spread_kernel(chips, cores, own_words, mask_hbm, topics_hbm, perm_hbm, counts_hbm, *refs):
    out_refs, (mask_ref, topics_ref, perm_ref, counts_ref, small_sems, in_sems) = (
        refs[:chips],
        refs[chips:],
    )
    small = [
        pltpu.make_async_copy(mask_hbm, mask_ref, small_sems.at[0]),
        pltpu.make_async_copy(topics_hbm, topics_ref, small_sems.at[1]),
        pltpu.make_async_copy(perm_hbm, perm_ref, small_sems.at[2]),
    ]
    for copy in small:
        copy.start()
    steps = list(range(chips - 1, -1, -1))
    at_chip = lax.axis_index("doc") // cores
    arriving = {}
    for step in steps:
        first = (at_chip ^ step) * cores * own_words
        arriving[step] = pltpu.make_async_copy(
            counts_hbm.at[:, pl.ds(pl.multiple_of(first, 128), cores * own_words)],
            counts_ref.at[step],
            in_sems.at[step],
        )
        arriving[step].start()
    docs, tiles = mask_ref.shape
    width = chips * cores * own_words // tiles
    own_tiles = own_words // width
    tile_ids = lax.broadcasted_iota(jnp.int32, (docs, tiles), 1)
    doc_ids = lax.axis_index("doc") * docs + lax.broadcasted_iota(jnp.int32, (docs, tiles), 0)
    forced = (tile_ids == doc_ids % tiles).astype(jnp.int32)
    for copy in small:
        copy.wait()
    occupied = jnp.maximum(mask_ref[...], forced).astype(jnp.float32)
    topic_count = topics_ref.shape[1]
    onehot = lax.broadcasted_iota(jnp.int32, (topic_count, 2 * topic_count), 0) == jnp.concatenate(
        [perm_ref[...]] * 2, axis=1
    )
    topics = moved_columns(topics_ref[...], onehot.astype(jnp.float32))
    for step in steps:
        for half, block in enumerate(blocks_of(chips, cores, step)):
            near = pltpu.roll(occupied, lax.rem(tiles - block * own_tiles, tiles), 1)
            for tile in range(own_tiles):
                at = slice(half * own_words + tile * width, half * own_words + (tile + 1) * width)
                out_refs[step][:, at] = jnp.broadcast_to(near[:, tile : tile + 1], (docs, width))
        out_refs[step][:, cores * own_words :] = topics
    for step in steps:
        arriving[step].wait()
        for half, block in enumerate(blocks_of(chips, cores, step)):
            at = slice(half * own_words, (half + 1) * own_words)
            first = pl.multiple_of(lax.rem(block, cores) * own_words, 128)
            out_refs[step][:, at] *= counts_ref[step, :, pl.ds(first, own_words)].astype(jnp.float32)


def base_kernel(chips, cores, counts_ref, topics_ref, *out_refs):
    span = out_refs[0].shape[1] - 2 * topics_ref.shape[1]
    own_words = span // cores
    for step in range(chips):
        for half, block in enumerate(blocks_of(chips, cores, step)):
            at = slice(half * own_words, (half + 1) * own_words)
            first = pl.multiple_of(block * own_words, 128)
            out_refs[step][:, at] = counts_ref[:, pl.ds(first, own_words)].astype(jnp.float32)
        out_refs[step][:, span:] = jnp.concatenate([topics_ref[...]] * 2, axis=1)


def moved_columns(x, onehot):
    rows = x.shape[0]
    high, rest = high_low(x)
    mid, low = high_low(rest)
    moved = matmul(jnp.concatenate([high, mid, low], axis=0), onehot)
    return moved[:rows] + moved[rows : 2 * rows] + moved[2 * rows :]


def dictionary_kernel(half_count, perm_ref, *refs):
    topics, words = refs[0].shape
    wide_ref, tall_ref, total_ref, own_ref = refs[half_count:]
    turned_onehot = (
        (lax.broadcasted_iota(jnp.int32, (topics, topics), 0) == perm_ref[...]).astype(jnp.float32).T
    )
    total = jnp.zeros((1, 2 * topics), jnp.float32)
    for half in range(half_count):
        at = slice(half * words, (half + 1) * words)
        high, rest = high_low(refs[half][...])
        mid, low = high_low(rest)
        aligned = matmul(
            jnp.concatenate([turned_onehot] * 3, axis=1), jnp.concatenate([high, mid, low], axis=0)
        )
        if half == 0:
            own_ref[...] = aligned
        wide = jnp.concatenate(high_low(aligned), axis=0)
        wide_ref[:, at] = wide.astype(jnp.bfloat16)
        tall = wide.T
        total += jnp.sum(tall, axis=0, keepdims=True)
        tall_ref[at, :] = tall.astype(jnp.bfloat16)
    total_ref[...] = jnp.broadcast_to(total + turned(total), total_ref.shape)


def recon_of(doubled, wide):
    rows = doubled.shape[0]
    both = matmul(jnp.concatenate(high_low(doubled), axis=0), wide)
    return both[:rows] + both[rows:]


def product_of(quotient, tall, ones=0):
    rows = quotient.shape[0]
    left = [*high_low(quotient)] + [jnp.ones((ones, quotient.shape[1]), jnp.float32)] * (ones > 0)
    both = matmul(jnp.concatenate(left, axis=0), tall)
    both = [both[:rows] + both[rows : 2 * rows], both[2 * rows :]]
    both = jnp.concatenate(both, axis=0) if ones else both[0]
    return both + turned(both)


def turned(x):
    return pltpu.roll(x, x.shape[1] // 2, 1)


def left_half(x):
    return lax.broadcasted_iota(jnp.int32, x.shape, 1) < x.shape[1] // 2


def pack(doubled):
    half = doubled.shape[0] // 2
    lower, upper = doubled[:half], doubled[half:]
    return jnp.where(left_half(lower), lower, upper)


def sum_packed(chips, parts):
    parts = [parts[0], *parts[:0:-1]]
    side = max(chips // 2, 1)
    rows = parts[0].shape[0] // side

    def moved(x, step):
        if step == 0:
            return x
        return jnp.concatenate([x[(c ^ step) * rows : ((c ^ step) + 1) * rows] for c in range(side)], axis=0)

    sums = []
    for first in range(0, chips, side):
        sums.append(sum(moved(parts[step], step - first) for step in range(first, first + side)))
    packed, other = sums[0] + turned(sums[1]), turned(sums[0]) + sums[1]
    left = left_half(packed)
    return jnp.concatenate([jnp.where(left, packed, other), jnp.where(left, other, packed)], axis=0)


def write_parts(refs, part):
    rows = part.shape[0]
    for ref in refs:
        ref[:rows] = part
        if ref.shape[0] > rows:
            ref[rows:] = jnp.zeros((ref.shape[0] - rows, part.shape[1]), part.dtype)


def first_kernel(chips, cores, order, wide_ref, tall_ref, col_part_ref, *refs):
    payload = [refs[order.index(step)] for step in range(chips)]
    topics_ref, part_ref, *half_refs = refs[-2 - cores :]
    span = wide_ref.shape[1]
    topics = jnp.concatenate([ref[:, span:] for ref in payload], axis=0)
    topics_ref[...] = topics
    weighted = jnp.concatenate([ref[:, :span] for ref in payload], axis=0)
    part = pack(product_of(weighted / recon_of(topics, wide_ref[...]), tall_ref[...]))
    part_ref[: part.shape[0]] = part
    part_ref[part.shape[0] :] = col_part_ref[:1]
    words = span // cores
    for half, ref in enumerate(half_refs):
        ref[...] = weighted[:, half * words : (half + 1) * words]


def update_kernel(chips, wide_ref, tall_ref, before_ref, *refs):
    packed = before_ref.shape[0] // 2
    if refs[-1].shape[0] == 8:
        payload, parts = refs[:chips][::-1], refs[chips : 2 * chips]
        topics_ref, *part_refs, total_ref = refs[2 * chips :]
        total = sum(ref[packed : packed + 1] for ref in parts)
        total_ref[...] = jnp.broadcast_to(total, total_ref.shape)
    else:
        total_ref, payload, parts = refs[0], refs[1 : chips + 1][::-1], refs[chips + 1 : 2 * chips + 1]
        topics_ref, *part_refs = refs[2 * chips + 1 :]
    span = wide_ref.shape[1]
    total = sum_packed(chips, [ref[:packed] for ref in parts])
    topics = before_ref[...] / total_ref[:1] * total
    topics_ref[...] = topics
    weighted = jnp.concatenate([ref[:, :span] for ref in payload], axis=0)
    write_parts(part_refs, pack(product_of(weighted / recon_of(topics, wide_ref[...]), tall_ref[...])))


def numerator_of(topics, quotient):
    high, low = high_low(topics.T[: topics.shape[1] // 2])
    quotient_high, quotient_low = high_low(quotient)
    return matmul(
        jnp.concatenate([high, low, high], axis=1),
        jnp.concatenate([quotient_high, quotient_high, quotient_low], axis=0),
    )


def topics_kernel(chips, before_ref, total_ref, *refs):
    parts, topics_ref = refs[:chips], refs[-1]
    total = sum_packed(chips, [ref[: before_ref.shape[0] // 2] for ref in parts])
    topics_ref[...] = before_ref[...] / total_ref[:1] * total


def numerator_kernel(wide_ref, topics_ref, weighted_ref, *refs):
    before, out_ref = refs[:-1], refs[-1]
    words = weighted_ref.shape[1]
    topics = topics_ref[...]
    load = jnp.sum(topics.T[: topics.shape[1] // 2], axis=1, keepdims=True)
    numerator = numerator_of(topics, weighted_ref[...] / recon_of(topics, wide_ref[:, :words]))
    if out_ref.shape[1] > words:
        out_ref[:, :words] = numerator
        out_ref[:, words:] = jnp.broadcast_to(load, (load.shape[0], out_ref.shape[1] - words))
    else:
        dict_ref, *other = before
        for ref in other:
            numerator = numerator + ref[:, :words]
            load = load + ref[:, words : words + 1]
        out_ref[...] = dict_ref[...] / load * numerator


def base_rows_of(refs, at):
    return jnp.concatenate([ref[:, at] for ref in refs], axis=0)


def refit_kernel(members, chips, half, *refs):
    pieces, payload = refs[:members], refs[members : members + chips]
    *before, wide_ref, tall_ref, part_ref, median_ref = refs[members + chips :]
    sub = pieces[0].shape[1]
    for me in range(members):

        @pl.when(lax.axis_index("pert") == me)
        def _():
            for at in range(members):
                owner = me ^ ((members - at) % members)
                median_ref[:, owner * sub : (owner + 1) * sub] = pieces[at][...]

    words = median_ref.shape[1]
    span = payload[0].shape[1] - part_ref.shape[1]
    wide = jnp.concatenate(high_low(median_ref[...]), axis=0)
    tall = wide.T.astype(jnp.bfloat16)
    wide = wide.astype(jnp.bfloat16)
    wide_ref[...] = wide
    tall_ref[...] = tall
    weighted = base_rows_of(payload, slice(half * words, (half + 1) * words))
    refit = base_rows_of(payload, slice(span, None))
    both = product_of(weighted / recon_of(refit, wide), tall, ones=8)
    both = jnp.concatenate([pack(both[:-8]), both[-8:]], axis=0)
    part_ref[...] = both + before[0][...] if before else both


def refit_again_kernel(chips, cores, base_docs, *refs):
    payload, parts, halves = refs[:chips], refs[chips : 2 * chips], refs[2 * chips : 2 * (chips + cores)]
    scale_ref, *part_refs = refs[2 * (chips + cores) :]
    packed = chips * base_docs // 2
    span = payload[0].shape[1] - scale_ref.shape[1]
    words = span // cores
    median_total = sum(ref[packed : packed + 1] for ref in parts)
    total = sum_packed(chips, [ref[:packed] for ref in parts])
    refit = base_rows_of(payload, slice(span, None)) / median_total * total
    scale_ref[...] = refit[:base_docs] / median_total
    part = None
    for half in range(cores):
        weighted = base_rows_of(payload, slice(half * words, (half + 1) * words))
        wide_ref, tall_ref = halves[2 * half], halves[2 * half + 1]
        new = product_of(weighted / recon_of(refit, wide_ref[...]), tall_ref[...])
        part = new if part is None else part + new
    for step in range(chips):
        part_refs[step][...] = part[step * base_docs : (step + 1) * base_docs]


def finish_kernel(scale_ref, *refs):
    parts, out_ref = refs[:-1], refs[-1]
    out_ref[...] = (scale_ref[...] * sum(ref[...] for ref in parts))[:, : out_ref.shape[1]]


def median_kernel(members, *refs):
    refs[-1][...] = middle([ref[...] for ref in refs[:members]])


def per_device(counts, tile_mask, member_topics, start_dict, align_perm, base_counts, base_topics):
    doc_size = lax.axis_size("doc")
    members = lax.axis_size("pert")
    cores = 2 - doc_size % 2
    chips = doc_size // cores
    at_pert = lax.axis_index("pert")
    at_doc = lax.axis_index("doc")
    at_chip, at_core = at_doc // cores, at_doc % cores
    docs = counts.shape[1]
    base_docs = base_counts.shape[0]
    topic_count = member_topics.shape[2]
    owned = start_dict.shape[1]
    span = cores * owned
    rows = chips * docs
    sub = owned // members

    def over_chips(array, step):
        return lax.ppermute(
            array,
            "doc",
            [
                (c * cores + k, (c ^ step) * cores + (k + step) % cores)
                for c in range(chips)
                for k in range(cores)
            ],
        )

    def over_cores(array):
        return lax.ppermute(array, "doc", [(d, d ^ 1) for d in range(doc_size)])

    def over_pert(array, step):
        return lax.ppermute(array, "pert", [(m, m ^ step) for m in range(members)])

    sent = pl.pallas_call(
        functools.partial(spread_kernel, chips, cores, owned),
        out_shape=[pltpu.VMEM((docs, span + 2 * topic_count), jnp.float32)] * chips,
        in_specs=[pl.BlockSpec(memory_space=pltpu.HBM)] * 4,
        out_specs=[pl.BlockSpec(memory_space=pltpu.VMEM)] * chips,
        scratch_shapes=[
            pltpu.VMEM(tile_mask.shape[1:], jnp.int32),
            pltpu.VMEM(member_topics.shape[1:], jnp.float32),
            pltpu.VMEM(align_perm.shape, jnp.int32),
            pltpu.VMEM((chips, docs, span), jnp.int32),
            pltpu.SemaphoreType.DMA((3,)),
            pltpu.SemaphoreType.DMA((chips,)),
        ],
        compiler_params=pltpu.CompilerParams(vmem_limit_bytes=VMEM_BYTES),
        cost_estimate=pl.CostEstimate(flops=0, bytes_accessed=12 * counts.size, transcendentals=0),
    )(*[pltpu.with_memory_space_constraint(x, pltpu.HBM) for x in (tile_mask[0], member_topics[0], align_perm, counts[0])])
    base_sent = call(
        functools.partial(base_kernel, chips, cores),
        [shape(base_docs, span + 2 * topic_count)] * chips,
        base_counts,
        base_topics,
        moved=8 * base_counts.size,
    )
    got = [over_chips(sent[step], step) for step in range(chips - 1, 0, -1)][::-1]
    payload = [sent[0]] + got
    near = [over_chips(base_sent[step], step) for step in range(1, min(chips, 2))]
    dict_own = start_dict[0].T
    halves = [dict_own] + [over_cores(dict_own)] * (cores - 1)
    wide, tall, col_part, dict_own = call(
        functools.partial(dictionary_kernel, cores),
        [
            shape(2 * topic_count, span, dtype=jnp.bfloat16),
            shape(span, 2 * topic_count, dtype=jnp.bfloat16),
            shape(8, 2 * topic_count),
            shape(topic_count, owned),
        ],
        align_perm,
        *halves,
        moved=4 * 4 * span * topic_count,
    )

    update_flops = 2 * 2 * 4 * rows * topic_count * span
    count_order = [chips - 1] + list(range(1, chips - 1)) + [0]
    topics, part, *weighted = call(
        functools.partial(first_kernel, chips, cores, count_order),
        [shape(rows, 2 * topic_count), shape(rows // 2 + 1, 2 * topic_count)]
        + [shape(rows, owned)] * cores,
        wide,
        tall,
        col_part,
        *[payload[step] for step in count_order],
        *near,
        unread=len(near),
        flops=update_flops,
        moved=4 * span * (rows + 2 * topic_count),
    )
    parts = [part] + [over_chips(part, step) for step in range(chips - 1, 0, -1)]
    crossed = []
    totals = []
    for update in range(1, UPDATES):
        topics, *outs = call(
            functools.partial(update_kernel, chips),
            [shape(rows, 2 * topic_count)]
            + [shape(rows // 2 + (0 if totals else step - 1), 2 * topic_count) for step in range(1, chips)]
            + ([] if totals else [shape(8, 2 * topic_count)]),
            wide,
            tall,
            topics,
            *totals,
            *payload[::-1],
            *parts,
            flops=update_flops,
            moved=4 * span * (rows + 2 * topic_count),
        )
        totals = totals or outs[chips - 1 :]
        if update == 1 and cores > 1:
            topics, weighted[1] = lax.optimization_barrier((topics, weighted[1]))
            crossed = [over_cores(weighted[1])]
        parts = [outs[0]] + [over_chips(outs[step - 1], step) for step in range(chips - 1, 0, -1)]
    (col_total,) = totals

    topics = call(
        functools.partial(topics_kernel, chips),
        shape(rows, 2 * topic_count),
        topics,
        col_total,
        *parts,
        *crossed,
        unread=len(crossed),
    )
    other = []
    if cores > 1:
        other_topics = over_cores(topics)
        other = [
            call(
                numerator_kernel,
                shape(topic_count, owned + 128),
                wide,
                topics,
                weighted[0],
                flops=update_flops // 2,
                moved=2 * span * (rows + 2 * topic_count),
            )
        ]
        topics, weighted = other_topics, crossed
    aligned = call(
        numerator_kernel,
        shape(topic_count, owned),
        wide,
        topics,
        weighted[0],
        dict_own,
        *other,
        flops=update_flops // 2,
        moved=2 * span * (rows + 2 * topic_count),
    )

    def words_of(array, member):
        return lax.dynamic_slice_in_dim(array, member * sub, sub, 1)

    aligned, base_sent = lax.optimization_barrier((aligned, base_sent))
    base_got = [over_chips(base_sent[step], step) for step in range(2, chips)]
    late = len(base_got) // 2
    base_got = base_got[::-1]
    median = call(
        functools.partial(median_kernel, members),
        pltpu.VMEM((topic_count, sub), jnp.float32),
        words_of(aligned, at_pert),
        *[over_pert(words_of(aligned, at_pert ^ step), step) for step in range(members - 1, 0, -1)],
        *base_got[late:],
        unread=len(base_got) - late,
    )
    pieces = [median] + [over_pert(median, step) for step in range(members - 1, 0, -1)]
    pieces[1], *base_got[:late] = lax.optimization_barrier((pieces[1], *base_got[:late]))
    median_halves = [pieces] + [[over_cores(piece) for piece in pieces]] * (cores - 1)
    base_all = [base_sent[0]] + near + base_got[::-1]

    base_rows = chips * base_docs
    refit_flops = 2 * 2 * 4 * base_rows * topic_count * owned
    forms, before = [], []
    for half in range(cores):
        wide, tall, part = call(
            functools.partial(refit_kernel, members, chips, half),
            [
                shape(2 * topic_count, owned, dtype=jnp.bfloat16),
                shape(owned, 2 * topic_count, dtype=jnp.bfloat16),
                shape(base_rows // 2 + 8, 2 * topic_count),
            ],
            *median_halves[half],
            *base_all,
            *before,
            flops=refit_flops,
            moved=16 * owned * topic_count,
            scratch=[pltpu.VMEM((topic_count, owned), jnp.float32)],
        )
        forms += [wide, tall]
        before = [part]
    scale, *parts = call(
        functools.partial(refit_again_kernel, chips, cores, base_docs),
        [shape(base_docs, 2 * topic_count)] * (chips + 1),
        *base_all,
        part,
        *[over_chips(part, step) for step in range(chips - 1, 0, -1)],
        *forms,
        flops=2 * refit_flops,
        moved=16 * owned * topic_count,
    )
    refit = call(
        finish_kernel,
        shape(base_docs, topic_count),
        scale,
        parts[0],
        *[over_chips(parts[step], step) for step in range(chips - 1, 0, -1)],
    )
    return (median.T[None, None], refit)


def solution(mesh):
    return jax.shard_map(
        per_device,
        mesh=mesh,
        in_specs=(
            P("pert", "doc", None),
            P("pert", "doc", None),
            P("pert", "doc", None),
            P("pert", "doc", None),
            P("pert", None),
            P(("pert", "doc"), None),
            P(("pert", "doc"), None),
        ),
        out_specs=(P("doc", "pert", None, None), P(("pert", "doc"), None)),
        check_vma=False,
    )
```

```python
import functools

import jax
import jax.numpy as jnp
from jax import lax
from jax.experimental import pallas as pl
from jax.experimental.pallas import tpu as pltpu
from jax.sharding import PartitionSpec as P

UPDATES = 3
REFITS = 2

EXACT = lax.Precision.HIGHEST
ROUGH = lax.Precision.HIGH
VMEM_BYTES = 14 * 1024 * 1024
SPREAD_BYTES = 60 * 1024 * 1024


def dot(left, right, dims, precision=ROUGH):
    return lax.dot_general(left, right, (dims, ((), ())), precision=precision)


def middle(pieces):
    pieces = list(pieces)
    count = len(pieces)
    for turn in range(count):
        for low in range(turn % 2, count - 1, 2):
            pieces[low], pieces[low + 1] = (
                jnp.minimum(pieces[low], pieces[low + 1]),
                jnp.maximum(pieces[low], pieces[low + 1]),
            )
    return 0.5 * (pieces[count // 2 - 1] + pieces[count // 2])


def call(kernel, outs, *args, flops=0, moved=0, unread=0, scratch=()):
    read = len(args) - unread
    return pl.pallas_call(
        kernel,
        out_shape=outs,
        in_specs=[pl.BlockSpec(memory_space=pltpu.VMEM)] * read
        + [pl.BlockSpec(memory_space=pl.ANY)] * unread,
        scratch_shapes=scratch,
        compiler_params=pltpu.CompilerParams(vmem_limit_bytes=VMEM_BYTES),
        cost_estimate=pl.CostEstimate(flops=flops, bytes_accessed=moved, transcendentals=0),
    )(*args)


def shape(*dims, dtype=jnp.float32):
    return jax.ShapeDtypeStruct(dims, dtype)


def high_low(x):
    high = x.astype(jnp.bfloat16).astype(jnp.float32)
    return high, x - high


def matmul(left, right):
    return jnp.dot(
        left.astype(jnp.bfloat16), right.astype(jnp.bfloat16), preferred_element_type=jnp.float32
    )


def blocks_of(chips, cores, step):
    at_doc = lax.axis_index("doc")
    at_chip, at_core = at_doc // cores, at_doc % cores
    return [(at_chip ^ step) * cores + (at_core ^ ((step + half) % cores)) for half in range(cores)]


def spread_kernel(chips, cores, own_words, mask_hbm, topics_hbm, perm_hbm, counts_hbm, *refs):
    out_refs, (mask_ref, topics_ref, perm_ref, counts_ref, small_sems, in_sems) = (
        refs[:chips],
        refs[chips:],
    )
    small = [
        pltpu.make_async_copy(mask_hbm, mask_ref, small_sems.at[0]),
        pltpu.make_async_copy(topics_hbm, topics_ref, small_sems.at[1]),
        pltpu.make_async_copy(perm_hbm, perm_ref, small_sems.at[2]),
    ]
    for copy in small:
        copy.start()
    steps = list(range(chips - 1, -1, -1))
    at_chip = lax.axis_index("doc") // cores
    arriving = {}
    for step in steps:
        first = (at_chip ^ step) * cores * own_words
        arriving[step] = pltpu.make_async_copy(
            counts_hbm.at[:, pl.ds(pl.multiple_of(first, 128), cores * own_words)],
            counts_ref.at[step],
            in_sems.at[step],
        )
        arriving[step].start()
    docs, tiles = mask_ref.shape
    width = chips * cores * own_words // tiles
    own_tiles = own_words // width
    tile_ids = lax.broadcasted_iota(jnp.int32, (docs, tiles), 1)
    doc_ids = lax.axis_index("doc") * docs + lax.broadcasted_iota(jnp.int32, (docs, tiles), 0)
    forced = (tile_ids == doc_ids % tiles).astype(jnp.int32)
    for copy in small:
        copy.wait()
    occupied = jnp.maximum(mask_ref[...], forced).astype(jnp.float32)
    topic_count = topics_ref.shape[1]
    onehot = lax.broadcasted_iota(jnp.int32, (topic_count, 2 * topic_count), 0) == jnp.concatenate(
        [perm_ref[...]] * 2, axis=1
    )
    topics = moved_columns(topics_ref[...], onehot.astype(jnp.float32))
    for step in steps:
        for half, block in enumerate(blocks_of(chips, cores, step)):
            near = pltpu.roll(occupied, lax.rem(tiles - block * own_tiles, tiles), 1)
            for tile in range(own_tiles):
                at = slice(half * own_words + tile * width, half * own_words + (tile + 1) * width)
                out_refs[step][:, at] = jnp.broadcast_to(near[:, tile : tile + 1], (docs, width))
        out_refs[step][:, cores * own_words :] = topics
    for step in steps:
        arriving[step].wait()
        for half, block in enumerate(blocks_of(chips, cores, step)):
            at = slice(half * own_words, (half + 1) * own_words)
            first = pl.multiple_of(lax.rem(block, cores) * own_words, 128)
            out_refs[step][:, at] *= counts_ref[step, :, pl.ds(first, own_words)].astype(jnp.float32)


def base_kernel(chips, cores, counts_ref, topics_ref, *out_refs):
    span = out_refs[0].shape[1] - 2 * topics_ref.shape[1]
    own_words = span // cores
    for step in range(chips):
        for half, block in enumerate(blocks_of(chips, cores, step)):
            at = slice(half * own_words, (half + 1) * own_words)
            first = pl.multiple_of(block * own_words, 128)
            out_refs[step][:, at] = counts_ref[:, pl.ds(first, own_words)].astype(jnp.float32)
        out_refs[step][:, span:] = jnp.concatenate([topics_ref[...]] * 2, axis=1)


def moved_columns(x, onehot):
    rows = x.shape[0]
    high, rest = high_low(x)
    mid, low = high_low(rest)
    moved = matmul(jnp.concatenate([high, mid, low], axis=0), onehot)
    return moved[:rows] + moved[rows : 2 * rows] + moved[2 * rows :]


def dictionary_kernel(half_count, perm_ref, *refs):
    topics, words = refs[0].shape
    wide_ref, tall_ref, total_ref, own_ref = refs[half_count:]
    turned_onehot = (
        (lax.broadcasted_iota(jnp.int32, (topics, topics), 0) == perm_ref[...]).astype(jnp.float32).T
    )
    total = jnp.zeros((1, 2 * topics), jnp.float32)
    for half in range(half_count):
        at = slice(half * words, (half + 1) * words)
        high, rest = high_low(refs[half][...])
        mid, low = high_low(rest)
        aligned = matmul(
            jnp.concatenate([turned_onehot] * 3, axis=1), jnp.concatenate([high, mid, low], axis=0)
        )
        if half == 0:
            own_ref[...] = aligned
        wide = jnp.concatenate(high_low(aligned), axis=0)
        wide_ref[:, at] = wide.astype(jnp.bfloat16)
        tall = wide.T
        total += jnp.sum(tall, axis=0, keepdims=True)
        tall_ref[at, :] = tall.astype(jnp.bfloat16)
    total_ref[...] = jnp.broadcast_to(total + turned(total), total_ref.shape)


def recon_of(doubled, wide):
    rows = doubled.shape[0]
    both = matmul(jnp.concatenate(high_low(doubled), axis=0), wide)
    return both[:rows] + both[rows:]


def product_of(quotient, tall, ones=0):
    rows = quotient.shape[0]
    left = [*high_low(quotient)] + [jnp.ones((ones, quotient.shape[1]), jnp.float32)] * (ones > 0)
    both = matmul(jnp.concatenate(left, axis=0), tall)
    both = [both[:rows] + both[rows : 2 * rows], both[2 * rows :]]
    both = jnp.concatenate(both, axis=0) if ones else both[0]
    return both + turned(both)


def turned(x):
    return pltpu.roll(x, x.shape[1] // 2, 1)


def left_half(x):
    return lax.broadcasted_iota(jnp.int32, x.shape, 1) < x.shape[1] // 2


def pack(doubled):
    half = doubled.shape[0] // 2
    lower, upper = doubled[:half], doubled[half:]
    return jnp.where(left_half(lower), lower, upper)


def sum_packed(chips, parts):
    parts = [parts[0], *parts[:0:-1]]
    side = max(chips // 2, 1)
    rows = parts[0].shape[0] // side

    def moved(x, step):
        if step == 0:
            return x
        return jnp.concatenate([x[(c ^ step) * rows : ((c ^ step) + 1) * rows] for c in range(side)], axis=0)

    sums = []
    for first in range(0, chips, side):
        sums.append(sum(moved(parts[step], step - first) for step in range(first, first + side)))
    packed, other = sums[0] + turned(sums[1]), turned(sums[0]) + sums[1]
    left = left_half(packed)
    return jnp.concatenate([jnp.where(left, packed, other), jnp.where(left, other, packed)], axis=0)


def write_parts(refs, part):
    rows = part.shape[0]
    for ref in refs:
        ref[:rows] = part
        if ref.shape[0] > rows:
            ref[rows:] = jnp.zeros((ref.shape[0] - rows, part.shape[1]), part.dtype)


def first_kernel(chips, cores, order, wide_ref, tall_ref, col_part_ref, *refs):
    payload = [refs[order.index(step)] for step in range(chips)]
    topics_ref, part_ref, *half_refs = refs[-2 - cores :]
    span = wide_ref.shape[1]
    topics = jnp.concatenate([ref[:, span:] for ref in payload], axis=0)
    topics_ref[...] = topics
    weighted = jnp.concatenate([ref[:, :span] for ref in payload], axis=0)
    part = pack(product_of(weighted / recon_of(topics, wide_ref[...]), tall_ref[...]))
    part_ref[: part.shape[0]] = part
    part_ref[part.shape[0] :] = col_part_ref[...]
    words = span // cores
    for half, ref in enumerate(half_refs):
        ref[...] = weighted[:, half * words : (half + 1) * words]


def update_kernel(chips, wide_ref, tall_ref, before_ref, *refs):
    packed = before_ref.shape[0] // 2
    if refs[-1].shape[0] == 8:
        payload, parts = refs[:chips][::-1], refs[chips : 2 * chips]
        topics_ref, *part_refs, total_ref = refs[2 * chips :]
        total_ref[...] = sum(ref[packed:] for ref in parts)
    else:
        total_ref, payload, parts = refs[0], refs[1 : chips + 1][::-1], refs[chips + 1 : 2 * chips + 1]
        topics_ref, *part_refs = refs[2 * chips + 1 :]
    span = wide_ref.shape[1]
    total = sum_packed(chips, [ref[:packed] for ref in parts])
    topics = before_ref[...] / total_ref[:1] * total
    topics_ref[...] = topics
    weighted = jnp.concatenate([ref[:, :span] for ref in payload], axis=0)
    write_parts(part_refs, pack(product_of(weighted / recon_of(topics, wide_ref[...]), tall_ref[...])))


def numerator_of(topics, quotient):
    high, low = high_low(topics.T[: topics.shape[1] // 2])
    quotient_high, quotient_low = high_low(quotient)
    return matmul(
        jnp.concatenate([high, low, high], axis=1),
        jnp.concatenate([quotient_high, quotient_high, quotient_low], axis=0),
    )


def topics_kernel(chips, before_ref, total_ref, *refs):
    parts, topics_ref = refs[:chips], refs[-1]
    total = sum_packed(chips, [ref[: before_ref.shape[0] // 2] for ref in parts])
    topics_ref[...] = before_ref[...] / total_ref[:1] * total


def numerator_kernel(wide_ref, topics_ref, weighted_ref, *refs):
    before, out_ref = refs[:-1], refs[-1]
    words = weighted_ref.shape[1]
    topics = topics_ref[...]
    load = jnp.sum(topics.T[: topics.shape[1] // 2], axis=1, keepdims=True)
    numerator = numerator_of(topics, weighted_ref[...] / recon_of(topics, wide_ref[:, :words]))
    if out_ref.shape[1] > words:
        out_ref[:, :words] = numerator
        out_ref[:, words:] = jnp.broadcast_to(load, (load.shape[0], out_ref.shape[1] - words))
    else:
        dict_ref, *other = before
        for ref in other:
            numerator = numerator + ref[:, :words]
            load = load + ref[:, words : words + 1]
        out_ref[...] = dict_ref[...] / load * numerator


def base_rows_of(refs, at):
    return jnp.concatenate([ref[:, at] for ref in refs], axis=0)


def refit_kernel(members, chips, half, *refs):
    pieces, payload = refs[:members], refs[members : members + chips]
    *before, wide_ref, tall_ref, part_ref, median_ref = refs[members + chips :]
    sub = pieces[0].shape[1]
    for me in range(members):

        @pl.when(lax.axis_index("pert") == me)
        def _():
            for at in range(members):
                owner = me ^ ((members - at) % members)
                median_ref[:, owner * sub : (owner + 1) * sub] = pieces[at][...]

    words = median_ref.shape[1]
    span = payload[0].shape[1] - part_ref.shape[1]
    wide = jnp.concatenate(high_low(median_ref[...]), axis=0)
    tall = wide.T.astype(jnp.bfloat16)
    wide = wide.astype(jnp.bfloat16)
    wide_ref[...] = wide
    tall_ref[...] = tall
    weighted = base_rows_of(payload, slice(half * words, (half + 1) * words))
    refit = base_rows_of(payload, slice(span, None))
    both = product_of(weighted / recon_of(refit, wide), tall, ones=8)
    both = jnp.concatenate([pack(both[:-8]), both[-8:]], axis=0)
    part_ref[...] = both + before[0][...] if before else both


def refit_again_kernel(chips, cores, base_docs, *refs):
    payload, parts, halves = refs[:chips], refs[chips : 2 * chips], refs[2 * chips : 2 * (chips + cores)]
    scale_ref, *part_refs = refs[2 * (chips + cores) :]
    packed = chips * base_docs // 2
    span = payload[0].shape[1] - scale_ref.shape[1]
    words = span // cores
    median_total = sum(ref[packed : packed + 1] for ref in parts)
    total = sum_packed(chips, [ref[:packed] for ref in parts])
    refit = base_rows_of(payload, slice(span, None)) / median_total * total
    scale_ref[...] = refit[:base_docs] / median_total
    wide = jnp.concatenate([ref[...] for ref in halves[0::2]], axis=1)
    tall = jnp.concatenate([ref[...] for ref in halves[1::2]], axis=0)
    weighted = base_rows_of(payload, slice(0, cores * words))
    part = product_of(weighted / recon_of(refit, wide), tall)
    for step in range(chips):
        part_refs[step][...] = part[step * base_docs : (step + 1) * base_docs]


def finish_kernel(scale_ref, *refs):
    parts, out_ref = refs[:-1], refs[-1]
    out_ref[...] = (scale_ref[...] * sum(ref[...] for ref in parts))[:, : out_ref.shape[1]]


def median_kernel(members, *refs):
    refs[-1][...] = middle([ref[...] for ref in refs[:members]])


def per_device(counts, tile_mask, member_topics, start_dict, align_perm, base_counts, base_topics):
    doc_size = lax.axis_size("doc")
    members = lax.axis_size("pert")
    cores = 2 - doc_size % 2
    chips = doc_size // cores
    at_pert = lax.axis_index("pert")
    at_doc = lax.axis_index("doc")
    at_chip, at_core = at_doc // cores, at_doc % cores
    docs = counts.shape[1]
    base_docs = base_counts.shape[0]
    topic_count = member_topics.shape[2]
    owned = start_dict.shape[1]
    span = cores * owned
    rows = chips * docs
    sub = owned // members

    def over_chips(array, step):
        return lax.ppermute(
            array,
            "doc",
            [
                (c * cores + k, (c ^ step) * cores + (k + step) % cores)
                for c in range(chips)
                for k in range(cores)
            ],
        )

    def over_cores(array):
        return lax.ppermute(array, "doc", [(d, d ^ 1) for d in range(doc_size)])

    def over_pert(array, step):
        return lax.ppermute(array, "pert", [(m, m ^ step) for m in range(members)])

    sent = pl.pallas_call(
        functools.partial(spread_kernel, chips, cores, owned),
        out_shape=[pltpu.VMEM((docs, span + 2 * topic_count), jnp.float32)] * chips,
        in_specs=[pl.BlockSpec(memory_space=pltpu.HBM)] * 4,
        out_specs=[pl.BlockSpec(memory_space=pltpu.VMEM)] * chips,
        scratch_shapes=[
            pltpu.VMEM(tile_mask.shape[1:], jnp.int32),
            pltpu.VMEM(member_topics.shape[1:], jnp.float32),
            pltpu.VMEM(align_perm.shape, jnp.int32),
            pltpu.VMEM((chips, docs, span), jnp.int32),
            pltpu.SemaphoreType.DMA((3,)),
            pltpu.SemaphoreType.DMA((chips,)),
        ],
        compiler_params=pltpu.CompilerParams(vmem_limit_bytes=VMEM_BYTES),
        cost_estimate=pl.CostEstimate(flops=0, bytes_accessed=12 * counts.size, transcendentals=0),
    )(*[pltpu.with_memory_space_constraint(x, pltpu.HBM) for x in (tile_mask[0], member_topics[0], align_perm, counts[0])])
    base_sent = call(
        functools.partial(base_kernel, chips, cores),
        [shape(base_docs, span + 2 * topic_count)] * chips,
        base_counts,
        base_topics,
        moved=8 * base_counts.size,
    )
    got = [over_chips(sent[step], step) for step in range(chips - 1, 0, -1)][::-1]
    payload = [sent[0]] + got
    near = [over_chips(base_sent[step], step) for step in range(1, min(chips, 2))]
    dict_own = start_dict[0].T
    halves = [dict_own] + [over_cores(dict_own)] * (cores - 1)
    wide, tall, col_part, dict_own = call(
        functools.partial(dictionary_kernel, cores),
        [
            shape(2 * topic_count, span, dtype=jnp.bfloat16),
            shape(span, 2 * topic_count, dtype=jnp.bfloat16),
            shape(8, 2 * topic_count),
            shape(topic_count, owned),
        ],
        align_perm,
        *halves,
        moved=4 * 4 * span * topic_count,
    )

    update_flops = 2 * 2 * 4 * rows * topic_count * span
    count_order = [chips - 1] + list(range(1, chips - 1)) + [0]
    topics, part, *weighted = call(
        functools.partial(first_kernel, chips, cores, count_order),
        [shape(rows, 2 * topic_count), shape(rows // 2 + 8, 2 * topic_count)]
        + [shape(rows, owned)] * cores,
        wide,
        tall,
        col_part,
        *[payload[step] for step in count_order],
        *near,
        unread=len(near),
        flops=update_flops,
        moved=4 * span * (rows + 2 * topic_count),
    )
    parts = [part] + [over_chips(part, step) for step in range(chips - 1, 0, -1)]
    crossed = [over_cores(weighted[1])] if cores > 1 else []
    totals = []
    for update in range(1, UPDATES):
        topics, *outs = call(
            functools.partial(update_kernel, chips),
            [shape(rows, 2 * topic_count)]
            + [shape(rows // 2 + (0 if totals else step - 1), 2 * topic_count) for step in range(1, chips)]
            + ([] if totals else [shape(8, 2 * topic_count)]),
            wide,
            tall,
            topics,
            *totals,
            *payload[::-1],
            *parts,
            flops=update_flops,
            moved=4 * span * (rows + 2 * topic_count),
        )
        totals = totals or outs[chips - 1 :]
        parts = [outs[0]] + [over_chips(outs[step - 1], step) for step in range(chips - 1, 0, -1)]
    (col_total,) = totals

    topics = call(
        functools.partial(topics_kernel, chips),
        shape(rows, 2 * topic_count),
        topics,
        col_total,
        *parts,
        *crossed,
        unread=len(crossed),
    )
    other = []
    if cores > 1:
        other_topics = over_cores(topics)
        other = [
            call(
                numerator_kernel,
                shape(topic_count, owned + 128),
                wide,
                topics,
                weighted[0],
                flops=update_flops // 2,
                moved=2 * span * (rows + 2 * topic_count),
            )
        ]
        topics, weighted = other_topics, crossed
    aligned = call(
        numerator_kernel,
        shape(topic_count, owned),
        wide,
        topics,
        weighted[0],
        dict_own,
        *other,
        flops=update_flops // 2,
        moved=2 * span * (rows + 2 * topic_count),
    )

    def words_of(array, member):
        return lax.dynamic_slice_in_dim(array, member * sub, sub, 1)

    aligned, base_sent = lax.optimization_barrier((aligned, base_sent))
    base_got = [over_chips(base_sent[step], step) for step in range(2, chips)]
    late = len(base_got) // 2
    base_got = base_got[::-1]
    median = call(
        functools.partial(median_kernel, members),
        pltpu.VMEM((topic_count, sub), jnp.float32),
        words_of(aligned, at_pert),
        *[over_pert(words_of(aligned, at_pert ^ step), step) for step in range(members - 1, 0, -1)],
        *base_got[late:],
        unread=len(base_got) - late,
    )
    pieces = [median] + [over_pert(median, step) for step in range(members - 1, 0, -1)]
    pieces[1], *base_got[:late] = lax.optimization_barrier((pieces[1], *base_got[:late]))
    median_halves = [pieces] + [[over_cores(piece) for piece in pieces]] * (cores - 1)
    base_all = [base_sent[0]] + near + base_got[::-1]

    base_rows = chips * base_docs
    refit_flops = 2 * 2 * 4 * base_rows * topic_count * owned
    forms, before = [], []
    for half in range(cores):
        wide, tall, part = call(
            functools.partial(refit_kernel, members, chips, half),
            [
                shape(2 * topic_count, owned, dtype=jnp.bfloat16),
                shape(owned, 2 * topic_count, dtype=jnp.bfloat16),
                shape(base_rows // 2 + 8, 2 * topic_count),
            ],
            *median_halves[half],
            *base_all,
            *before,
            flops=refit_flops,
            moved=16 * owned * topic_count,
            scratch=[pltpu.VMEM((topic_count, owned), jnp.float32)],
        )
        forms += [wide, tall]
        before = [part]
    scale, *parts = call(
        functools.partial(refit_again_kernel, chips, cores, base_docs),
        [shape(base_docs, 2 * topic_count)] * (chips + 1),
        *base_all,
        part,
        *[over_chips(part, step) for step in range(chips - 1, 0, -1)],
        *forms,
        flops=2 * refit_flops,
        moved=16 * owned * topic_count,
    )
    refit = call(
        finish_kernel,
        shape(base_docs, topic_count),
        scale,
        parts[0],
        *[over_chips(parts[step], step) for step in range(chips - 1, 0, -1)],
    )
    return (median.T[None, None], refit)


def solution(mesh):
    return jax.shard_map(
        per_device,
        mesh=mesh,
        in_specs=(
            P("pert", "doc", None),
            P("pert", "doc", None),
            P("pert", "doc", None),
            P("pert", "doc", None),
            P("pert", None),
            P(("pert", "doc"), None),
            P(("pert", "doc"), None),
        ),
        out_specs=(P("doc", "pert", None, None), P(("pert", "doc"), None)),
        check_vma=False,
    )
```

```python
import functools

import jax
import jax.numpy as jnp
from jax import lax
from jax.experimental import pallas as pl
from jax.experimental.pallas import tpu as pltpu
from jax.sharding import PartitionSpec as P

UPDATES = 3
REFITS = 2

EXACT = lax.Precision.HIGHEST
ROUGH = lax.Precision.HIGH
VMEM_BYTES = 14 * 1024 * 1024
SPREAD_BYTES = 60 * 1024 * 1024


def dot(left, right, dims, precision=ROUGH):
    return lax.dot_general(left, right, (dims, ((), ())), precision=precision)


def middle(pieces):
    pieces = list(pieces)
    count = len(pieces)
    for turn in range(count):
        for low in range(turn % 2, count - 1, 2):
            pieces[low], pieces[low + 1] = (
                jnp.minimum(pieces[low], pieces[low + 1]),
                jnp.maximum(pieces[low], pieces[low + 1]),
            )
    return 0.5 * (pieces[count // 2 - 1] + pieces[count // 2])


def call(kernel, outs, *args, flops=0, moved=0, unread=0, scratch=()):
    read = len(args) - unread
    return pl.pallas_call(
        kernel,
        out_shape=outs,
        in_specs=[pl.BlockSpec(memory_space=pltpu.VMEM)] * read
        + [pl.BlockSpec(memory_space=pl.ANY)] * unread,
        scratch_shapes=scratch,
        compiler_params=pltpu.CompilerParams(vmem_limit_bytes=VMEM_BYTES),
        cost_estimate=pl.CostEstimate(flops=flops, bytes_accessed=moved, transcendentals=0),
    )(*args)


def shape(*dims, dtype=jnp.float32):
    return jax.ShapeDtypeStruct(dims, dtype)


def high_low(x):
    high = x.astype(jnp.bfloat16).astype(jnp.float32)
    return high, x - high


def matmul(left, right):
    return jnp.dot(
        left.astype(jnp.bfloat16), right.astype(jnp.bfloat16), preferred_element_type=jnp.float32
    )


def blocks_of(chips, cores, step):
    at_doc = lax.axis_index("doc")
    at_chip, at_core = at_doc // cores, at_doc % cores
    return [(at_chip ^ step) * cores + (at_core ^ ((step + half) % cores)) for half in range(cores)]


def spread_kernel(chips, cores, own_words, mask_hbm, topics_hbm, perm_hbm, counts_hbm, *refs):
    out_refs, (mask_ref, topics_ref, perm_ref, counts_ref, small_sems, in_sems) = (
        refs[:chips],
        refs[chips:],
    )
    small = [
        pltpu.make_async_copy(mask_hbm, mask_ref, small_sems.at[0]),
        pltpu.make_async_copy(topics_hbm, topics_ref, small_sems.at[1]),
        pltpu.make_async_copy(perm_hbm, perm_ref, small_sems.at[2]),
    ]
    for copy in small:
        copy.start()
    steps = list(range(chips - 1, -1, -1))
    at_chip = lax.axis_index("doc") // cores
    arriving = {}
    for step in steps:
        first = (at_chip ^ step) * cores * own_words
        arriving[step] = pltpu.make_async_copy(
            counts_hbm.at[:, pl.ds(pl.multiple_of(first, 128), cores * own_words)],
            counts_ref.at[step],
            in_sems.at[step],
        )
        arriving[step].start()
    docs, tiles = mask_ref.shape
    width = chips * cores * own_words // tiles
    own_tiles = own_words // width
    tile_ids = lax.broadcasted_iota(jnp.int32, (docs, tiles), 1)
    doc_ids = lax.axis_index("doc") * docs + lax.broadcasted_iota(jnp.int32, (docs, tiles), 0)
    forced = (tile_ids == doc_ids % tiles).astype(jnp.int32)
    for copy in small:
        copy.wait()
    occupied = jnp.maximum(mask_ref[...], forced).astype(jnp.float32)
    topic_count = topics_ref.shape[1]
    onehot = lax.broadcasted_iota(jnp.int32, (topic_count, 2 * topic_count), 0) == jnp.concatenate(
        [perm_ref[...]] * 2, axis=1
    )
    topics = moved_columns(topics_ref[...], onehot.astype(jnp.float32))
    for step in steps:
        for half, block in enumerate(blocks_of(chips, cores, step)):
            near = pltpu.roll(occupied, lax.rem(tiles - block * own_tiles, tiles), 1)
            for tile in range(own_tiles):
                at = slice(half * own_words + tile * width, half * own_words + (tile + 1) * width)
                out_refs[step][:, at] = jnp.broadcast_to(near[:, tile : tile + 1], (docs, width))
        out_refs[step][:, cores * own_words :] = topics
    for step in steps:
        arriving[step].wait()
        for half, block in enumerate(blocks_of(chips, cores, step)):
            at = slice(half * own_words, (half + 1) * own_words)
            first = pl.multiple_of(lax.rem(block, cores) * own_words, 128)
            out_refs[step][:, at] *= counts_ref[step, :, pl.ds(first, own_words)].astype(jnp.float32)


def base_kernel(chips, cores, counts_ref, topics_ref, *out_refs):
    span = out_refs[0].shape[1] - 2 * topics_ref.shape[1]
    own_words = span // cores
    for step in range(chips):
        for half, block in enumerate(blocks_of(chips, cores, step)):
            at = slice(half * own_words, (half + 1) * own_words)
            first = pl.multiple_of(block * own_words, 128)
            out_refs[step][:, at] = counts_ref[:, pl.ds(first, own_words)].astype(jnp.float32)
        out_refs[step][:, span:] = jnp.concatenate([topics_ref[...]] * 2, axis=1)


def moved_columns(x, onehot):
    rows = x.shape[0]
    high, rest = high_low(x)
    mid, low = high_low(rest)
    moved = matmul(jnp.concatenate([high, mid, low], axis=0), onehot)
    return moved[:rows] + moved[rows : 2 * rows] + moved[2 * rows :]


def dictionary_kernel(half_count, perm_ref, *refs):
    topics, words = refs[0].shape
    wide_ref, tall_ref, total_ref, own_ref = refs[half_count:]
    turned_onehot = (
        (lax.broadcasted_iota(jnp.int32, (topics, topics), 0) == perm_ref[...]).astype(jnp.float32).T
    )
    total = jnp.zeros((1, 2 * topics), jnp.float32)
    for half in range(half_count):
        at = slice(half * words, (half + 1) * words)
        high, rest = high_low(refs[half][...])
        mid, low = high_low(rest)
        aligned = matmul(
            jnp.concatenate([turned_onehot] * 3, axis=1), jnp.concatenate([high, mid, low], axis=0)
        )
        if half == 0:
            own_ref[...] = aligned
        wide = jnp.concatenate(high_low(aligned), axis=0)
        wide_ref[:, at] = wide.astype(jnp.bfloat16)
        tall = wide.T
        total += jnp.sum(tall, axis=0, keepdims=True)
        tall_ref[at, :] = tall.astype(jnp.bfloat16)
    total_ref[...] = jnp.broadcast_to(total + turned(total), total_ref.shape)


def recon_of(doubled, wide):
    rows = doubled.shape[0]
    both = matmul(jnp.concatenate(high_low(doubled), axis=0), wide)
    return both[:rows] + both[rows:]


def product_of(quotient, tall, ones=0):
    rows = quotient.shape[0]
    left = [*high_low(quotient)] + [jnp.ones((ones, quotient.shape[1]), jnp.float32)] * (ones > 0)
    both = matmul(jnp.concatenate(left, axis=0), tall)
    both = [both[:rows] + both[rows : 2 * rows], both[2 * rows :]]
    both = jnp.concatenate(both, axis=0) if ones else both[0]
    return both + turned(both)


def turned(x):
    return pltpu.roll(x, x.shape[1] // 2, 1)


def left_half(x):
    return lax.broadcasted_iota(jnp.int32, x.shape, 1) < x.shape[1] // 2


def pack(doubled):
    half = doubled.shape[0] // 2
    lower, upper = doubled[:half], doubled[half:]
    return jnp.where(left_half(lower), lower, upper)


def sum_packed(chips, parts):
    parts = [parts[0], *parts[:0:-1]]
    side = max(chips // 2, 1)
    rows = parts[0].shape[0] // side

    def moved(x, step):
        if step == 0:
            return x
        return jnp.concatenate([x[(c ^ step) * rows : ((c ^ step) + 1) * rows] for c in range(side)], axis=0)

    sums = []
    for first in range(0, chips, side):
        sums.append(sum(moved(parts[step], step - first) for step in range(first, first + side)))
    packed, other = sums[0] + turned(sums[1]), turned(sums[0]) + sums[1]
    left = left_half(packed)
    return jnp.concatenate([jnp.where(left, packed, other), jnp.where(left, other, packed)], axis=0)


def write_parts(refs, part):
    rows = part.shape[0]
    for ref in refs:
        ref[:rows] = part
        if ref.shape[0] > rows:
            ref[rows:] = jnp.zeros((ref.shape[0] - rows, part.shape[1]), part.dtype)


def first_kernel(chips, cores, order, wide_ref, tall_ref, col_part_ref, *refs):
    payload = [refs[order.index(step)] for step in range(chips)]
    topics_ref, part_ref, *half_refs = refs[-2 - cores :]
    span = wide_ref.shape[1]
    topics = jnp.concatenate([ref[:, span:] for ref in payload], axis=0)
    topics_ref[...] = topics
    weighted = jnp.concatenate([ref[:, :span] for ref in payload], axis=0)
    part = pack(product_of(weighted / recon_of(topics, wide_ref[...]), tall_ref[...]))
    part_ref[: part.shape[0]] = part
    part_ref[part.shape[0] :] = col_part_ref[...]
    words = span // cores
    for half, ref in enumerate(half_refs):
        ref[...] = weighted[:, half * words : (half + 1) * words]


def update_kernel(chips, wide_ref, tall_ref, before_ref, *refs):
    packed = before_ref.shape[0] // 2
    if refs[-1].shape[0] == 8:
        payload, parts = refs[:chips][::-1], refs[chips : 2 * chips]
        topics_ref, *part_refs, total_ref = refs[2 * chips :]
        total_ref[...] = sum(ref[packed:] for ref in parts)
    else:
        total_ref, payload, parts = refs[0], refs[1 : chips + 1][::-1], refs[chips + 1 : 2 * chips + 1]
        topics_ref, *part_refs = refs[2 * chips + 1 :]
    span = wide_ref.shape[1]
    total = sum_packed(chips, [ref[:packed] for ref in parts])
    topics = before_ref[...] / total_ref[:1] * total
    topics_ref[...] = topics
    weighted = jnp.concatenate([ref[:, :span] for ref in payload], axis=0)
    write_parts(part_refs, pack(product_of(weighted / recon_of(topics, wide_ref[...]), tall_ref[...])))


def numerator_of(topics, quotient):
    high, low = high_low(topics.T[: topics.shape[1] // 2])
    quotient_high, quotient_low = high_low(quotient)
    return matmul(
        jnp.concatenate([high, low, high], axis=1),
        jnp.concatenate([quotient_high, quotient_high, quotient_low], axis=0),
    )


def topics_kernel(chips, before_ref, total_ref, *refs):
    parts, topics_ref = refs[:chips], refs[-1]
    total = sum_packed(chips, [ref[: before_ref.shape[0] // 2] for ref in parts])
    topics_ref[...] = before_ref[...] / total_ref[:1] * total


def numerator_kernel(wide_ref, topics_ref, weighted_ref, *refs):
    before, out_ref = refs[:-1], refs[-1]
    words = weighted_ref.shape[1]
    topics = topics_ref[...]
    load = jnp.sum(topics.T[: topics.shape[1] // 2], axis=1, keepdims=True)
    numerator = numerator_of(topics, weighted_ref[...] / recon_of(topics, wide_ref[:, :words]))
    if out_ref.shape[1] > words:
        out_ref[:, :words] = numerator
        out_ref[:, words:] = jnp.broadcast_to(load, (load.shape[0], out_ref.shape[1] - words))
    else:
        dict_ref, *other = before
        for ref in other:
            numerator = numerator + ref[:, :words]
            load = load + ref[:, words : words + 1]
        out_ref[...] = dict_ref[...] / load * numerator


def base_rows_of(refs, at):
    return jnp.concatenate([ref[:, at] for ref in refs], axis=0)


def refit_kernel(members, chips, half, *refs):
    pieces, payload = refs[:members], refs[members : members + chips]
    *before, wide_ref, tall_ref, part_ref, median_ref = refs[members + chips :]
    sub = pieces[0].shape[1]
    for me in range(members):

        @pl.when(lax.axis_index("pert") == me)
        def _():
            for at in range(members):
                owner = me ^ ((members - at) % members)
                median_ref[:, owner * sub : (owner + 1) * sub] = pieces[at][...]

    words = median_ref.shape[1]
    span = payload[0].shape[1] - part_ref.shape[1]
    wide = jnp.concatenate(high_low(median_ref[...]), axis=0)
    wide = wide.astype(jnp.bfloat16)
    tall = wide.T
    wide_ref[...] = wide
    tall_ref[...] = tall
    weighted = base_rows_of(payload, slice(half * words, (half + 1) * words))
    refit = base_rows_of(payload, slice(span, None))
    both = product_of(weighted / recon_of(refit, wide), tall, ones=8)
    both = jnp.concatenate([pack(both[:-8]), both[-8:]], axis=0)
    part_ref[...] = both + before[0][...] if before else both


def refit_again_kernel(chips, cores, base_docs, *refs):
    payload, parts, halves = refs[:chips], refs[chips : 2 * chips], refs[2 * chips : 2 * (chips + cores)]
    scale_ref, *part_refs = refs[2 * (chips + cores) :]
    packed = chips * base_docs // 2
    span = payload[0].shape[1] - scale_ref.shape[1]
    words = span // cores
    median_total = sum(ref[packed : packed + 1] for ref in parts)
    total = sum_packed(chips, [ref[:packed] for ref in parts])
    refit = base_rows_of(payload, slice(span, None)) / median_total * total
    scale_ref[...] = refit[:base_docs] / median_total
    wide = jnp.concatenate([ref[...] for ref in halves[0::2]], axis=1)
    tall = jnp.concatenate([ref[...] for ref in halves[1::2]], axis=0)
    weighted = base_rows_of(payload, slice(0, cores * words))
    part = product_of(weighted / recon_of(refit, wide), tall)
    for step in range(chips):
        part_refs[step][...] = part[step * base_docs : (step + 1) * base_docs]


def finish_kernel(scale_ref, *refs):
    parts, out_ref = refs[:-1], refs[-1]
    out_ref[...] = (scale_ref[...] * sum(ref[...] for ref in parts))[:, : out_ref.shape[1]]


def median_kernel(members, *refs):
    refs[-1][...] = middle([ref[...] for ref in refs[:members]])


def per_device(counts, tile_mask, member_topics, start_dict, align_perm, base_counts, base_topics):
    doc_size = lax.axis_size("doc")
    members = lax.axis_size("pert")
    cores = 2 - doc_size % 2
    chips = doc_size // cores
    at_pert = lax.axis_index("pert")
    at_doc = lax.axis_index("doc")
    at_chip, at_core = at_doc // cores, at_doc % cores
    docs = counts.shape[1]
    base_docs = base_counts.shape[0]
    topic_count = member_topics.shape[2]
    owned = start_dict.shape[1]
    span = cores * owned
    rows = chips * docs
    sub = owned // members

    def over_chips(array, step):
        return lax.ppermute(
            array,
            "doc",
            [
                (c * cores + k, (c ^ step) * cores + (k + step) % cores)
                for c in range(chips)
                for k in range(cores)
            ],
        )

    def over_cores(array):
        return lax.ppermute(array, "doc", [(d, d ^ 1) for d in range(doc_size)])

    def over_pert(array, step):
        return lax.ppermute(array, "pert", [(m, m ^ step) for m in range(members)])

    sent = pl.pallas_call(
        functools.partial(spread_kernel, chips, cores, owned),
        out_shape=[pltpu.VMEM((docs, span + 2 * topic_count), jnp.float32)] * chips,
        in_specs=[pl.BlockSpec(memory_space=pltpu.HBM)] * 4,
        out_specs=[pl.BlockSpec(memory_space=pltpu.VMEM)] * chips,
        scratch_shapes=[
            pltpu.VMEM(tile_mask.shape[1:], jnp.int32),
            pltpu.VMEM(member_topics.shape[1:], jnp.float32),
            pltpu.VMEM(align_perm.shape, jnp.int32),
            pltpu.VMEM((chips, docs, span), jnp.int32),
            pltpu.SemaphoreType.DMA((3,)),
            pltpu.SemaphoreType.DMA((chips,)),
        ],
        compiler_params=pltpu.CompilerParams(vmem_limit_bytes=VMEM_BYTES),
        cost_estimate=pl.CostEstimate(flops=0, bytes_accessed=12 * counts.size, transcendentals=0),
    )(*[pltpu.with_memory_space_constraint(x, pltpu.HBM) for x in (tile_mask[0], member_topics[0], align_perm, counts[0])])
    base_sent = call(
        functools.partial(base_kernel, chips, cores),
        [shape(base_docs, span + 2 * topic_count)] * chips,
        base_counts,
        base_topics,
        moved=8 * base_counts.size,
    )
    got = [over_chips(sent[step], step) for step in range(chips - 1, 0, -1)][::-1]
    payload = [sent[0]] + got
    near = [over_chips(base_sent[step], step) for step in range(1, min(chips, 2))]
    dict_own = start_dict[0].T
    halves = [dict_own] + [over_cores(dict_own)] * (cores - 1)
    wide, tall, col_part, dict_own = call(
        functools.partial(dictionary_kernel, cores),
        [
            shape(2 * topic_count, span, dtype=jnp.bfloat16),
            shape(span, 2 * topic_count, dtype=jnp.bfloat16),
            shape(8, 2 * topic_count),
            shape(topic_count, owned),
        ],
        align_perm,
        *halves,
        moved=4 * 4 * span * topic_count,
    )

    update_flops = 2 * 2 * 4 * rows * topic_count * span
    count_order = [chips - 1] + list(range(1, chips - 1)) + [0]
    topics, part, *weighted = call(
        functools.partial(first_kernel, chips, cores, count_order),
        [shape(rows, 2 * topic_count), shape(rows // 2 + 8, 2 * topic_count)]
        + [shape(rows, owned)] * cores,
        wide,
        tall,
        col_part,
        *[payload[step] for step in count_order],
        *near,
        unread=len(near),
        flops=update_flops,
        moved=4 * span * (rows + 2 * topic_count),
    )
    parts = [part] + [over_chips(part, step) for step in range(chips - 1, 0, -1)]
    crossed = [over_cores(weighted[1])] if cores > 1 else []
    totals = []
    for update in range(1, UPDATES):
        topics, *outs = call(
            functools.partial(update_kernel, chips),
            [shape(rows, 2 * topic_count)]
            + [shape(rows // 2 + (0 if totals else step - 1), 2 * topic_count) for step in range(1, chips)]
            + ([] if totals else [shape(8, 2 * topic_count)]),
            wide,
            tall,
            topics,
            *totals,
            *payload[::-1],
            *parts,
            flops=update_flops,
            moved=4 * span * (rows + 2 * topic_count),
        )
        totals = totals or outs[chips - 1 :]
        parts = [outs[0]] + [over_chips(outs[step - 1], step) for step in range(chips - 1, 0, -1)]
    (col_total,) = totals

    topics = call(
        functools.partial(topics_kernel, chips),
        shape(rows, 2 * topic_count),
        topics,
        col_total,
        *parts,
        *crossed,
        unread=len(crossed),
    )
    other = []
    if cores > 1:
        other_topics = over_cores(topics)
        other = [
            call(
                numerator_kernel,
                shape(topic_count, owned + 128),
                wide,
                topics,
                weighted[0],
                flops=update_flops // 2,
                moved=2 * span * (rows + 2 * topic_count),
            )
        ]
        topics, weighted = other_topics, crossed
    aligned = call(
        numerator_kernel,
        shape(topic_count, owned),
        wide,
        topics,
        weighted[0],
        dict_own,
        *other,
        flops=update_flops // 2,
        moved=2 * span * (rows + 2 * topic_count),
    )

    def words_of(array, member):
        return lax.dynamic_slice_in_dim(array, member * sub, sub, 1)

    aligned, base_sent = lax.optimization_barrier((aligned, base_sent))
    base_got = [over_chips(base_sent[step], step) for step in range(2, chips)]
    late = len(base_got) // 2
    base_got = base_got[::-1]
    median = call(
        functools.partial(median_kernel, members),
        pltpu.VMEM((topic_count, sub), jnp.float32),
        words_of(aligned, at_pert),
        *[over_pert(words_of(aligned, at_pert ^ step), step) for step in range(members - 1, 0, -1)],
        *base_got[late:],
        unread=len(base_got) - late,
    )
    pieces = [median] + [over_pert(median, step) for step in range(members - 1, 0, -1)]
    pieces[1], *base_got[:late] = lax.optimization_barrier((pieces[1], *base_got[:late]))
    median_halves = [pieces] + [[over_cores(piece) for piece in pieces]] * (cores - 1)
    base_all = [base_sent[0]] + near + base_got[::-1]

    base_rows = chips * base_docs
    refit_flops = 2 * 2 * 4 * base_rows * topic_count * owned
    forms, before = [], []
    for half in range(cores):
        wide, tall, part = call(
            functools.partial(refit_kernel, members, chips, half),
            [
                shape(2 * topic_count, owned, dtype=jnp.bfloat16),
                shape(owned, 2 * topic_count, dtype=jnp.bfloat16),
                shape(base_rows // 2 + 8, 2 * topic_count),
            ],
            *median_halves[half],
            *base_all,
            *before,
            flops=refit_flops,
            moved=16 * owned * topic_count,
            scratch=[pltpu.VMEM((topic_count, owned), jnp.float32)],
        )
        forms += [wide, tall]
        before = [part]
    scale, *parts = call(
        functools.partial(refit_again_kernel, chips, cores, base_docs),
        [shape(base_docs, 2 * topic_count)] * (chips + 1),
        *base_all,
        part,
        *[over_chips(part, step) for step in range(chips - 1, 0, -1)],
        *forms,
        flops=2 * refit_flops,
        moved=16 * owned * topic_count,
    )
    refit = call(
        finish_kernel,
        shape(base_docs, topic_count),
        scale,
        parts[0],
        *[over_chips(parts[step], step) for step in range(chips - 1, 0, -1)],
    )
    return (median.T[None, None], refit)


def solution(mesh):
    return jax.shard_map(
        per_device,
        mesh=mesh,
        in_specs=(
            P("pert", "doc", None),
            P("pert", "doc", None),
            P("pert", "doc", None),
            P("pert", "doc", None),
            P("pert", None),
            P(("pert", "doc"), None),
            P(("pert", "doc"), None),
        ),
        out_specs=(P("doc", "pert", None, None), P(("pert", "doc"), None)),
        check_vma=False,
    )
```

```python
import functools

import jax
import jax.numpy as jnp
from jax import lax
from jax.experimental import pallas as pl
from jax.experimental.pallas import tpu as pltpu
from jax.sharding import PartitionSpec as P

UPDATES = 3
REFITS = 2

EXACT = lax.Precision.HIGHEST
ROUGH = lax.Precision.HIGH
VMEM_BYTES = 14 * 1024 * 1024
SPREAD_BYTES = 60 * 1024 * 1024


def dot(left, right, dims, precision=ROUGH):
    return lax.dot_general(left, right, (dims, ((), ())), precision=precision)


def middle(pieces):
    pieces = list(pieces)
    count = len(pieces)
    for turn in range(count):
        for low in range(turn % 2, count - 1, 2):
            pieces[low], pieces[low + 1] = (
                jnp.minimum(pieces[low], pieces[low + 1]),
                jnp.maximum(pieces[low], pieces[low + 1]),
            )
    return 0.5 * (pieces[count // 2 - 1] + pieces[count // 2])


def call(kernel, outs, *args, flops=0, moved=0, unread=0, scratch=()):
    read = len(args) - unread
    return pl.pallas_call(
        kernel,
        out_shape=outs,
        in_specs=[pl.BlockSpec(memory_space=pltpu.VMEM)] * read
        + [pl.BlockSpec(memory_space=pl.ANY)] * unread,
        scratch_shapes=scratch,
        compiler_params=pltpu.CompilerParams(vmem_limit_bytes=VMEM_BYTES),
        cost_estimate=pl.CostEstimate(flops=flops, bytes_accessed=moved, transcendentals=0),
    )(*args)


def shape(*dims, dtype=jnp.float32):
    return jax.ShapeDtypeStruct(dims, dtype)


def high_low(x):
    high = x.astype(jnp.bfloat16).astype(jnp.float32)
    return high, x - high


def matmul(left, right):
    return jnp.dot(
        left.astype(jnp.bfloat16), right.astype(jnp.bfloat16), preferred_element_type=jnp.float32
    )


def blocks_of(chips, cores, step):
    at_doc = lax.axis_index("doc")
    at_chip, at_core = at_doc // cores, at_doc % cores
    return [(at_chip ^ step) * cores + (at_core ^ ((step + half) % cores)) for half in range(cores)]


def spread_kernel(chips, cores, own_words, mask_hbm, topics_hbm, perm_hbm, counts_hbm, *refs):
    out_refs, (mask_ref, topics_ref, perm_ref, counts_ref, small_sems, in_sems) = (
        refs[:chips],
        refs[chips:],
    )
    small = [
        pltpu.make_async_copy(mask_hbm, mask_ref, small_sems.at[0]),
        pltpu.make_async_copy(topics_hbm, topics_ref, small_sems.at[1]),
        pltpu.make_async_copy(perm_hbm, perm_ref, small_sems.at[2]),
    ]
    for copy in small:
        copy.start()
    steps = list(range(chips - 1, -1, -1))
    at_chip = lax.axis_index("doc") // cores
    arriving = {}
    for step in steps:
        first = (at_chip ^ step) * cores * own_words
        arriving[step] = pltpu.make_async_copy(
            counts_hbm.at[:, pl.ds(pl.multiple_of(first, 128), cores * own_words)],
            counts_ref.at[step],
            in_sems.at[step],
        )
        arriving[step].start()
    docs, tiles = mask_ref.shape
    width = chips * cores * own_words // tiles
    own_tiles = own_words // width
    tile_ids = lax.broadcasted_iota(jnp.int32, (docs, tiles), 1)
    doc_ids = lax.axis_index("doc") * docs + lax.broadcasted_iota(jnp.int32, (docs, tiles), 0)
    forced = (tile_ids == doc_ids % tiles).astype(jnp.int32)
    for copy in small:
        copy.wait()
    occupied = jnp.maximum(mask_ref[...], forced).astype(jnp.float32)
    topic_count = topics_ref.shape[1]
    onehot = lax.broadcasted_iota(jnp.int32, (topic_count, 2 * topic_count), 0) == jnp.concatenate(
        [perm_ref[...]] * 2, axis=1
    )
    topics = moved_columns(topics_ref[...], onehot.astype(jnp.float32))
    for step in steps:
        for half, block in enumerate(blocks_of(chips, cores, step)):
            near = pltpu.roll(occupied, lax.rem(tiles - block * own_tiles, tiles), 1)
            for tile in range(own_tiles):
                at = slice(half * own_words + tile * width, half * own_words + (tile + 1) * width)
                out_refs[step][:, at] = jnp.broadcast_to(near[:, tile : tile + 1], (docs, width))
        out_refs[step][:, cores * own_words :] = topics
    for step in steps:
        arriving[step].wait()
        for half, block in enumerate(blocks_of(chips, cores, step)):
            at = slice(half * own_words, (half + 1) * own_words)
            first = pl.multiple_of(lax.rem(block, cores) * own_words, 128)
            out_refs[step][:, at] *= counts_ref[step, :, pl.ds(first, own_words)].astype(jnp.float32)


def base_kernel(chips, cores, counts_ref, topics_ref, *out_refs):
    span = out_refs[0].shape[1] - 2 * topics_ref.shape[1]
    own_words = span // cores
    for step in range(chips):
        for half, block in enumerate(blocks_of(chips, cores, step)):
            at = slice(half * own_words, (half + 1) * own_words)
            first = pl.multiple_of(block * own_words, 128)
            out_refs[step][:, at] = counts_ref[:, pl.ds(first, own_words)].astype(jnp.float32)
        out_refs[step][:, span:] = jnp.concatenate([topics_ref[...]] * 2, axis=1)


def moved_columns(x, onehot):
    rows = x.shape[0]
    high, rest = high_low(x)
    mid, low = high_low(rest)
    moved = matmul(jnp.concatenate([high, mid, low], axis=0), onehot)
    return moved[:rows] + moved[rows : 2 * rows] + moved[2 * rows :]


def dictionary_kernel(half_count, perm_ref, *refs):
    topics, words = refs[0].shape
    wide_ref, tall_ref, total_ref, own_ref = refs[half_count:]
    turned_onehot = (
        (lax.broadcasted_iota(jnp.int32, (topics, topics), 0) == perm_ref[...]).astype(jnp.float32).T
    )
    total = jnp.zeros((1, 2 * topics), jnp.float32)
    for half in range(half_count):
        at = slice(half * words, (half + 1) * words)
        high, rest = high_low(refs[half][...])
        mid, low = high_low(rest)
        aligned = matmul(
            jnp.concatenate([turned_onehot] * 3, axis=1), jnp.concatenate([high, mid, low], axis=0)
        )
        if half == 0:
            own_ref[...] = aligned
        wide = jnp.concatenate(high_low(aligned), axis=0)
        wide_ref[:, at] = wide.astype(jnp.bfloat16)
        tall = wide.T
        total += jnp.sum(tall, axis=0, keepdims=True)
        tall_ref[at, :] = tall.astype(jnp.bfloat16)
    total_ref[...] = jnp.broadcast_to(total + turned(total), total_ref.shape)


def recon_of(doubled, wide):
    rows = doubled.shape[0]
    both = matmul(jnp.concatenate(high_low(doubled), axis=0), wide)
    return both[:rows] + both[rows:]


def product_of(quotient, tall, ones=0):
    rows = quotient.shape[0]
    left = [*high_low(quotient)] + [jnp.ones((ones, quotient.shape[1]), jnp.float32)] * (ones > 0)
    both = matmul(jnp.concatenate(left, axis=0), tall)
    both = [both[:rows] + both[rows : 2 * rows], both[2 * rows :]]
    both = jnp.concatenate(both, axis=0) if ones else both[0]
    return both + turned(both)


def turned(x):
    return pltpu.roll(x, x.shape[1] // 2, 1)


def left_half(x):
    return lax.broadcasted_iota(jnp.int32, x.shape, 1) < x.shape[1] // 2


def pack(doubled):
    half = doubled.shape[0] // 2
    lower, upper = doubled[:half], doubled[half:]
    return jnp.where(left_half(lower), lower, upper)


def sum_packed(chips, parts):
    parts = [parts[0], *parts[:0:-1]]
    side = max(chips // 2, 1)
    rows = parts[0].shape[0] // side

    def moved(x, step):
        if step == 0:
            return x
        return jnp.concatenate([x[(c ^ step) * rows : ((c ^ step) + 1) * rows] for c in range(side)], axis=0)

    sums = []
    for first in range(0, chips, side):
        sums.append(sum(moved(parts[step], step - first) for step in range(first, first + side)))
    packed, other = sums[0] + turned(sums[1]), turned(sums[0]) + sums[1]
    left = left_half(packed)
    return jnp.concatenate([jnp.where(left, packed, other), jnp.where(left, other, packed)], axis=0)


def write_parts(refs, part):
    rows = part.shape[0]
    for ref in refs:
        ref[:rows] = part
        if ref.shape[0] > rows:
            ref[rows:] = jnp.zeros((ref.shape[0] - rows, part.shape[1]), part.dtype)


def first_kernel(chips, cores, order, wide_ref, tall_ref, col_part_ref, *refs):
    payload = [refs[order.index(step)] for step in range(chips)]
    topics_ref, part_ref, *half_refs = refs[-2 - cores :]
    span = wide_ref.shape[1]
    topics = jnp.concatenate([ref[:, span:] for ref in payload], axis=0)
    topics_ref[...] = topics
    weighted = jnp.concatenate([ref[:, :span] for ref in payload], axis=0)
    part = pack(product_of(weighted / recon_of(topics, wide_ref[...]), tall_ref[...]))
    part_ref[: part.shape[0]] = part
    part_ref[part.shape[0] :] = col_part_ref[:1]
    words = span // cores
    for half, ref in enumerate(half_refs):
        ref[...] = weighted[:, half * words : (half + 1) * words]


def update_kernel(chips, wide_ref, tall_ref, before_ref, *refs):
    packed = before_ref.shape[0] // 2
    if refs[-1].shape[0] == 8:
        payload, parts = refs[:chips][::-1], refs[chips : 2 * chips]
        topics_ref, *part_refs, total_ref = refs[2 * chips :]
        total = sum(ref[packed : packed + 1] for ref in parts)
        total_ref[...] = jnp.broadcast_to(total, total_ref.shape)
    else:
        total_ref, payload, parts = refs[0], refs[1 : chips + 1][::-1], refs[chips + 1 : 2 * chips + 1]
        topics_ref, *part_refs = refs[2 * chips + 1 :]
    span = wide_ref.shape[1]
    total = sum_packed(chips, [ref[:packed] for ref in parts])
    topics = before_ref[...] / total_ref[:1] * total
    topics_ref[...] = topics
    weighted = jnp.concatenate([ref[:, :span] for ref in payload], axis=0)
    write_parts(part_refs, pack(product_of(weighted / recon_of(topics, wide_ref[...]), tall_ref[...])))


def numerator_of(topics, quotient):
    high, low = high_low(topics.T[: topics.shape[1] // 2])
    quotient_high, quotient_low = high_low(quotient)
    return matmul(
        jnp.concatenate([high, low, high], axis=1),
        jnp.concatenate([quotient_high, quotient_high, quotient_low], axis=0),
    )


def topics_kernel(chips, before_ref, total_ref, *refs):
    parts, topics_ref = refs[:chips], refs[-1]
    total = sum_packed(chips, [ref[: before_ref.shape[0] // 2] for ref in parts])
    topics_ref[...] = before_ref[...] / total_ref[:1] * total


def numerator_kernel(wide_ref, topics_ref, weighted_ref, *refs):
    before, out_ref = refs[:-1], refs[-1]
    words = weighted_ref.shape[1]
    topics = topics_ref[...]
    load = jnp.sum(topics.T[: topics.shape[1] // 2], axis=1, keepdims=True)
    numerator = numerator_of(topics, weighted_ref[...] / recon_of(topics, wide_ref[:, :words]))
    if out_ref.shape[1] > words:
        out_ref[:, :words] = numerator
        out_ref[:, words:] = jnp.broadcast_to(load, (load.shape[0], out_ref.shape[1] - words))
    else:
        dict_ref, *other = before
        for ref in other:
            numerator = numerator + ref[:, :words]
            load = load + ref[:, words : words + 1]
        out_ref[...] = dict_ref[...] / load * numerator


def base_rows_of(refs, at):
    return jnp.concatenate([ref[:, at] for ref in refs], axis=0)


def refit_kernel(members, chips, half, *refs):
    pieces, payload = refs[:members], refs[members : members + chips]
    *before, wide_ref, tall_ref, part_ref, median_ref = refs[members + chips :]
    sub = pieces[0].shape[1]
    for me in range(members):

        @pl.when(lax.axis_index("pert") == me)
        def _():
            for at in range(members):
                owner = me ^ ((members - at) % members)
                median_ref[:, owner * sub : (owner + 1) * sub] = pieces[at][...]

    words = median_ref.shape[1]
    span = payload[0].shape[1] - part_ref.shape[1]
    wide = jnp.concatenate(high_low(median_ref[...]), axis=0)
    wide = wide.astype(jnp.bfloat16)
    tall = wide.T
    wide_ref[...] = wide
    tall_ref[...] = tall
    weighted = base_rows_of(payload, slice(half * words, (half + 1) * words))
    refit = base_rows_of(payload, slice(span, None))
    both = product_of(weighted / recon_of(refit, wide), tall, ones=8)
    both = jnp.concatenate([pack(both[:-8]), both[-8:]], axis=0)
    part_ref[...] = both + before[0][...] if before else both


def refit_again_kernel(chips, cores, base_docs, *refs):
    payload, parts, halves = refs[:chips], refs[chips : 2 * chips], refs[2 * chips : 2 * (chips + cores)]
    scale_ref, *part_refs = refs[2 * (chips + cores) :]
    packed = chips * base_docs // 2
    span = payload[0].shape[1] - scale_ref.shape[1]
    words = span // cores
    median_total = sum(ref[packed : packed + 1] for ref in parts)
    total = sum_packed(chips, [ref[:packed] for ref in parts])
    refit = base_rows_of(payload, slice(span, None)) / median_total * total
    scale_ref[...] = refit[:base_docs] / median_total
    wide = jnp.concatenate([ref[...] for ref in halves[0::2]], axis=1)
    tall = jnp.concatenate([ref[...] for ref in halves[1::2]], axis=0)
    weighted = base_rows_of(payload, slice(0, cores * words))
    part = product_of(weighted / recon_of(refit, wide), tall)
    for step in range(chips):
        part_refs[step][...] = part[step * base_docs : (step + 1) * base_docs]


def finish_kernel(scale_ref, *refs):
    parts, out_ref = refs[:-1], refs[-1]
    out_ref[...] = (scale_ref[...] * sum(ref[...] for ref in parts))[:, : out_ref.shape[1]]


def median_kernel(members, *refs):
    refs[-1][...] = middle([ref[...] for ref in refs[:members]])


def per_device(counts, tile_mask, member_topics, start_dict, align_perm, base_counts, base_topics):
    doc_size = lax.axis_size("doc")
    members = lax.axis_size("pert")
    cores = 2 - doc_size % 2
    chips = doc_size // cores
    at_pert = lax.axis_index("pert")
    at_doc = lax.axis_index("doc")
    at_chip, at_core = at_doc // cores, at_doc % cores
    docs = counts.shape[1]
    base_docs = base_counts.shape[0]
    topic_count = member_topics.shape[2]
    owned = start_dict.shape[1]
    span = cores * owned
    rows = chips * docs
    sub = owned // members

    def over_chips(array, step):
        return lax.ppermute(
            array,
            "doc",
            [
                (c * cores + k, (c ^ step) * cores + (k + step) % cores)
                for c in range(chips)
                for k in range(cores)
            ],
        )

    def over_cores(array):
        return lax.ppermute(array, "doc", [(d, d ^ 1) for d in range(doc_size)])

    def over_pert(array, step):
        return lax.ppermute(array, "pert", [(m, m ^ step) for m in range(members)])

    sent = pl.pallas_call(
        functools.partial(spread_kernel, chips, cores, owned),
        out_shape=[pltpu.VMEM((docs, span + 2 * topic_count), jnp.float32)] * chips,
        in_specs=[pl.BlockSpec(memory_space=pltpu.HBM)] * 4,
        out_specs=[pl.BlockSpec(memory_space=pltpu.VMEM)] * chips,
        scratch_shapes=[
            pltpu.VMEM(tile_mask.shape[1:], jnp.int32),
            pltpu.VMEM(member_topics.shape[1:], jnp.float32),
            pltpu.VMEM(align_perm.shape, jnp.int32),
            pltpu.VMEM((chips, docs, span), jnp.int32),
            pltpu.SemaphoreType.DMA((3,)),
            pltpu.SemaphoreType.DMA((chips,)),
        ],
        compiler_params=pltpu.CompilerParams(vmem_limit_bytes=VMEM_BYTES),
        cost_estimate=pl.CostEstimate(flops=0, bytes_accessed=12 * counts.size, transcendentals=0),
    )(*[pltpu.with_memory_space_constraint(x, pltpu.HBM) for x in (tile_mask[0], member_topics[0], align_perm, counts[0])])
    base_sent = call(
        functools.partial(base_kernel, chips, cores),
        [shape(base_docs, span + 2 * topic_count)] * chips,
        base_counts,
        base_topics,
        moved=8 * base_counts.size,
    )
    got = [over_chips(sent[step], step) for step in range(chips - 1, 0, -1)][::-1]
    payload = [sent[0]] + got
    near = [over_chips(base_sent[step], step) for step in range(1, min(chips, 2))]
    dict_own = start_dict[0].T
    halves = [dict_own] + [over_cores(dict_own)] * (cores - 1)
    wide, tall, col_part, dict_own = call(
        functools.partial(dictionary_kernel, cores),
        [
            shape(2 * topic_count, span, dtype=jnp.bfloat16),
            shape(span, 2 * topic_count, dtype=jnp.bfloat16),
            shape(8, 2 * topic_count),
            shape(topic_count, owned),
        ],
        align_perm,
        *halves,
        moved=4 * 4 * span * topic_count,
    )

    update_flops = 2 * 2 * 4 * rows * topic_count * span
    count_order = [chips - 1] + list(range(1, chips - 1)) + [0]
    topics, part, *weighted = call(
        functools.partial(first_kernel, chips, cores, count_order),
        [shape(rows, 2 * topic_count), shape(rows // 2 + 1, 2 * topic_count)]
        + [shape(rows, owned)] * cores,
        wide,
        tall,
        col_part,
        *[payload[step] for step in count_order],
        *near,
        unread=len(near),
        flops=update_flops,
        moved=4 * span * (rows + 2 * topic_count),
    )
    parts = [part] + [over_chips(part, step) for step in range(chips - 1, 0, -1)]
    crossed = [over_cores(weighted[1])] if cores > 1 else []
    totals = []
    for update in range(1, UPDATES):
        topics, *outs = call(
            functools.partial(update_kernel, chips),
            [shape(rows, 2 * topic_count)]
            + [shape(rows // 2 + (0 if totals else step - 1), 2 * topic_count) for step in range(1, chips)]
            + ([] if totals else [shape(8, 2 * topic_count)]),
            wide,
            tall,
            topics,
            *totals,
            *payload[::-1],
            *parts,
            flops=update_flops,
            moved=4 * span * (rows + 2 * topic_count),
        )
        totals = totals or outs[chips - 1 :]
        parts = [outs[0]] + [over_chips(outs[step - 1], step) for step in range(chips - 1, 0, -1)]
    (col_total,) = totals

    topics = call(
        functools.partial(topics_kernel, chips),
        shape(rows, 2 * topic_count),
        topics,
        col_total,
        *parts,
        *crossed,
        unread=len(crossed),
    )
    other = []
    if cores > 1:
        other_topics = over_cores(topics)
        other = [
            call(
                numerator_kernel,
                shape(topic_count, owned + 128),
                wide,
                topics,
                weighted[0],
                flops=update_flops // 2,
                moved=2 * span * (rows + 2 * topic_count),
            )
        ]
        topics, weighted = other_topics, crossed
    aligned = call(
        numerator_kernel,
        shape(topic_count, owned),
        wide,
        topics,
        weighted[0],
        dict_own,
        *other,
        flops=update_flops // 2,
        moved=2 * span * (rows + 2 * topic_count),
    )

    def words_of(array, member):
        return lax.dynamic_slice_in_dim(array, member * sub, sub, 1)

    aligned, base_sent = lax.optimization_barrier((aligned, base_sent))
    base_got = [over_chips(base_sent[step], step) for step in range(2, chips)]
    late = len(base_got) // 2
    base_got = base_got[::-1]
    median = call(
        functools.partial(median_kernel, members),
        pltpu.VMEM((topic_count, sub), jnp.float32),
        words_of(aligned, at_pert),
        *[over_pert(words_of(aligned, at_pert ^ step), step) for step in range(members - 1, 0, -1)],
        *base_got[late:],
        unread=len(base_got) - late,
    )
    pieces = [median] + [over_pert(median, step) for step in range(members - 1, 0, -1)]
    pieces[1], *base_got[:late] = lax.optimization_barrier((pieces[1], *base_got[:late]))
    median_halves = [pieces] + [[over_cores(piece) for piece in pieces]] * (cores - 1)
    base_all = [base_sent[0]] + near + base_got[::-1]

    base_rows = chips * base_docs
    refit_flops = 2 * 2 * 4 * base_rows * topic_count * owned
    forms, before = [], []
    for half in range(cores):
        wide, tall, part = call(
            functools.partial(refit_kernel, members, chips, half),
            [
                shape(2 * topic_count, owned, dtype=jnp.bfloat16),
                shape(owned, 2 * topic_count, dtype=jnp.bfloat16),
                shape(base_rows // 2 + 8, 2 * topic_count),
            ],
            *median_halves[half],
            *base_all,
            *before,
            flops=refit_flops,
            moved=16 * owned * topic_count,
            scratch=[pltpu.VMEM((topic_count, owned), jnp.float32)],
        )
        forms += [wide, tall]
        before = [part]
    scale, *parts = call(
        functools.partial(refit_again_kernel, chips, cores, base_docs),
        [shape(base_docs, 2 * topic_count)] * (chips + 1),
        *base_all,
        part,
        *[over_chips(part, step) for step in range(chips - 1, 0, -1)],
        *forms,
        flops=2 * refit_flops,
        moved=16 * owned * topic_count,
    )
    refit = call(
        finish_kernel,
        shape(base_docs, topic_count),
        scale,
        parts[0],
        *[over_chips(parts[step], step) for step in range(chips - 1, 0, -1)],
    )
    return (median.T[None, None], refit)


def solution(mesh):
    return jax.shard_map(
        per_device,
        mesh=mesh,
        in_specs=(
            P("pert", "doc", None),
            P("pert", "doc", None),
            P("pert", "doc", None),
            P("pert", "doc", None),
            P("pert", None),
            P(("pert", "doc"), None),
            P(("pert", "doc"), None),
        ),
        out_specs=(P("doc", "pert", None, None), P(("pert", "doc"), None)),
        check_vma=False,
    )
```
